32 devices in a mesh: det: 4 (over x, core), tm: 8 (over z, y).
Axes of the slice: x: 2, y: 2, z: 4, core: 2. Of those that a mesh axis runs over, the one named last changes fastest.
Arguments:
- sky_map: bfloat16 [32, 3, 128, 128], P('tm', None, 'det'), may hold values from -6 to 6
- tile_home: int32 [32], replicated, may hold values from 0 to 31, as said below
- piece_tiles: int32 [4, 8, 32], P('det', 'tm'), may hold values from 0 to 31, as said below
- run_slot: int32 [32, 128], P('det', 'tm'), may hold values from 0 to 31
- hit_row: int32 [32, 16384], P('det', 'tm'), may hold values from 0 to 126
- hit_col: int32 [32, 16384], P('det', 'tm'), may hold values from 0 to 126
- frac_row: bfloat16 [32, 16384], P('det', 'tm'), may hold values from 0 to 1
- frac_col: bfloat16 [32, 16384], P('det', 'tm'), may hold values from 0 to 1
- angle: float32 [32, 16384], P('det', 'tm'), may hold values from -3.140625 to 3.140625
- noise_coef: float32 [32, 1025], P('det'), may hold values from -0.3 to 0.3
Outputs:
- normal_map: float32 [32, 3, 128, 128], P('tm', None, 'det')
The draws below stay inside these ranges and needn't reach their ends.
Inputs may be any that keep to these rules, and one draw needn't show every extreme that they name: A permutation: tile g lies in row tile_home[g] of sky_map. `piece_tiles`: the 32 tiles listed by one piece are distinct, and at most 4 of them lie in rows of one index of tm (rows o * 4 to o * 4 + 3 of sky_map); every piece has exactly 4 tile in each index of tm that it reads from.
All inputs are finite; a program needn't handle non-finite values.
Results may differ from the reference program's by a relative error of at most 0.0048.
Values may be sent and summed in bfloat16 or wider, within the bound.
No kernel may reach another device: no remote copies, remote signals or barrier semaphores. Data moves between devices by JAX's collectives and lax.ppermute only.
A program may use at most 128 MiB of HBM per device.

```python
import jax
import jax.numpy as jnp
from jax import lax

PIX = 128
HALF_BAND = 1024
LISTED = 32
DET_DEV = 8
TIME_DEV = 2048
RUN = 128
TILE_DEV = 4
DETECTORS = 32
SAMPLES = 16384
TILES = 32
CAP = 4
N_DET = 4
N_TM = 8


def layout(key):
    base_key = jax.random.fold_in(key, 11)
    home_key, hot_key, owner_key, slot_key = jax.random.split(base_key, 4)
    tile_home = jax.random.permutation(home_key, TILES).astype(jnp.int32)
    tile_at = jnp.argsort(tile_home).astype(jnp.int32)
    hot_total = max(1, N_TM // 8)
    hot_owner = (jax.random.permutation(hot_key, N_TM) < hot_total).astype(jnp.int32)
    piece_total = N_DET * N_TM
    owners_used = LISTED // CAP
    owner_noise = jax.random.randint(owner_key, (piece_total, N_TM), 0, 1000)
    owner_score = (owner_noise + 600 * hot_owner[None, :]) * N_TM + jnp.arange(N_TM, dtype=jnp.int32)[None, :]
    owner_pick = lax.top_k(owner_score.astype(jnp.int32), owners_used)[1]
    slot_noise = jax.random.randint(slot_key, (piece_total, owners_used, TILE_DEV), 0, 1000)
    slot_score = slot_noise * TILE_DEV + jnp.arange(TILE_DEV, dtype=jnp.int32)
    slot_pick = lax.top_k(slot_score.astype(jnp.int32), CAP)[1]
    rows_read = owner_pick[:, :, None] * TILE_DEV + slot_pick
    piece_tiles = tile_at[rows_read.reshape(piece_total, LISTED)]
    return (tile_home, piece_tiles.reshape(N_DET, N_TM, LISTED).astype(jnp.int32))


def draw_tile_home(key, part):
    return layout(key)[0]


def draw_piece_tiles(key, part):
    return layout(key)[1]


def touch_ends(values, key, smallest, top_value):
    longest = values.shape.index(max(values.shape))
    spots = []
    for shift in (0, 1):
        where = [jax.random.randint(jax.random.fold_in(key, axis), (), 0, length) for axis, length in enumerate(values.shape)]
        where[longest] = (where[longest] + shift) % values.shape[longest]
        spots.append(tuple(where))
    return values.at[spots[0]].set(smallest).at[spots[1]].set(top_value)


def block_scale(own_key, shape, pieces, smallest, top_value):
    gain, own = 1.0, jax.random.fold_in(own_key, 6)
    for dim, shards_of in pieces:
        steps = jnp.exp(jax.random.uniform(jax.random.fold_in(own, dim), (shards_of,), jnp.float32, smallest / len(pieces), top_value / len(pieces)))
        gain = gain * jnp.repeat(steps, shape[dim] // shards_of).reshape([-1 if axis == dim else 1 for axis in range(len(shape))])
    return gain


def gaussian(own_key, shape, scale, limit, cuts=(), kind=jnp.bfloat16):
    result = scale * jax.random.normal(own_key, shape, jnp.float32)
    if cuts:
        result = result * block_scale(own_key, shape, cuts, -0.22, 0.18)
    return jnp.clip(result, -limit, limit).astype(kind)


def setup_inputs(seed: int = 0) -> dict:
    key_of = jax.random.split(jax.random.key(seed), 11)
    return {
        "sky_map": gaussian(key_of[0], (TILES, 3, PIX, PIX), 1.0, 6.0, ((0, 8), (2, 4))),
        "tile_home": draw_tile_home(jax.random.fold_in(key_of[10], 71), 0),
        "piece_tiles": draw_piece_tiles(jax.random.fold_in(key_of[10], 71), 0),
        "run_slot": touch_ends(jax.random.randint(key_of[3], (DETECTORS, SAMPLES // RUN), 0, LISTED), jax.random.fold_in(key_of[3], 1), 0, LISTED - 1).astype(jnp.int32),
        "hit_row": touch_ends(jax.random.randint(key_of[4], (DETECTORS, SAMPLES), 0, PIX - 1), jax.random.fold_in(key_of[4], 1), 0, (PIX - 1) - 1).astype(jnp.int32),
        "hit_col": touch_ends(jax.random.randint(key_of[5], (DETECTORS, SAMPLES), 0, PIX - 1), jax.random.fold_in(key_of[5], 1), 0, (PIX - 1) - 1).astype(jnp.int32),
        "frac_row": jnp.clip(1.0 * jax.random.uniform(key_of[6], (DETECTORS, SAMPLES), jnp.float32) ** block_scale(key_of[6], (DETECTORS, SAMPLES), ((0, 4), (1, 8)), -0.2, 0.2), 0.0, 1.0).astype(jnp.bfloat16),
        "frac_col": jnp.clip(1.0 * jax.random.uniform(key_of[7], (DETECTORS, SAMPLES), jnp.float32) ** block_scale(key_of[7], (DETECTORS, SAMPLES), ((0, 4), (1, 8)), -0.2, 0.2), 0.0, 1.0).astype(jnp.bfloat16),
        "angle": jnp.clip(jax.random.uniform(key_of[8], (DETECTORS, SAMPLES), jnp.float32, -3.140625, 3.140625), -3.140625, 3.140625),
        "noise_coef": gaussian(key_of[9], (DETECTORS, HALF_BAND + 1), 0.05, 0.3, ((0, 4),), jnp.float32),
    }


def rounded(values):
    return lax.optimization_barrier(values.astype(jnp.bfloat16)).astype(jnp.float32)


def reference(sky_map, tile_home, piece_tiles, run_slot, hit_row, hit_col, frac_row, frac_col, angle, noise_coef):
    position = tile_home[piece_tiles]
    det_group = (jnp.arange(DETECTORS) // DET_DEV).astype(jnp.int32)
    run_total = SAMPLES // RUN
    time_piece = (jnp.arange(run_total) * RUN // TIME_DEV).astype(jnp.int32)
    run_position = position[det_group[:, None], time_piece[None, :], run_slot]
    run_tile = jnp.repeat(run_position, RUN, axis=1).astype(jnp.int32)
    row_low = rounded(1.0 - frac_row.astype(jnp.float32))
    col_low = rounded(1.0 - frac_col.astype(jnp.float32))
    row_high = frac_row.astype(jnp.float32)
    col_high = frac_col.astype(jnp.float32)
    twice = 2.0 * angle.astype(jnp.float32)
    response = [jnp.ones_like(twice), jnp.cos(twice), jnp.sin(twice)]
    offset = (run_tile * (PIX * PIX) + hit_row * PIX + hit_col).astype(jnp.int32)
    sky_flat = sky_map.astype(jnp.float32).reshape(TILES, 3, PIX * PIX)
    signal = jnp.zeros((DETECTORS, SAMPLES), jnp.float32)
    for stokes in range(3):
        plane = sky_flat[:, stokes].reshape(-1)
        inner = row_low * (col_low * plane[offset] + col_high * plane[offset + 1])
        inner = inner + row_high * (col_low * plane[offset + PIX] + col_high * plane[offset + PIX + 1])
        signal = signal + response[stokes] * inner
    weights = jnp.concatenate([noise_coef[:, :1] + 1.0, noise_coef[:, 1:]], axis=1)
    kernel = jnp.concatenate([weights[:, ::-1], weights[:, 1:]], axis=1)
    length = SAMPLES + 2 * HALF_BAND
    spectrum = jnp.fft.rfft(signal, n=length, axis=1) * jnp.fft.rfft(kernel, n=length, axis=1)
    full_line = jnp.fft.irfft(spectrum, n=length, axis=1)
    filtered = full_line[:, HALF_BAND:HALF_BAND + SAMPLES]
    planes = []
    for stokes in range(3):
        scaled = response[stokes] * filtered
        low_part = rounded(scaled * row_low)
        high_part = rounded(scaled * row_high)
        summed = jnp.zeros((TILES * PIX * PIX,), jnp.float32)
        summed = summed.at[offset].add(low_part * col_low)
        summed = summed.at[offset + 1].add(low_part * col_high)
        summed = summed.at[offset + PIX].add(high_part * col_low)
        summed = summed.at[offset + PIX + 1].add(high_part * col_high)
        planes.append(summed.reshape(TILES, PIX, PIX))
    return jnp.stack(planes, axis=1)
```

```python
import functools
import math

import jax
import jax.numpy as jnp
from jax import lax
from jax.experimental import pallas as pl
from jax.experimental.pallas import tpu as pltpu
from jax.sharding import PartitionSpec as P

LISTED = 32


block_cols = 128
group_runs = 32


def extended_2(cells, sides, width):
    for axis, dim in sides:
        count = lax.axis_size(axis)
        ends = count - 1
        head = lax.slice_in_dim(cells, 0, width, axis=dim)
        tail = lax.slice_in_dim(cells, cells.shape[dim] - width, cells.shape[dim], axis=dim)
        cells = jnp.concatenate(
            [
                lax.ppermute(tail, axis, [(i, (i + 1) % count) for i in range(ends)]),
                cells,
                lax.ppermute(head, axis, [((i + 1) % count, i) for i in range(ends)]),
            ],
            axis=dim,
        )
    return cells


def positions_of(piece_list, tile_home):
    table_rows = jnp.arange(tile_home.shape[0], dtype=jnp.int32)
    matched = piece_list[:, None] == table_rows[None, :]
    return jnp.sum(jnp.where(matched, tile_home[None, :], 0), axis=1)


def run_weights(pixel_index, upper_frac, side_len):
    lower_weight = (1.0 - upper_frac.astype(jnp.float32)).astype(jnp.bfloat16)
    pixels = lax.broadcasted_iota(jnp.int32, pixel_index.shape + (side_len,), pixel_index.ndim)
    zero_value = jnp.zeros((), jnp.bfloat16)
    low_part = jnp.where(pixels == pixel_index[..., None], lower_weight[..., None], zero_value)
    high_part = jnp.where(pixels == pixel_index[..., None] + 1, upper_frac[..., None], zero_value)
    return low_part + high_part


def responses(angles):
    twice = 2.0 * angles
    return jnp.stack([jnp.ones_like(twice), jnp.cos(twice), jnp.sin(twice)], axis=1)


def banded(signal, noise_coef):
    det_count = signal.shape[0]
    half_band = noise_coef.shape[1] - 1
    reach_blocks = half_band // block_cols
    span_cols = (2 * reach_blocks + 1) * block_cols
    weights = jnp.concatenate([noise_coef[:, :1] + 1.0, noise_coef[:, 1:]], axis=1)
    zero_pad = jnp.zeros((det_count, block_cols - 1), jnp.float32)
    kernel_row = jnp.concatenate(
        [
            zero_pad,
            weights[:, ::-1],
            weights[:, 1:],
            zero_pad,
            jnp.zeros((det_count, 1), jnp.float32),
        ],
        axis=1,
    )
    period = span_cols + block_cols
    tiled_rows = jnp.tile(kernel_row, (1, block_cols))[:, : block_cols * (period - 1)]
    tiled_rows = tiled_rows.reshape(det_count, block_cols, period - 1)
    matrix = tiled_rows[:, :, block_cols - 1 : block_cols - 1 + span_cols]
    matrix = matrix.reshape(det_count, block_cols, 2 * reach_blocks + 1, block_cols)
    extended = extended_2(signal, (("tm", 1),), half_band)
    block_count = signal.shape[1] // block_cols
    blocks = extended.reshape(det_count, block_count + 2 * reach_blocks, block_cols)
    stacked = jnp.stack(
        [blocks[:, offset : offset + block_count] for offset in range(2 * reach_blocks + 1)], axis=1
    )
    result = jnp.einsum(
        "diml,dmnl->dni",
        matrix,
        stacked,
        precision=lax.Precision.HIGHEST,
        preferred_element_type=jnp.float32,
    )
    return result.reshape(det_count, block_count * block_cols)


GROUP = 4
META = 16
VMEM_LIMIT = 48 * 1024 * 1024
f32 = jnp.float32
bf16 = jnp.bfloat16


def round_up(value, step):
    return -(-value // step) * step


def iota(shape, dim):
    return lax.broadcasted_iota(jnp.int32, shape, dim)


def dot_nn(a, b):
    return lax.dot_general(a, b, (((1,), (0,)), ((), ())), preferred_element_type=f32)


def dot_nt(a, b):
    return lax.dot_general(a, b, (((1,), (1,)), ((), ())), preferred_element_type=f32)


def ones_where(mask):
    return jnp.where(mask, 1.0, 0.0).astype(bf16)


def pack_kernel(owners, cap, tile_dev, pt_ref, th_ref, slot_ref, r_ref, c_ref, fr_ref, fc_ref, ang_ref, out_ref, meta_ref):
    dets, blocks = slot_ref.shape
    runs = dets * blocks
    width = r_ref.shape[1] // blocks
    listed = pt_ref.shape[0]
    spread = dot_nn(
        slot_ref[...].astype(f32).astype(bf16),
        ones_where(iota((blocks, runs), 1) // dets == iota((blocks, runs), 0)),
    )
    run_id = iota((dets, runs), 1)
    own_det = run_id % dets == iota((dets, runs), 0)
    slot_row = jnp.sum(jnp.where(own_det, spread, 0.0), axis=0, keepdims=True)
    slot_row = slot_row.astype(jnp.int32)
    owner_row = jnp.zeros((1, runs), jnp.int32)
    tile_row = jnp.zeros((1, runs), jnp.int32)
    for k in range(listed):
        pos = th_ref[pt_ref[k]]
        own = lax.div(pos, jnp.int32(tile_dev))
        owner_row = jnp.where(slot_row == k, own, owner_row)
        tile_row = jnp.where(slot_row == k, pos - own * tile_dev, tile_row)
    owner_hot = iota((owners, runs), 0) == owner_row
    owner_one = ones_where(owner_hot)
    before = ones_where(iota((runs, runs), 0) < iota((runs, runs), 1))
    prefix = dot_nn(owner_one, before)
    rank = jnp.sum(jnp.where(owner_hot, prefix, 0.0), axis=0, keepdims=True).astype(jnp.int32)
    counts = dot_nt(jnp.ones((8, runs), bf16), owner_one)
    dest = jnp.where(rank < cap, owner_row * cap + rank, -1)
    place = ones_where(iota((owners * cap, runs), 0) == dest)

    def by_run(ref):
        return jnp.concatenate(
            [ref[:, b * width : (b + 1) * width].astype(f32) for b in range(blocks)], axis=0
        )

    angle = by_run(ang_ref)
    angle_high = angle.astype(bf16)
    angle_low = (angle - angle_high.astype(f32)).astype(bf16)
    fields = [by_run(ref).astype(bf16) for ref in (r_ref, c_ref, fr_ref, fc_ref)]
    fields += [angle_high, angle_low]
    for f, field in enumerate(fields):
        sent = dot_nn(place, field).astype(bf16)
        for o in range(owners):
            out_ref[o, f * cap : (f + 1) * cap, :] = sent[o * cap : (o + 1) * cap]
    sub = iota((8, runs), 0)
    lane_run = iota((8, runs), 1)
    facts = jnp.where(sub == 0, tile_row + 1, jnp.where(sub == 1, lane_run // dets, lane_run % dets))
    facts = dot_nt(facts.astype(f32).astype(bf16), place)
    meta_ref[...] = jnp.zeros_like(meta_ref)
    for o in range(owners):
        meta_ref[o, 0:8, 0:cap] = facts[:, o * cap : (o + 1) * cap]
        meta_ref[o, 8:16, 0:owners] = counts
    out_ref[:, len(fields) * cap :, :] = meta_ref[...].astype(bf16)


def weights_of(index, high, shape):
    rows = iota(shape, 0)
    low = (1.0 - high).astype(bf16).astype(f32)
    return jnp.where(rows == index, low, jnp.where(rows == index + 1, high, 0.0))


def project_kernel(
    cap, kept, recv_ref, tiles_ref, out_ref, fields_ref, ids_ref, seg_ref, scratch_ref, sig_ref, lanes_ref
):
    owners = recv_ref.shape[0]
    slots = owners * cap
    width = recv_ref.shape[2]
    groups_det, tile_dev, rows_dev, side = tiles_ref.shape
    part = rows_dev // 3
    for s in range(owners):
        lanes_ref[:, s * cap : (s + 1) * cap] = recv_ref[s, 6 * cap : 6 * cap + META, :].astype(f32)[0:8, 0:cap]
    facts = lanes_ref[...]
    tile1 = facts[0:1].astype(jnp.int32)
    tile_hot = iota((8, slots), 0) + 1 == tile1
    tile_one = ones_where(tile_hot)
    before = ones_where(iota((slots, slots), 0) < iota((slots, slots), 1))
    prefix = dot_nn(tile_one, before)
    count = jnp.sum(jnp.where(tile_hot, 1.0, 0.0), axis=1, keepdims=True)
    padded = jnp.floor((count + (GROUP - 1)) * (1.0 / GROUP)) * GROUP
    padded = jnp.broadcast_to(padded, (8, width))
    start = jnp.zeros((8, width), f32)
    for tile in range(tile_dev - 1):
        start += jnp.where(iota((8, width), 0) > tile, padded[tile : tile + 1], 0.0)
    stop = jnp.minimum(start + padded, float(kept))
    seg_ref[0:8, :] = start
    seg_ref[8:16, :] = stop
    where_to = jnp.sum(jnp.where(tile_hot, prefix + start[:, 0:1], 0.0), axis=0, keepdims=True)
    where_to = jnp.where(tile1 > 0, where_to, -1.0).astype(jnp.int32)
    order = ones_where(iota((kept, slots), 0) == where_to)
    source = (iota((1, slots), 1) // cap).astype(f32)
    sub = iota((8, slots), 0)
    facts = jnp.where(sub == 0, jnp.where(tile1 > 0, 1.0, 0.0), jnp.where(sub == 3, source, facts))
    facts = facts.astype(bf16)
    id_lanes = dot_nt(facts, order)
    scratch_ref[...] = jnp.zeros_like(scratch_ref)
    for q in range(-(-kept // width)):
        many = min(width, kept - q * width)
        scratch_ref[q * 8 : q * 8 + 8, 0:many] = id_lanes[:, q * width : q * width + many]
    ids_ref[...] = dot_nt(order, facts)
    sorted_fields = []
    for f in range(6):
        field = jnp.concatenate([recv_ref[s, f * cap : (f + 1) * cap, :] for s in range(owners)], axis=0)
        sorted_fields.append(dot_nn(order, field))
    twice = 2.0 * (sorted_fields[4] + sorted_fields[5])
    for f in range(4):
        fields_ref[f] = sorted_fields[f]
    fields_ref[4] = jnp.cos(twice)
    fields_ref[5] = jnp.sin(twice)
    sig_ref[...] = jnp.zeros_like(sig_ref)
    for tile in range(tile_dev):
        rows = jnp.concatenate([tiles_ref[d, tile] for d in range(groups_det)], axis=0)
        first = jnp.max(start[tile : tile + 1, :]).astype(jnp.int32) // GROUP
        last = jnp.max(stop[tile : tile + 1, :]).astype(jnp.int32) // GROUP

        def step(g, carry, rows=rows):
            base = g * GROUP
            cols = []
            for k in range(GROUP):
                c = fields_ref[1, pl.ds(base + k, 1), :].astype(jnp.int32)
                fc = fields_ref[3, pl.ds(base + k, 1), :]
                cols.append(weights_of(c, fc, (side, width)).astype(bf16))
            partial_rows = dot_nn(rows, jnp.concatenate(cols, axis=1))
            for k in range(GROUP):
                r = fields_ref[0, pl.ds(base + k, 1), :].astype(jnp.int32)
                fr = fields_ref[2, pl.ds(base + k, 1), :]
                row_weight = weights_of(r, fr, (side, width))
                values = []
                for p in range(3):
                    total = None
                    for d in range(groups_det):
                        at = d * rows_dev + p * part
                        term = partial_rows[at : at + part, k * width : (k + 1) * width]
                        term = term * row_weight[d * part : (d + 1) * part]
                        total = term if total is None else total + term
                    values.append(jnp.sum(total, axis=0, keepdims=True))
                cos = fields_ref[4, pl.ds(base + k, 1), :]
                sin = fields_ref[5, pl.ds(base + k, 1), :]
                sig_ref[pl.ds(base + k, 1), :] = values[0] + cos * values[1] + sin * values[2]
            return carry

        lax.fori_loop(first, last, step, 0)
    sent = sig_ref[...].astype(bf16)
    notes = scratch_ref[...].astype(bf16)

    def copy(o, carry):
        out_ref[o, 0:kept, :] = sent
        out_ref[o, kept:, :] = notes
        return carry

    lax.fori_loop(0, owners, copy, 0)


def toeplitz_kernel(line_ref, out_ref):
    width = out_ref.shape[2] // 2
    blocks = out_ref.shape[1] // width
    for m in range(blocks):
        at = (blocks - 1 - m) * width
        piece = jnp.broadcast_to(line_ref[0, :, at : at + 2 * width], (width, 2 * width))
        block = pltpu.roll(piece, width, 1, stride=1, stride_axis=0)[:, :width]
        high = block.astype(bf16)
        out_ref[0, m * width : (m + 1) * width, :width] = high
        out_ref[0, m * width : (m + 1) * width, width:] = (block - high.astype(f32)).astype(bf16)


def filter_kernel(kept, blocks_dev, recv_ref, mat_ref, out_ref, line_ref):
    det = pl.program_id(0)
    owners = recv_ref.shape[0]
    width = recv_ref.shape[2]
    count = owners * blocks_dev
    spans = mat_ref.shape[1] // width
    edge = spans // 2
    line_ref[...] = jnp.zeros_like(line_ref)
    rows = iota((count, kept), 0)

    def one(o, carry):
        notes = recv_ref[o, kept:, :].astype(f32)
        notes = jnp.concatenate([notes[q * 8 : q * 8 + 8] for q in range(notes.shape[0] // 8)], axis=1)[:, :kept]
        at = notes[3:4] * blocks_dev + notes[1:2]
        mine = jnp.logical_and(notes[0:1] > 0.5, notes[2:3] == det.astype(f32))
        at = jnp.where(mine, at, -1.0).astype(jnp.int32)
        line_ref[edge : edge + count, :] += dot_nn(ones_where(rows == at), recv_ref[o, 0:kept, :])
        return carry

    lax.fori_loop(0, owners, one, 0, unroll=owners <= 8)
    spread = jnp.concatenate([line_ref[m : m + count, :].astype(bf16) for m in range(spans)], axis=1)
    both = dot_nn(spread, mat_ref[0])
    out_ref[0] = both[:, :width] + both[:, width:]


def back_kernel(blocks_dev, fields_ref, ids_ref, seg_ref, filt_ref, out_ref, scaled_ref, acc_ref):
    width = fields_ref.shape[2]
    kept = fields_ref.shape[1]
    groups_det, tile_dev, rows_dev, side = out_ref.shape
    part = rows_dev // 3
    lines, count, _ = filt_ref.shape
    ids = ids_ref[...]
    at = ids[:, 2:3] * count + ids[:, 3:4] * blocks_dev + ids[:, 1:2]
    at = jnp.where(ids[:, 0:1] > 0.5, at, -1.0).astype(jnp.int32)
    filtered = jnp.zeros((kept, 2 * width), f32)
    for d in range(lines):
        line = filt_ref[d]
        high = line.astype(bf16)
        pair = jnp.concatenate([high, (line - high.astype(f32)).astype(bf16)], axis=1)
        filtered += dot_nn(ones_where(iota((kept, count), 1) + d * count == at), pair)
    filtered = filtered[:, :width] + filtered[:, width:]
    scaled_ref[0] = filtered
    scaled_ref[1] = filtered * fields_ref[4]
    scaled_ref[2] = filtered * fields_ref[5]
    for tile in range(tile_dev):
        first = jnp.max(seg_ref[tile : tile + 1, :]).astype(jnp.int32) // GROUP
        last = jnp.max(seg_ref[8 + tile : 9 + tile, :]).astype(jnp.int32) // GROUP
        acc_ref[...] = jnp.zeros_like(acc_ref)

        def step(g, carry):
            base = g * GROUP
            cols, terms = [], []
            for k in range(GROUP):
                c = fields_ref[1, pl.ds(base + k, 1), :].astype(jnp.int32)
                fc = fields_ref[3, pl.ds(base + k, 1), :]
                cols.append(weights_of(c, fc, (side, width)).astype(bf16))
                r = fields_ref[0, pl.ds(base + k, 1), :].astype(jnp.int32)
                fr = fields_ref[2, pl.ds(base + k, 1), :]
                row_weight = weights_of(r, fr, (side, width))
                terms.append(
                    jnp.concatenate(
                        [(scaled_ref[p, pl.ds(base + k, 1), :] * row_weight).astype(bf16) for p in range(3)],
                        axis=0,
                    )
                )
            acc_ref[...] += dot_nt(jnp.concatenate(terms, axis=1), jnp.concatenate(cols, axis=1))
            return carry

        lax.fori_loop(first, last, step, 0)
        for d in range(groups_det):
            for p in range(3):
                at_row = p * side + d * part
                out_ref[d, tile, p * part : (p + 1) * part, :] = acc_ref[at_row : at_row + part, :].astype(bf16)


def call(kernel, out, scratch=(), **more):
    return pl.pallas_call(
        kernel,
        out_shape=out,
        scratch_shapes=list(scratch),
        compiler_params=pltpu.CompilerParams(vmem_limit_bytes=VMEM_LIMIT),
        **more,
    )


def whole_tiles(
    tiles, position, run_slot, hit_row, hit_col, frac_row, frac_col, angle, noise_coef
):
    owner_total = lax.axis_size("tm")
    groups_det, tile_dev, rows_dev, side_len = tiles.shape
    part = rows_dev // 3
    owned_tiles = tiles.reshape(groups_det, tile_dev, 3, part, side_len)
    owned_tiles = owned_tiles.transpose(1, 2, 0, 3, 4).reshape(tile_dev, 3, side_len, side_len)
    listed_total = position.shape[0]
    per_owner = max(1, listed_total // owner_total)
    slot_total = owner_total * per_owner
    owner_of = position // tile_dev
    local_slot = position % tile_dev
    listing = jnp.arange(listed_total, dtype=jnp.int32)
    earlier_same = (owner_of[:, None] == owner_of[None, :]) & (listing[:, None] > listing[None, :])
    rank_within = jnp.sum(earlier_same.astype(jnp.int32), axis=1)
    outbox_row = owner_of * per_owner + rank_within
    slot_rows = jnp.arange(slot_total, dtype=jnp.int32)
    asked_slot = (
        jnp.sum(
            jnp.where(slot_rows[:, None] == outbox_row[None, :], local_slot[None, :] + 1, 0), axis=1
        )
        - 1
    )
    served_slot = lax.all_to_all(asked_slot, "tm", split_axis=0, concat_axis=0, tiled=True)
    every_tile = lax.all_gather(owned_tiles, "tm", axis=0, tiled=True)
    listed = jnp.take(every_tile, position, axis=0)
    det_local, time_local = hit_row.shape
    run_length = time_local // run_slot.shape[1]
    run_total = det_local * run_slot.shape[1]
    per_group = math.gcd(run_total, group_runs)
    group_total = run_total // per_group

    def grouped(values):
        return values.reshape(group_total, per_group, run_length)

    run_items = (
        run_slot.reshape(group_total, per_group),
        grouped(hit_row),
        grouped(hit_col),
        grouped(frac_row),
        grouped(frac_col),
        grouped(angle),
    )

    def project(items):
        slots, rows_at, cols_at, frac_rows, frac_cols, angles = items
        tiles = jnp.take(listed, slots, axis=0)
        row_weight = run_weights(rows_at, frac_rows, side_len).astype(jnp.float32)
        col_weight = run_weights(cols_at, frac_cols, side_len)
        partial_rows = jnp.einsum(
            "bpij,bsj->bpsi", tiles, col_weight, preferred_element_type=jnp.float32
        )
        values = jnp.sum(partial_rows * row_weight[:, None], axis=3)
        return jnp.sum(values * responses(angles), axis=1)

    signal = lax.map(project, run_items).reshape(det_local, time_local)
    filtered = banded(signal, noise_coef)

    def back_project(carry, items):
        slots, rows_at, cols_at, frac_rows, frac_cols, angles, filt_runs = items
        row_weight = run_weights(rows_at, frac_rows, side_len).astype(jnp.float32)
        col_weight = run_weights(cols_at, frac_cols, side_len)
        scaled = responses(angles) * filt_runs[:, None]
        weighted = (scaled[..., None] * row_weight[:, None]).astype(jnp.bfloat16)
        tile_terms = jnp.einsum(
            "bpsi,bsj->bpij", weighted, col_weight, preferred_element_type=jnp.float32
        )
        return (carry.at[slots].add(tile_terms), None)

    initial = jnp.zeros((listed_total, 3, side_len, side_len), jnp.float32)
    contrib, _ = lax.scan(back_project, initial, run_items + (grouped(filtered),))
    outbox = jnp.zeros((slot_total, 3, side_len, side_len), jnp.float32).at[outbox_row].set(contrib)
    arrived = lax.all_to_all(outbox, "tm", split_axis=0, concat_axis=0, tiled=True)
    summed = jnp.stack(
        [
            jnp.sum(jnp.where((served_slot == slot_id)[:, None, None, None], arrived, 0.0), axis=0)
            for slot_id in range(tile_dev)
        ]
    )
    summed = summed.reshape(tile_dev, 3, groups_det, part, side_len).transpose(2, 0, 1, 3, 4)
    return summed.reshape(groups_det, tile_dev, rows_dev, side_len).astype(jnp.bfloat16)


def body(
    sky_map,
    tile_home,
    piece_tiles,
    run_slot,
    hit_row,
    hit_col,
    frac_row,
    frac_col,
    angle,
    noise_coef,
):
    owners = lax.axis_size("tm")
    groups_det = lax.axis_size("det")
    tile_dev, _, part, side = sky_map.shape
    dets, blocks = run_slot.shape
    runs = dets * blocks
    width = hit_row.shape[1] // blocks
    listed = piece_tiles.shape[2]
    half_band = noise_coef.shape[1] - 1
    cap = round_up(2 * runs // min(owners, listed), META)
    kept = round_up(runs + runs // 2, META)
    slots = owners * cap
    piece_list = piece_tiles.reshape(listed)
    smem = pl.BlockSpec(memory_space=pltpu.SMEM)
    vmem = pl.BlockSpec(memory_space=pltpu.VMEM)

    packed = call(
        functools.partial(pack_kernel, owners, cap, tile_dev),
        jax.ShapeDtypeStruct((owners, 6 * cap + META, width), bf16),
        [pltpu.VMEM((owners, META, width), f32)],
        in_specs=[smem, smem] + [vmem] * 6,
        out_specs=vmem,
    )(piece_list, tile_home, run_slot, hit_row, hit_col, frac_row, frac_col, angle)
    recv = lax.all_to_all(packed, "tm", split_axis=0, concat_axis=0, tiled=True)
    tiles = lax.all_gather(sky_map.reshape(tile_dev, 3 * part, side), "det", axis=0)

    weights = jnp.concatenate([noise_coef[:, :1] + 1.0, noise_coef[:, 1:]], axis=1)
    line = jnp.concatenate(
        [
            jnp.zeros((dets, width), f32),
            weights[:, ::-1],
            weights[:, 1:],
            jnp.zeros((dets, width - 1), f32),
        ],
        axis=1,
    )
    spans = 2 * (half_band // width) + 1
    matrix = call(
        toeplitz_kernel,
        jax.ShapeDtypeStruct((dets, spans * width, 2 * width), bf16),
        grid=(dets,),
        in_specs=[pl.BlockSpec((1, 1, line.shape[1]), lambda d: (d, 0, 0))],
        out_specs=pl.BlockSpec((1, spans * width, 2 * width), lambda d: (d, 0, 0)),
    )(line[:, None, :])

    notes = round_up(kept, width) // width * 8
    sent, fields, ids, seg = call(
        functools.partial(project_kernel, cap, kept),
        (
            jax.ShapeDtypeStruct((owners, kept + notes, width), bf16),
            jax.ShapeDtypeStruct((6, kept, width), f32),
            jax.ShapeDtypeStruct((kept, 8), f32),
            jax.ShapeDtypeStruct((16, width), f32),
        ),
        [pltpu.VMEM((notes, width), f32), pltpu.VMEM((kept, width), f32), pltpu.VMEM((8, slots), f32)],
    )(recv, tiles)
    heard = lax.all_to_all(sent, "tm", split_axis=0, concat_axis=0, tiled=True)

    count = owners * blocks
    filtered = call(
        functools.partial(filter_kernel, kept, blocks),
        jax.ShapeDtypeStruct((dets, count, width), f32),
        [pltpu.VMEM((count + spans - 1, width), f32)],
        grid=(dets,),
        in_specs=[
            pl.BlockSpec((owners, kept + notes, width), lambda d: (0, 0, 0)),
            pl.BlockSpec((1, spans * width, 2 * width), lambda d: (d, 0, 0)),
        ],
        out_specs=pl.BlockSpec((1, count, width), lambda d: (d, 0, 0)),
    )(heard, matrix)
    share = call(
        functools.partial(back_kernel, blocks),
        jax.ShapeDtypeStruct((groups_det, tile_dev, 3 * part, side), bf16),
        [pltpu.VMEM((3, kept, width), f32), pltpu.VMEM((3 * side, side), f32)],
    )(fields, ids, seg, filtered)

    counts = recv[:, 6 * cap + 8, :owners].astype(f32)
    fits = (jnp.max(counts) <= cap) & (
        jnp.max(jnp.sum(counts, axis=0)) + tile_dev * (GROUP - 1) <= kept
    )

    def travelling(_):
        position = positions_of(piece_list, tile_home)
        return whole_tiles(
            tiles, position, run_slot, hit_row, hit_col, frac_row, frac_col, angle, noise_coef
        )

    share = lax.cond(fits, lambda s: s, travelling, share)
    shares = lax.all_to_all(share, "det", split_axis=0, concat_axis=0, tiled=True)
    total = jnp.sum(shares.reshape(groups_det, tile_dev, 3, part, side).astype(f32), axis=0)
    return total


def solution(mesh):
    placed = (
        P("tm", None, "det", None),
        P(),
        P("det", "tm", None),
        P("det", "tm"),
        P("det", "tm"),
        P("det", "tm"),
        P("det", "tm"),
        P("det", "tm"),
        P("det", "tm"),
        P("det", None),
    )
    return jax.shard_map(
        body, mesh=mesh, in_specs=placed, out_specs=P("tm", None, "det", None), check_vma=False
    )
```

```python
import functools
import math

import jax
import jax.numpy as jnp
from jax import lax
from jax.experimental import pallas as pl
from jax.experimental.pallas import tpu as pltpu
from jax.sharding import PartitionSpec as P

LISTED = 32


block_cols = 128
group_runs = 32


def extended_2(cells, sides, width):
    for axis, dim in sides:
        count = lax.axis_size(axis)
        ends = count - 1
        head = lax.slice_in_dim(cells, 0, width, axis=dim)
        tail = lax.slice_in_dim(cells, cells.shape[dim] - width, cells.shape[dim], axis=dim)
        cells = jnp.concatenate(
            [
                lax.ppermute(tail, axis, [(i, (i + 1) % count) for i in range(ends)]),
                cells,
                lax.ppermute(head, axis, [((i + 1) % count, i) for i in range(ends)]),
            ],
            axis=dim,
        )
    return cells


def positions_of(piece_list, tile_home):
    table_rows = jnp.arange(tile_home.shape[0], dtype=jnp.int32)
    matched = piece_list[:, None] == table_rows[None, :]
    return jnp.sum(jnp.where(matched, tile_home[None, :], 0), axis=1)


def run_weights(pixel_index, upper_frac, side_len):
    lower_weight = (1.0 - upper_frac.astype(jnp.float32)).astype(jnp.bfloat16)
    pixels = lax.broadcasted_iota(jnp.int32, pixel_index.shape + (side_len,), pixel_index.ndim)
    zero_value = jnp.zeros((), jnp.bfloat16)
    low_part = jnp.where(pixels == pixel_index[..., None], lower_weight[..., None], zero_value)
    high_part = jnp.where(pixels == pixel_index[..., None] + 1, upper_frac[..., None], zero_value)
    return low_part + high_part


def responses(angles):
    twice = 2.0 * angles
    return jnp.stack([jnp.ones_like(twice), jnp.cos(twice), jnp.sin(twice)], axis=1)


def banded(signal, noise_coef):
    det_count = signal.shape[0]
    half_band = noise_coef.shape[1] - 1
    reach_blocks = half_band // block_cols
    span_cols = (2 * reach_blocks + 1) * block_cols
    weights = jnp.concatenate([noise_coef[:, :1] + 1.0, noise_coef[:, 1:]], axis=1)
    zero_pad = jnp.zeros((det_count, block_cols - 1), jnp.float32)
    kernel_row = jnp.concatenate(
        [
            zero_pad,
            weights[:, ::-1],
            weights[:, 1:],
            zero_pad,
            jnp.zeros((det_count, 1), jnp.float32),
        ],
        axis=1,
    )
    period = span_cols + block_cols
    tiled_rows = jnp.tile(kernel_row, (1, block_cols))[:, : block_cols * (period - 1)]
    tiled_rows = tiled_rows.reshape(det_count, block_cols, period - 1)
    matrix = tiled_rows[:, :, block_cols - 1 : block_cols - 1 + span_cols]
    matrix = matrix.reshape(det_count, block_cols, 2 * reach_blocks + 1, block_cols)
    extended = extended_2(signal, (("tm", 1),), half_band)
    block_count = signal.shape[1] // block_cols
    blocks = extended.reshape(det_count, block_count + 2 * reach_blocks, block_cols)
    stacked = jnp.stack(
        [blocks[:, offset : offset + block_count] for offset in range(2 * reach_blocks + 1)], axis=1
    )
    result = jnp.einsum(
        "diml,dmnl->dni",
        matrix,
        stacked,
        precision=lax.Precision.HIGHEST,
        preferred_element_type=jnp.float32,
    )
    return result.reshape(det_count, block_count * block_cols)


GROUP = 4
META = 16
VMEM_LIMIT = 48 * 1024 * 1024
f32 = jnp.float32
bf16 = jnp.bfloat16


def round_up(value, step):
    return -(-value // step) * step


def iota(shape, dim):
    return lax.broadcasted_iota(jnp.int32, shape, dim)


def dot_nn(a, b):
    return lax.dot_general(a, b, (((1,), (0,)), ((), ())), preferred_element_type=f32)


def dot_nt(a, b):
    return lax.dot_general(a, b, (((1,), (1,)), ((), ())), preferred_element_type=f32)


def ones_where(mask):
    return jnp.where(mask, 1.0, 0.0).astype(bf16)


def pack_kernel(owners, cap, tile_dev, pt_ref, th_ref, slot_ref, r_ref, c_ref, fr_ref, fc_ref, ang_ref, out_ref, meta_ref):
    dets, blocks = slot_ref.shape
    runs = dets * blocks
    width = r_ref.shape[1] // blocks
    listed = pt_ref.shape[0]
    spread = dot_nn(
        slot_ref[...].astype(f32).astype(bf16),
        ones_where(iota((blocks, runs), 1) // dets == iota((blocks, runs), 0)),
    )
    run_id = iota((dets, runs), 1)
    own_det = run_id % dets == iota((dets, runs), 0)
    slot_row = jnp.sum(jnp.where(own_det, spread, 0.0), axis=0, keepdims=True)
    slot_row = slot_row.astype(jnp.int32)
    owner_row = jnp.zeros((1, runs), jnp.int32)
    tile_row = jnp.zeros((1, runs), jnp.int32)
    for k in range(listed):
        pos = th_ref[pt_ref[k]]
        own = lax.div(pos, jnp.int32(tile_dev))
        owner_row = jnp.where(slot_row == k, own, owner_row)
        tile_row = jnp.where(slot_row == k, pos - own * tile_dev, tile_row)
    owner_hot = iota((owners, runs), 0) == owner_row
    owner_one = ones_where(owner_hot)
    before = ones_where(iota((runs, runs), 0) < iota((runs, runs), 1))
    prefix = dot_nn(owner_one, before)
    rank = jnp.sum(jnp.where(owner_hot, prefix, 0.0), axis=0, keepdims=True).astype(jnp.int32)
    counts = dot_nt(jnp.ones((8, runs), bf16), owner_one)
    dest = jnp.where(rank < cap, owner_row * cap + rank, -1)
    place = ones_where(iota((owners * cap, runs), 0) == dest)

    def by_run(ref):
        return jnp.concatenate(
            [ref[:, b * width : (b + 1) * width].astype(f32) for b in range(blocks)], axis=0
        )

    angle = by_run(ang_ref)
    angle_high = angle.astype(bf16)
    angle_low = (angle - angle_high.astype(f32)).astype(bf16)
    fields = [by_run(ref).astype(bf16) for ref in (r_ref, c_ref, fr_ref, fc_ref)]
    fields += [angle_high, angle_low]
    for f, field in enumerate(fields):
        sent = dot_nn(place, field).astype(bf16)
        for o in range(owners):
            out_ref[o, f * cap : (f + 1) * cap, :] = sent[o * cap : (o + 1) * cap]
    sub = iota((8, runs), 0)
    lane_run = iota((8, runs), 1)
    facts = jnp.where(sub == 0, tile_row + 1, jnp.where(sub == 1, lane_run // dets, lane_run % dets))
    facts = dot_nt(facts.astype(f32).astype(bf16), place)
    meta_ref[...] = jnp.zeros_like(meta_ref)
    for o in range(owners):
        meta_ref[o, 0:8, 0:cap] = facts[:, o * cap : (o + 1) * cap]
        meta_ref[o, 8:16, 0:owners] = counts
    out_ref[:, len(fields) * cap :, :] = meta_ref[...].astype(bf16)


def weights_of(index, high, shape):
    rows = iota(shape, 0)
    low = (1.0 - high).astype(bf16).astype(f32)
    return jnp.where(rows == index, low, jnp.where(rows == index + 1, high, 0.0))


def project_kernel(
    cap, kept, recv_ref, tiles_ref, out_ref, fields_ref, ids_ref, seg_ref, scratch_ref, sig_ref, lanes_ref
):
    owners = recv_ref.shape[0]
    slots = owners * cap
    width = recv_ref.shape[2]
    groups_det, tile_dev, rows_dev, side = tiles_ref.shape
    part = rows_dev // 3
    for s in range(owners):
        lanes_ref[:, s * cap : (s + 1) * cap] = recv_ref[s, 6 * cap : 6 * cap + META, :].astype(f32)[0:8, 0:cap]
    facts = lanes_ref[...]
    tile1 = facts[0:1].astype(jnp.int32)
    tile_hot = iota((8, slots), 0) + 1 == tile1
    tile_one = ones_where(tile_hot)
    before = ones_where(iota((slots, slots), 0) < iota((slots, slots), 1))
    prefix = dot_nn(tile_one, before)
    count = jnp.sum(jnp.where(tile_hot, 1.0, 0.0), axis=1, keepdims=True)
    padded = jnp.floor((count + (GROUP - 1)) * (1.0 / GROUP)) * GROUP
    padded = jnp.broadcast_to(padded, (8, width))
    start = jnp.zeros((8, width), f32)
    for tile in range(tile_dev - 1):
        start += jnp.where(iota((8, width), 0) > tile, padded[tile : tile + 1], 0.0)
    stop = jnp.minimum(start + padded, float(kept))
    seg_ref[0:8, :] = start
    seg_ref[8:16, :] = stop
    at = 6 * cap + 8
    counts = jnp.concatenate([recv_ref[s, at : at + 8, :].astype(f32)[0:1] for s in range(owners)], axis=0)
    most = jnp.max(jnp.max(counts, axis=0, keepdims=True), axis=1, keepdims=True)
    fullest = jnp.max(jnp.sum(counts, axis=0, keepdims=True), axis=1, keepdims=True)
    over = jnp.logical_or(most > cap, fullest + tile_dev * (GROUP - 1) > kept)
    seg_ref[16:24, :] = jnp.broadcast_to(jnp.where(over, 1.0, 0.0), (8, width))
    where_to = jnp.sum(jnp.where(tile_hot, prefix + start[:, 0:1], 0.0), axis=0, keepdims=True)
    where_to = jnp.where(tile1 > 0, where_to, -1.0).astype(jnp.int32)
    order = ones_where(iota((kept, slots), 0) == where_to)
    source = (iota((1, slots), 1) // cap).astype(f32)
    sub = iota((8, slots), 0)
    facts = jnp.where(sub == 0, jnp.where(tile1 > 0, 1.0, 0.0), jnp.where(sub == 3, source, facts))
    facts = facts.astype(bf16)
    id_lanes = dot_nt(facts, order)
    scratch_ref[...] = jnp.zeros_like(scratch_ref)
    for q in range(-(-kept // width)):
        many = min(width, kept - q * width)
        scratch_ref[q * 8 : q * 8 + 8, 0:many] = id_lanes[:, q * width : q * width + many]
    ids_ref[...] = dot_nt(order, facts)
    sorted_fields = []
    for f in range(6):
        field = jnp.concatenate([recv_ref[s, f * cap : (f + 1) * cap, :] for s in range(owners)], axis=0)
        sorted_fields.append(dot_nn(order, field))
    twice = 2.0 * (sorted_fields[4] + sorted_fields[5])
    for f in range(4):
        fields_ref[f] = sorted_fields[f]
    fields_ref[4] = jnp.cos(twice)
    fields_ref[5] = jnp.sin(twice)
    sig_ref[...] = jnp.zeros_like(sig_ref)
    for tile in range(tile_dev):
        rows = jnp.concatenate([tiles_ref[d, tile] for d in range(groups_det)], axis=0)
        first = jnp.max(start[tile : tile + 1, :]).astype(jnp.int32) // GROUP
        last = jnp.max(stop[tile : tile + 1, :]).astype(jnp.int32) // GROUP

        def step(g, carry, rows=rows):
            base = g * GROUP
            cols = []
            for k in range(GROUP):
                c = fields_ref[1, pl.ds(base + k, 1), :].astype(jnp.int32)
                fc = fields_ref[3, pl.ds(base + k, 1), :]
                cols.append(weights_of(c, fc, (side, width)).astype(bf16))
            partial_rows = dot_nn(rows, jnp.concatenate(cols, axis=1))
            for k in range(GROUP):
                r = fields_ref[0, pl.ds(base + k, 1), :].astype(jnp.int32)
                fr = fields_ref[2, pl.ds(base + k, 1), :]
                row_weight = weights_of(r, fr, (side, width))
                values = []
                for p in range(3):
                    total = None
                    for d in range(groups_det):
                        at = d * rows_dev + p * part
                        term = partial_rows[at : at + part, k * width : (k + 1) * width]
                        term = term * row_weight[d * part : (d + 1) * part]
                        total = term if total is None else total + term
                    values.append(jnp.sum(total, axis=0, keepdims=True))
                cos = fields_ref[4, pl.ds(base + k, 1), :]
                sin = fields_ref[5, pl.ds(base + k, 1), :]
                sig_ref[pl.ds(base + k, 1), :] = values[0] + cos * values[1] + sin * values[2]
            return carry

        lax.fori_loop(first, last, step, 0)
    sent = sig_ref[...].astype(bf16)
    notes = scratch_ref[...].astype(bf16)

    def copy(o, carry):
        out_ref[o, 0:kept, :] = sent
        out_ref[o, kept:, :] = notes
        return carry

    lax.fori_loop(0, owners, copy, 0)


def toeplitz_kernel(line_ref, out_ref):
    width = out_ref.shape[2] // 2
    blocks = out_ref.shape[1] // width
    for m in range(blocks):
        at = (blocks - 1 - m) * width
        piece = jnp.broadcast_to(line_ref[0, :, at : at + 2 * width], (width, 2 * width))
        block = pltpu.roll(piece, width, 1, stride=1, stride_axis=0)[:, :width]
        high = block.astype(bf16)
        out_ref[0, m * width : (m + 1) * width, :width] = high
        out_ref[0, m * width : (m + 1) * width, width:] = (block - high.astype(f32)).astype(bf16)


def filter_kernel(kept, blocks_dev, recv_ref, mat_ref, out_ref, line_ref):
    det = pl.program_id(0)
    owners = recv_ref.shape[0]
    width = recv_ref.shape[2]
    count = owners * blocks_dev
    spans = mat_ref.shape[1] // width
    edge = spans // 2
    line_ref[...] = jnp.zeros_like(line_ref)
    rows = iota((count, kept), 0)

    def one(o, carry):
        notes = recv_ref[o, kept:, :].astype(f32)
        notes = jnp.concatenate([notes[q * 8 : q * 8 + 8] for q in range(notes.shape[0] // 8)], axis=1)[:, :kept]
        at = notes[3:4] * blocks_dev + notes[1:2]
        mine = jnp.logical_and(notes[0:1] > 0.5, notes[2:3] == det.astype(f32))
        at = jnp.where(mine, at, -1.0).astype(jnp.int32)
        line_ref[edge : edge + count, :] += dot_nn(ones_where(rows == at), recv_ref[o, 0:kept, :])
        return carry

    lax.fori_loop(0, owners, one, 0, unroll=owners <= 8)
    spread = jnp.concatenate([line_ref[m : m + count, :].astype(bf16) for m in range(spans)], axis=1)
    both = dot_nn(spread, mat_ref[0])
    out_ref[0] = both[:, :width] + both[:, width:]


def back_kernel(
    blocks_dev, core_ref, fields_ref, ids_ref, seg_ref, filt_ref, mine_ref, theirs_ref, scaled_ref, acc_ref
):
    width = fields_ref.shape[2]
    kept = fields_ref.shape[1]
    pairs, tile_dev, rows_dev, side = mine_ref.shape
    part = rows_dev // 3
    core = core_ref[0]
    poison = jnp.where(seg_ref[16:17, :] > 0.5, jnp.nan, 0.0)
    lines, count, _ = filt_ref.shape
    ids = ids_ref[...]
    at = ids[:, 2:3] * count + ids[:, 3:4] * blocks_dev + ids[:, 1:2]
    at = jnp.where(ids[:, 0:1] > 0.5, at, -1.0).astype(jnp.int32)
    filtered = jnp.zeros((kept, 2 * width), f32)
    for d in range(lines):
        line = filt_ref[d]
        high = line.astype(bf16)
        pair = jnp.concatenate([high, (line - high.astype(f32)).astype(bf16)], axis=1)
        filtered += dot_nn(ones_where(iota((kept, count), 1) + d * count == at), pair)
    filtered = filtered[:, :width] + filtered[:, width:]
    scaled_ref[0] = filtered
    scaled_ref[1] = filtered * fields_ref[4]
    scaled_ref[2] = filtered * fields_ref[5]
    for tile in range(tile_dev):
        first = jnp.max(seg_ref[tile : tile + 1, :]).astype(jnp.int32) // GROUP
        last = jnp.max(seg_ref[8 + tile : 9 + tile, :]).astype(jnp.int32) // GROUP
        acc_ref[...] = jnp.zeros_like(acc_ref)

        def step(g, carry):
            base = g * GROUP
            cols, terms = [], []
            for k in range(GROUP):
                c = fields_ref[1, pl.ds(base + k, 1), :].astype(jnp.int32)
                fc = fields_ref[3, pl.ds(base + k, 1), :]
                cols.append(weights_of(c, fc, (side, width)).astype(bf16))
                r = fields_ref[0, pl.ds(base + k, 1), :].astype(jnp.int32)
                fr = fields_ref[2, pl.ds(base + k, 1), :]
                row_weight = weights_of(r, fr, (side, width))
                terms.append(
                    jnp.concatenate(
                        [(scaled_ref[p, pl.ds(base + k, 1), :] * row_weight).astype(bf16) for p in range(3)],
                        axis=0,
                    )
                )
            acc_ref[...] += dot_nt(jnp.concatenate(terms, axis=1), jnp.concatenate(cols, axis=1))
            return carry

        lax.fori_loop(first, last, step, 0)
        for h in range(pairs):
            for p in range(3):
                base = p * side + h * 2 * part
                mine = acc_ref[pl.ds(pl.multiple_of(base + core * part, part), part), :]
                theirs = acc_ref[pl.ds(pl.multiple_of(base + (1 - core) * part, part), part), :]
                mine_ref[h, tile, p * part : (p + 1) * part, :] = mine + poison
                theirs_ref[h, tile, p * part : (p + 1) * part, :] = (theirs + poison).astype(bf16)


def call(kernel, out, scratch=(), **more):
    return pl.pallas_call(
        kernel,
        out_shape=out,
        scratch_shapes=list(scratch),
        compiler_params=pltpu.CompilerParams(vmem_limit_bytes=VMEM_LIMIT),
        **more,
    )


def whole_tiles(
    tiles, position, run_slot, hit_row, hit_col, frac_row, frac_col, angle, noise_coef
):
    owner_total = lax.axis_size("tm")
    groups_det, tile_dev, rows_dev, side_len = tiles.shape
    part = rows_dev // 3
    owned_tiles = tiles.reshape(groups_det, tile_dev, 3, part, side_len)
    owned_tiles = owned_tiles.transpose(1, 2, 0, 3, 4).reshape(tile_dev, 3, side_len, side_len)
    listed_total = position.shape[0]
    per_owner = max(1, listed_total // owner_total)
    slot_total = owner_total * per_owner
    owner_of = position // tile_dev
    local_slot = position % tile_dev
    listing = jnp.arange(listed_total, dtype=jnp.int32)
    earlier_same = (owner_of[:, None] == owner_of[None, :]) & (listing[:, None] > listing[None, :])
    rank_within = jnp.sum(earlier_same.astype(jnp.int32), axis=1)
    outbox_row = owner_of * per_owner + rank_within
    slot_rows = jnp.arange(slot_total, dtype=jnp.int32)
    asked_slot = (
        jnp.sum(
            jnp.where(slot_rows[:, None] == outbox_row[None, :], local_slot[None, :] + 1, 0), axis=1
        )
        - 1
    )
    served_slot = lax.all_to_all(asked_slot, "tm", split_axis=0, concat_axis=0, tiled=True)
    every_tile = lax.all_gather(owned_tiles, "tm", axis=0, tiled=True)
    listed = jnp.take(every_tile, position, axis=0)
    det_local, time_local = hit_row.shape
    run_length = time_local // run_slot.shape[1]
    run_total = det_local * run_slot.shape[1]
    per_group = math.gcd(run_total, group_runs)
    group_total = run_total // per_group

    def grouped(values):
        return values.reshape(group_total, per_group, run_length)

    run_items = (
        run_slot.reshape(group_total, per_group),
        grouped(hit_row),
        grouped(hit_col),
        grouped(frac_row),
        grouped(frac_col),
        grouped(angle),
    )

    def project(items):
        slots, rows_at, cols_at, frac_rows, frac_cols, angles = items
        tiles = jnp.take(listed, slots, axis=0)
        row_weight = run_weights(rows_at, frac_rows, side_len).astype(jnp.float32)
        col_weight = run_weights(cols_at, frac_cols, side_len)
        partial_rows = jnp.einsum(
            "bpij,bsj->bpsi", tiles, col_weight, preferred_element_type=jnp.float32
        )
        values = jnp.sum(partial_rows * row_weight[:, None], axis=3)
        return jnp.sum(values * responses(angles), axis=1)

    signal = lax.map(project, run_items).reshape(det_local, time_local)
    filtered = banded(signal, noise_coef)

    def back_project(carry, items):
        slots, rows_at, cols_at, frac_rows, frac_cols, angles, filt_runs = items
        row_weight = run_weights(rows_at, frac_rows, side_len).astype(jnp.float32)
        col_weight = run_weights(cols_at, frac_cols, side_len)
        scaled = responses(angles) * filt_runs[:, None]
        weighted = (scaled[..., None] * row_weight[:, None]).astype(jnp.bfloat16)
        tile_terms = jnp.einsum(
            "bpsi,bsj->bpij", weighted, col_weight, preferred_element_type=jnp.float32
        )
        return (carry.at[slots].add(tile_terms), None)

    initial = jnp.zeros((listed_total, 3, side_len, side_len), jnp.float32)
    contrib, _ = lax.scan(back_project, initial, run_items + (grouped(filtered),))
    outbox = jnp.zeros((slot_total, 3, side_len, side_len), jnp.float32).at[outbox_row].set(contrib)
    arrived = lax.all_to_all(outbox, "tm", split_axis=0, concat_axis=0, tiled=True)
    summed = jnp.stack(
        [
            jnp.sum(jnp.where((served_slot == slot_id)[:, None, None, None], arrived, 0.0), axis=0)
            for slot_id in range(tile_dev)
        ]
    )
    return lax.psum_scatter(summed, "det", scatter_dimension=2, tiled=True)


def body(
    sky_map,
    tile_home,
    piece_tiles,
    run_slot,
    hit_row,
    hit_col,
    frac_row,
    frac_col,
    angle,
    noise_coef,
):
    owners = lax.axis_size("tm")
    groups_det = lax.axis_size("det")
    tile_dev, _, part, side = sky_map.shape
    dets, blocks = run_slot.shape
    runs = dets * blocks
    width = hit_row.shape[1] // blocks
    listed = piece_tiles.shape[2]
    half_band = noise_coef.shape[1] - 1
    cap = round_up(2 * runs // min(owners, listed), META)
    kept = round_up(runs + runs // 2, META)
    slots = owners * cap
    piece_list = piece_tiles.reshape(listed)
    smem = pl.BlockSpec(memory_space=pltpu.SMEM)
    vmem = pl.BlockSpec(memory_space=pltpu.VMEM)

    packed = call(
        functools.partial(pack_kernel, owners, cap, tile_dev),
        jax.ShapeDtypeStruct((owners, 6 * cap + META, width), bf16),
        [pltpu.VMEM((owners, META, width), f32)],
        in_specs=[smem, smem] + [vmem] * 6,
        out_specs=vmem,
    )(piece_list, tile_home, run_slot, hit_row, hit_col, frac_row, frac_col, angle)
    recv = lax.all_to_all(packed, "tm", split_axis=0, concat_axis=0, tiled=True)
    tiles = lax.all_gather(sky_map.reshape(tile_dev, 3 * part, side), "det", axis=0)

    weights = jnp.concatenate([noise_coef[:, :1] + 1.0, noise_coef[:, 1:]], axis=1)
    line = jnp.concatenate(
        [
            jnp.zeros((dets, width), f32),
            weights[:, ::-1],
            weights[:, 1:],
            jnp.zeros((dets, width - 1), f32),
        ],
        axis=1,
    )
    spans = 2 * (half_band // width) + 1
    matrix = call(
        toeplitz_kernel,
        jax.ShapeDtypeStruct((dets, spans * width, 2 * width), bf16),
        grid=(dets,),
        in_specs=[pl.BlockSpec((1, 1, line.shape[1]), lambda d: (d, 0, 0))],
        out_specs=pl.BlockSpec((1, spans * width, 2 * width), lambda d: (d, 0, 0)),
    )(line[:, None, :])

    notes = round_up(kept, width) // width * 8
    sent, fields, ids, seg = call(
        functools.partial(project_kernel, cap, kept),
        (
            jax.ShapeDtypeStruct((owners, kept + notes, width), bf16),
            jax.ShapeDtypeStruct((6, kept, width), f32),
            jax.ShapeDtypeStruct((kept, 8), f32),
            jax.ShapeDtypeStruct((24, width), f32),
        ),
        [pltpu.VMEM((notes, width), f32), pltpu.VMEM((kept, width), f32), pltpu.VMEM((8, slots), f32)],
    )(recv, tiles)
    heard = lax.all_to_all(sent, "tm", split_axis=0, concat_axis=0, tiled=True)

    count = owners * blocks
    filtered = call(
        functools.partial(filter_kernel, kept, blocks),
        jax.ShapeDtypeStruct((dets, count, width), f32),
        [pltpu.VMEM((count + spans - 1, width), f32)],
        grid=(dets,),
        in_specs=[
            pl.BlockSpec((owners, kept + notes, width), lambda d: (0, 0, 0)),
            pl.BlockSpec((1, spans * width, 2 * width), lambda d: (d, 0, 0)),
        ],
        out_specs=pl.BlockSpec((1, count, width), lambda d: (d, 0, 0)),
    )(heard, matrix)
    place = lax.axis_index("det")
    core = lax.rem(place, 2)
    half = lax.div(place, 2)
    pairs = groups_det // 2
    mine, theirs = call(
        functools.partial(back_kernel, blocks),
        (
            jax.ShapeDtypeStruct((pairs, tile_dev, 3 * part, side), f32),
            jax.ShapeDtypeStruct((pairs, tile_dev, 3 * part, side), bf16),
        ),
        [pltpu.VMEM((3, kept, width), f32), pltpu.VMEM((3 * side, side), f32)],
        in_specs=[smem] + [vmem] * 4,
        out_specs=(vmem, vmem),
    )(core[None].astype(jnp.int32), fields, ids, seg, filtered)

    beside = lax.ppermute(theirs, "det", [(i, i ^ 1) for i in range(groups_det)])

    def of_pair(h):
        pick = lambda values: lax.dynamic_index_in_dim(values, h, 0, keepdims=False).astype(f32)
        return pick(mine) + pick(beside)

    total = of_pair(half)
    for step in range(1, pairs):
        ring = [(i, (i + 2 * step) % groups_det) for i in range(groups_det)]
        total = total + lax.ppermute(
            of_pair(lax.rem(half + step, pairs)).astype(bf16), "det", ring
        ).astype(f32)
    total = total.reshape(tile_dev, 3, part, side)

    def travelling(_):
        position = positions_of(piece_list, tile_home)
        return whole_tiles(
            tiles, position, run_slot, hit_row, hit_col, frac_row, frac_col, angle, noise_coef
        )

    fits = jnp.logical_not(jnp.isnan(total[0, 0, 0, 0]))
    return lax.cond(fits, lambda t: t, travelling, total)


def solution(mesh):
    placed = (
        P("tm", None, "det", None),
        P(),
        P("det", "tm", None),
        P("det", "tm"),
        P("det", "tm"),
        P("det", "tm"),
        P("det", "tm"),
        P("det", "tm"),
        P("det", "tm"),
        P("det", None),
    )
    return jax.shard_map(
        body, mesh=mesh, in_specs=placed, out_specs=P("tm", None, "det", None), check_vma=False
    )
```

```python
import functools
import math

import jax
import jax.numpy as jnp
from jax import lax
from jax.experimental import pallas as pl
from jax.experimental.pallas import tpu as pltpu
from jax.sharding import PartitionSpec as P

LISTED = 32


block_cols = 128
group_runs = 32


def extended_2(cells, sides, width):
    for axis, dim in sides:
        count = lax.axis_size(axis)
        ends = count - 1
        head = lax.slice_in_dim(cells, 0, width, axis=dim)
        tail = lax.slice_in_dim(cells, cells.shape[dim] - width, cells.shape[dim], axis=dim)
        cells = jnp.concatenate(
            [
                lax.ppermute(tail, axis, [(i, (i + 1) % count) for i in range(ends)]),
                cells,
                lax.ppermute(head, axis, [((i + 1) % count, i) for i in range(ends)]),
            ],
            axis=dim,
        )
    return cells


def positions_of(piece_list, tile_home):
    table_rows = jnp.arange(tile_home.shape[0], dtype=jnp.int32)
    matched = piece_list[:, None] == table_rows[None, :]
    return jnp.sum(jnp.where(matched, tile_home[None, :], 0), axis=1)


def run_weights(pixel_index, upper_frac, side_len):
    lower_weight = (1.0 - upper_frac.astype(jnp.float32)).astype(jnp.bfloat16)
    pixels = lax.broadcasted_iota(jnp.int32, pixel_index.shape + (side_len,), pixel_index.ndim)
    zero_value = jnp.zeros((), jnp.bfloat16)
    low_part = jnp.where(pixels == pixel_index[..., None], lower_weight[..., None], zero_value)
    high_part = jnp.where(pixels == pixel_index[..., None] + 1, upper_frac[..., None], zero_value)
    return low_part + high_part


def responses(angles):
    twice = 2.0 * angles
    return jnp.stack([jnp.ones_like(twice), jnp.cos(twice), jnp.sin(twice)], axis=1)


def banded(signal, noise_coef):
    det_count = signal.shape[0]
    half_band = noise_coef.shape[1] - 1
    reach_blocks = half_band // block_cols
    span_cols = (2 * reach_blocks + 1) * block_cols
    weights = jnp.concatenate([noise_coef[:, :1] + 1.0, noise_coef[:, 1:]], axis=1)
    zero_pad = jnp.zeros((det_count, block_cols - 1), jnp.float32)
    kernel_row = jnp.concatenate(
        [
            zero_pad,
            weights[:, ::-1],
            weights[:, 1:],
            zero_pad,
            jnp.zeros((det_count, 1), jnp.float32),
        ],
        axis=1,
    )
    period = span_cols + block_cols
    tiled_rows = jnp.tile(kernel_row, (1, block_cols))[:, : block_cols * (period - 1)]
    tiled_rows = tiled_rows.reshape(det_count, block_cols, period - 1)
    matrix = tiled_rows[:, :, block_cols - 1 : block_cols - 1 + span_cols]
    matrix = matrix.reshape(det_count, block_cols, 2 * reach_blocks + 1, block_cols)
    extended = extended_2(signal, (("tm", 1),), half_band)
    block_count = signal.shape[1] // block_cols
    blocks = extended.reshape(det_count, block_count + 2 * reach_blocks, block_cols)
    stacked = jnp.stack(
        [blocks[:, offset : offset + block_count] for offset in range(2 * reach_blocks + 1)], axis=1
    )
    result = jnp.einsum(
        "diml,dmnl->dni",
        matrix,
        stacked,
        precision=lax.Precision.HIGHEST,
        preferred_element_type=jnp.float32,
    )
    return result.reshape(det_count, block_count * block_cols)


GROUP = 4
META = 16
VMEM_LIMIT = 48 * 1024 * 1024
f32 = jnp.float32
bf16 = jnp.bfloat16


def round_up(value, step):
    return -(-value // step) * step


def iota(shape, dim):
    return lax.broadcasted_iota(jnp.int32, shape, dim)


def dot_nn(a, b):
    return lax.dot_general(a, b, (((1,), (0,)), ((), ())), preferred_element_type=f32)


def dot_nt(a, b):
    return lax.dot_general(a, b, (((1,), (1,)), ((), ())), preferred_element_type=f32)


def ones_where(mask):
    return jnp.where(mask, 1.0, 0.0).astype(bf16)


def pack_kernel(owners, cap, tile_dev, pt_ref, th_ref, slot_ref, r_ref, c_ref, fr_ref, fc_ref, ang_ref, out_ref, meta_ref):
    dets, blocks = slot_ref.shape
    runs = dets * blocks
    width = r_ref.shape[1] // blocks
    listed = pt_ref.shape[0]
    spread = dot_nn(
        slot_ref[...].astype(f32).astype(bf16),
        ones_where(iota((blocks, runs), 1) // dets == iota((blocks, runs), 0)),
    )
    run_id = iota((dets, runs), 1)
    own_det = run_id % dets == iota((dets, runs), 0)
    slot_row = jnp.sum(jnp.where(own_det, spread, 0.0), axis=0, keepdims=True)
    slot_row = slot_row.astype(jnp.int32)
    owner_row = jnp.zeros((1, runs), jnp.int32)
    tile_row = jnp.zeros((1, runs), jnp.int32)
    for k in range(listed):
        pos = th_ref[pt_ref[k]]
        own = lax.div(pos, jnp.int32(tile_dev))
        owner_row = jnp.where(slot_row == k, own, owner_row)
        tile_row = jnp.where(slot_row == k, pos - own * tile_dev, tile_row)
    owner_hot = iota((owners, runs), 0) == owner_row
    owner_one = ones_where(owner_hot)
    before = ones_where(iota((runs, runs), 0) < iota((runs, runs), 1))
    prefix = dot_nn(owner_one, before)
    rank = jnp.sum(jnp.where(owner_hot, prefix, 0.0), axis=0, keepdims=True).astype(jnp.int32)
    counts = dot_nt(jnp.ones((8, runs), bf16), owner_one)
    dest = jnp.where(rank < cap, owner_row * cap + rank, -1)
    place = ones_where(iota((owners * cap, runs), 0) == dest)

    def by_run(ref):
        return jnp.concatenate(
            [ref[:, b * width : (b + 1) * width].astype(f32) for b in range(blocks)], axis=0
        )

    angle = by_run(ang_ref)
    angle_high = angle.astype(bf16)
    angle_low = (angle - angle_high.astype(f32)).astype(bf16)
    fields = [by_run(ref).astype(bf16) for ref in (r_ref, c_ref, fr_ref, fc_ref)]
    fields += [angle_high, angle_low]
    for f, field in enumerate(fields):
        sent = dot_nn(place, field).astype(bf16)
        for o in range(owners):
            out_ref[o, f * cap : (f + 1) * cap, :] = sent[o * cap : (o + 1) * cap]
    sub = iota((8, runs), 0)
    lane_run = iota((8, runs), 1)
    facts = jnp.where(sub == 0, tile_row + 1, jnp.where(sub == 1, lane_run // dets, lane_run % dets))
    facts = dot_nt(facts.astype(f32).astype(bf16), place)
    meta_ref[...] = jnp.zeros_like(meta_ref)
    for o in range(owners):
        meta_ref[o, 0:8, 0:cap] = facts[:, o * cap : (o + 1) * cap]
        meta_ref[o, 8:16, 0:owners] = counts
    out_ref[:, len(fields) * cap :, :] = meta_ref[...].astype(bf16)


def weights_of(index, high, shape):
    rows = iota(shape, 0)
    low = (1.0 - high).astype(bf16).astype(f32)
    return jnp.where(rows == index, low, jnp.where(rows == index + 1, high, 0.0))


def project_kernel(
    cap, kept, recv_ref, tiles_ref, out_ref, fields_ref, ids_ref, seg_ref, scratch_ref, sig_ref, lanes_ref
):
    owners = recv_ref.shape[0]
    slots = owners * cap
    width = recv_ref.shape[2]
    groups_det, tile_dev, rows_dev, side = tiles_ref.shape
    part = rows_dev // 3
    for s in range(owners):
        lanes_ref[:, s * cap : (s + 1) * cap] = recv_ref[s, 6 * cap : 6 * cap + META, :].astype(f32)[0:8, 0:cap]
    facts = lanes_ref[...]
    tile1 = facts[0:1].astype(jnp.int32)
    tile_hot = iota((8, slots), 0) + 1 == tile1
    tile_one = ones_where(tile_hot)
    before = ones_where(iota((slots, slots), 0) < iota((slots, slots), 1))
    prefix = dot_nn(tile_one, before)
    count = jnp.sum(jnp.where(tile_hot, 1.0, 0.0), axis=1, keepdims=True)
    padded = jnp.floor((count + (GROUP - 1)) * (1.0 / GROUP)) * GROUP
    padded = jnp.broadcast_to(padded, (8, width))
    start = jnp.zeros((8, width), f32)
    for tile in range(tile_dev - 1):
        start += jnp.where(iota((8, width), 0) > tile, padded[tile : tile + 1], 0.0)
    stop = jnp.minimum(start + padded, float(kept))
    seg_ref[0:8, :] = start
    seg_ref[8:16, :] = stop
    at = 6 * cap + 8
    counts = jnp.concatenate([recv_ref[s, at : at + 8, :].astype(f32)[0:1] for s in range(owners)], axis=0)
    most = jnp.max(jnp.max(counts, axis=0, keepdims=True), axis=1, keepdims=True)
    fullest = jnp.max(jnp.sum(counts, axis=0, keepdims=True), axis=1, keepdims=True)
    over = jnp.logical_or(most > cap, fullest + tile_dev * (GROUP - 1) > kept)
    seg_ref[16:24, :] = jnp.broadcast_to(jnp.where(over, 1.0, 0.0), (8, width))
    where_to = jnp.sum(jnp.where(tile_hot, prefix + start[:, 0:1], 0.0), axis=0, keepdims=True)
    where_to = jnp.where(tile1 > 0, where_to, -1.0).astype(jnp.int32)
    order = ones_where(iota((kept, slots), 0) == where_to)
    source = (iota((1, slots), 1) // cap).astype(f32)
    sub = iota((8, slots), 0)
    facts = jnp.where(sub == 0, jnp.where(tile1 > 0, 1.0, 0.0), jnp.where(sub == 3, source, facts))
    facts = facts.astype(bf16)
    id_lanes = dot_nt(facts, order)
    scratch_ref[...] = jnp.zeros_like(scratch_ref)
    for q in range(-(-kept // width)):
        many = min(width, kept - q * width)
        scratch_ref[q * 8 : q * 8 + 8, 0:many] = id_lanes[:, q * width : q * width + many]
    ids_ref[...] = dot_nt(order, facts)
    sorted_fields = []
    for f in range(6):
        field = jnp.concatenate([recv_ref[s, f * cap : (f + 1) * cap, :] for s in range(owners)], axis=0)
        sorted_fields.append(dot_nn(order, field))
    twice = 2.0 * (sorted_fields[4] + sorted_fields[5])
    for f in range(4):
        fields_ref[f] = sorted_fields[f]
    fields_ref[4] = jnp.cos(twice)
    fields_ref[5] = jnp.sin(twice)
    sig_ref[...] = jnp.zeros_like(sig_ref)
    for tile in range(tile_dev):
        rows = jnp.concatenate([tiles_ref[d, tile] for d in range(groups_det)], axis=0)
        first = jnp.max(start[tile : tile + 1, :]).astype(jnp.int32) // GROUP
        last = jnp.max(stop[tile : tile + 1, :]).astype(jnp.int32) // GROUP

        def step(g, carry, rows=rows):
            base = g * GROUP
            cols = []
            for k in range(GROUP):
                c = fields_ref[1, pl.ds(base + k, 1), :].astype(jnp.int32)
                fc = fields_ref[3, pl.ds(base + k, 1), :]
                cols.append(weights_of(c, fc, (side, width)).astype(bf16))
            partial_rows = dot_nn(rows, jnp.concatenate(cols, axis=1))
            for k in range(GROUP):
                r = fields_ref[0, pl.ds(base + k, 1), :].astype(jnp.int32)
                fr = fields_ref[2, pl.ds(base + k, 1), :]
                row_weight = weights_of(r, fr, (side, width))
                values = []
                for p in range(3):
                    total = None
                    for d in range(groups_det):
                        at = d * rows_dev + p * part
                        term = partial_rows[at : at + part, k * width : (k + 1) * width]
                        term = term * row_weight[d * part : (d + 1) * part]
                        total = term if total is None else total + term
                    values.append(jnp.sum(total, axis=0, keepdims=True))
                cos = fields_ref[4, pl.ds(base + k, 1), :]
                sin = fields_ref[5, pl.ds(base + k, 1), :]
                sig_ref[pl.ds(base + k, 1), :] = values[0] + cos * values[1] + sin * values[2]
            return carry

        lax.fori_loop(first, last, step, 0)
    sent = sig_ref[...].astype(bf16)
    notes = scratch_ref[...].astype(bf16)

    def copy(o, carry):
        out_ref[o, 0:kept, :] = sent
        out_ref[o, kept:, :] = notes
        return carry

    lax.fori_loop(0, owners, copy, 0)


def toeplitz_kernel(line_ref, out_ref):
    width = out_ref.shape[2] // 2
    blocks = out_ref.shape[1] // width
    for m in range(blocks):
        at = (blocks - 1 - m) * width
        piece = jnp.broadcast_to(line_ref[0, :, at : at + 2 * width], (width, 2 * width))
        block = pltpu.roll(piece, width, 1, stride=1, stride_axis=0)[:, :width]
        high = block.astype(bf16)
        out_ref[0, m * width : (m + 1) * width, :width] = high
        out_ref[0, m * width : (m + 1) * width, width:] = (block - high.astype(f32)).astype(bf16)


def filter_kernel(kept, blocks_dev, recv_ref, mat_ref, out_ref, line_ref):
    det = pl.program_id(0)
    owners = recv_ref.shape[0]
    width = recv_ref.shape[2]
    count = owners * blocks_dev
    spans = mat_ref.shape[1] // width
    edge = spans // 2
    line_ref[...] = jnp.zeros_like(line_ref)
    rows = iota((count, kept), 0)

    def one(o, carry):
        notes = recv_ref[o, kept:, :].astype(f32)
        notes = jnp.concatenate([notes[q * 8 : q * 8 + 8] for q in range(notes.shape[0] // 8)], axis=1)[:, :kept]
        at = notes[3:4] * blocks_dev + notes[1:2]
        mine = jnp.logical_and(notes[0:1] > 0.5, notes[2:3] == det.astype(f32))
        at = jnp.where(mine, at, -1.0).astype(jnp.int32)
        line_ref[edge : edge + count, :] += dot_nn(ones_where(rows == at), recv_ref[o, 0:kept, :])
        return carry

    lax.fori_loop(0, owners, one, 0, unroll=owners <= 8)
    spread = jnp.concatenate([line_ref[m : m + count, :].astype(bf16) for m in range(spans)], axis=1)
    both = dot_nn(spread, mat_ref[0])
    out_ref[0] = both[:, :width] + both[:, width:]


def back_kernel(
    blocks_dev, core_ref, fields_ref, ids_ref, seg_ref, filt_ref, mine_ref, theirs_ref, scaled_ref, acc_ref
):
    width = fields_ref.shape[2]
    kept = fields_ref.shape[1]
    pairs, tile_dev, rows_dev, side = mine_ref.shape
    part = rows_dev // 3
    core = core_ref[0]
    poison = jnp.where(seg_ref[16:17, :] > 0.5, jnp.nan, 0.0)
    lines, count, _ = filt_ref.shape
    ids = ids_ref[...]
    at = ids[:, 2:3] * count + ids[:, 3:4] * blocks_dev + ids[:, 1:2]
    at = jnp.where(ids[:, 0:1] > 0.5, at, -1.0).astype(jnp.int32)
    filtered = jnp.zeros((kept, 2 * width), f32)
    for d in range(lines):
        line = filt_ref[d]
        high = line.astype(bf16)
        pair = jnp.concatenate([high, (line - high.astype(f32)).astype(bf16)], axis=1)
        filtered += dot_nn(ones_where(iota((kept, count), 1) + d * count == at), pair)
    filtered = filtered[:, :width] + filtered[:, width:]
    scaled_ref[0] = filtered
    scaled_ref[1] = filtered * fields_ref[4]
    scaled_ref[2] = filtered * fields_ref[5]
    for tile in range(tile_dev):
        first = jnp.max(seg_ref[tile : tile + 1, :]).astype(jnp.int32) // GROUP
        last = jnp.max(seg_ref[8 + tile : 9 + tile, :]).astype(jnp.int32) // GROUP
        acc_ref[...] = jnp.zeros_like(acc_ref)

        def step(g, carry):
            base = g * GROUP
            cols, terms = [], []
            for k in range(GROUP):
                c = fields_ref[1, pl.ds(base + k, 1), :].astype(jnp.int32)
                fc = fields_ref[3, pl.ds(base + k, 1), :]
                cols.append(weights_of(c, fc, (side, width)).astype(bf16))
                r = fields_ref[0, pl.ds(base + k, 1), :].astype(jnp.int32)
                fr = fields_ref[2, pl.ds(base + k, 1), :]
                row_weight = weights_of(r, fr, (side, width))
                terms.append(
                    jnp.concatenate(
                        [(scaled_ref[p, pl.ds(base + k, 1), :] * row_weight).astype(bf16) for p in range(3)],
                        axis=0,
                    )
                )
            acc_ref[...] += dot_nt(jnp.concatenate(terms, axis=1), jnp.concatenate(cols, axis=1))
            return carry

        lax.fori_loop(first, last, step, 0)
        for h in range(pairs):
            for p in range(3):
                base = p * side + h * 2 * part
                mine = acc_ref[pl.ds(pl.multiple_of(base + core * part, part), part), :]
                theirs = acc_ref[pl.ds(pl.multiple_of(base + (1 - core) * part, part), part), :]
                mine_ref[h, tile, p * part : (p + 1) * part, :] = mine + poison
                theirs_ref[h, tile, p * part : (p + 1) * part, :] = (theirs + poison).astype(bf16)


def call(kernel, out, scratch=(), **more):
    return pl.pallas_call(
        kernel,
        out_shape=out,
        scratch_shapes=list(scratch),
        compiler_params=pltpu.CompilerParams(vmem_limit_bytes=VMEM_LIMIT),
        **more,
    )


def whole_tiles(
    tiles, position, run_slot, hit_row, hit_col, frac_row, frac_col, angle, noise_coef
):
    owner_total = lax.axis_size("tm")
    groups_det, tile_dev, rows_dev, side_len = tiles.shape
    part = rows_dev // 3
    owned_tiles = tiles.reshape(groups_det, tile_dev, 3, part, side_len)
    owned_tiles = owned_tiles.transpose(1, 2, 0, 3, 4).reshape(tile_dev, 3, side_len, side_len)
    listed_total = position.shape[0]
    per_owner = max(1, listed_total // owner_total)
    slot_total = owner_total * per_owner
    owner_of = position // tile_dev
    local_slot = position % tile_dev
    listing = jnp.arange(listed_total, dtype=jnp.int32)
    earlier_same = (owner_of[:, None] == owner_of[None, :]) & (listing[:, None] > listing[None, :])
    rank_within = jnp.sum(earlier_same.astype(jnp.int32), axis=1)
    outbox_row = owner_of * per_owner + rank_within
    slot_rows = jnp.arange(slot_total, dtype=jnp.int32)
    asked_slot = (
        jnp.sum(
            jnp.where(slot_rows[:, None] == outbox_row[None, :], local_slot[None, :] + 1, 0), axis=1
        )
        - 1
    )
    served_slot = lax.all_to_all(asked_slot, "tm", split_axis=0, concat_axis=0, tiled=True)
    every_tile = jnp.broadcast_to(owned_tiles[None], (owner_total,) + owned_tiles.shape)
    every_tile = lax.all_to_all(every_tile, "tm", split_axis=0, concat_axis=0)
    every_tile = every_tile.reshape((owner_total * tile_dev,) + owned_tiles.shape[1:])
    listed = jnp.take(every_tile, position, axis=0)
    det_local, time_local = hit_row.shape
    run_length = time_local // run_slot.shape[1]
    run_total = det_local * run_slot.shape[1]
    per_group = math.gcd(run_total, group_runs)
    group_total = run_total // per_group

    def grouped(values):
        return values.reshape(group_total, per_group, run_length)

    run_items = (
        run_slot.reshape(group_total, per_group),
        grouped(hit_row),
        grouped(hit_col),
        grouped(frac_row),
        grouped(frac_col),
        grouped(angle),
    )

    def project(items):
        slots, rows_at, cols_at, frac_rows, frac_cols, angles = items
        tiles = jnp.take(listed, slots, axis=0)
        row_weight = run_weights(rows_at, frac_rows, side_len).astype(jnp.float32)
        col_weight = run_weights(cols_at, frac_cols, side_len)
        partial_rows = jnp.einsum(
            "bpij,bsj->bpsi", tiles, col_weight, preferred_element_type=jnp.float32
        )
        values = jnp.sum(partial_rows * row_weight[:, None], axis=3)
        return jnp.sum(values * responses(angles), axis=1)

    signal = lax.map(project, run_items).reshape(det_local, time_local)
    filtered = banded(signal, noise_coef)

    def back_project(carry, items):
        slots, rows_at, cols_at, frac_rows, frac_cols, angles, filt_runs = items
        row_weight = run_weights(rows_at, frac_rows, side_len).astype(jnp.float32)
        col_weight = run_weights(cols_at, frac_cols, side_len)
        scaled = responses(angles) * filt_runs[:, None]
        weighted = (scaled[..., None] * row_weight[:, None]).astype(jnp.bfloat16)
        tile_terms = jnp.einsum(
            "bpsi,bsj->bpij", weighted, col_weight, preferred_element_type=jnp.float32
        )
        return (carry.at[slots].add(tile_terms), None)

    initial = jnp.zeros((listed_total, 3, side_len, side_len), jnp.float32)
    contrib, _ = lax.scan(back_project, initial, run_items + (grouped(filtered),))
    outbox = jnp.zeros((slot_total, 3, side_len, side_len), jnp.float32).at[outbox_row].set(contrib)
    arrived = lax.all_to_all(outbox, "tm", split_axis=0, concat_axis=0, tiled=True)
    summed = jnp.stack(
        [
            jnp.sum(jnp.where((served_slot == slot_id)[:, None, None, None], arrived, 0.0), axis=0)
            for slot_id in range(tile_dev)
        ]
    )
    summed = summed.reshape(tile_dev, 3, groups_det, part, side_len)
    shares = lax.all_to_all(summed, "det", split_axis=2, concat_axis=0)
    return jnp.sum(shares.reshape(groups_det, tile_dev, 3, part, side_len), axis=0)


def body(
    sky_map,
    tile_home,
    piece_tiles,
    run_slot,
    hit_row,
    hit_col,
    frac_row,
    frac_col,
    angle,
    noise_coef,
):
    owners = lax.axis_size("tm")
    groups_det = lax.axis_size("det")
    tile_dev, _, part, side = sky_map.shape
    dets, blocks = run_slot.shape
    runs = dets * blocks
    width = hit_row.shape[1] // blocks
    listed = piece_tiles.shape[2]
    half_band = noise_coef.shape[1] - 1
    cap = round_up(2 * runs // min(owners, listed), META)
    kept = round_up(runs + runs // 2, META)
    slots = owners * cap
    piece_list = piece_tiles.reshape(listed)
    smem = pl.BlockSpec(memory_space=pltpu.SMEM)
    vmem = pl.BlockSpec(memory_space=pltpu.VMEM)

    packed = call(
        functools.partial(pack_kernel, owners, cap, tile_dev),
        jax.ShapeDtypeStruct((owners, 6 * cap + META, width), bf16),
        [pltpu.VMEM((owners, META, width), f32)],
        in_specs=[smem, smem] + [vmem] * 6,
        out_specs=vmem,
    )(piece_list, tile_home, run_slot, hit_row, hit_col, frac_row, frac_col, angle)
    recv = lax.all_to_all(packed, "tm", split_axis=0, concat_axis=0, tiled=True)
    tiles = lax.all_gather(sky_map.reshape(tile_dev, 3 * part, side), "det", axis=0)

    weights = jnp.concatenate([noise_coef[:, :1] + 1.0, noise_coef[:, 1:]], axis=1)
    line = jnp.concatenate(
        [
            jnp.zeros((dets, width), f32),
            weights[:, ::-1],
            weights[:, 1:],
            jnp.zeros((dets, width - 1), f32),
        ],
        axis=1,
    )
    spans = 2 * (half_band // width) + 1
    matrix = call(
        toeplitz_kernel,
        jax.ShapeDtypeStruct((dets, spans * width, 2 * width), bf16),
        grid=(dets,),
        in_specs=[pl.BlockSpec((1, 1, line.shape[1]), lambda d: (d, 0, 0))],
        out_specs=pl.BlockSpec((1, spans * width, 2 * width), lambda d: (d, 0, 0)),
    )(line[:, None, :])

    notes = round_up(kept, width) // width * 8
    sent, fields, ids, seg = call(
        functools.partial(project_kernel, cap, kept),
        (
            jax.ShapeDtypeStruct((owners, kept + notes, width), bf16),
            jax.ShapeDtypeStruct((6, kept, width), f32),
            jax.ShapeDtypeStruct((kept, 8), f32),
            jax.ShapeDtypeStruct((24, width), f32),
        ),
        [pltpu.VMEM((notes, width), f32), pltpu.VMEM((kept, width), f32), pltpu.VMEM((8, slots), f32)],
    )(recv, tiles)
    heard = lax.all_to_all(sent, "tm", split_axis=0, concat_axis=0, tiled=True)

    count = owners * blocks
    filtered = call(
        functools.partial(filter_kernel, kept, blocks),
        jax.ShapeDtypeStruct((dets, count, width), f32),
        [pltpu.VMEM((count + spans - 1, width), f32)],
        grid=(dets,),
        in_specs=[
            pl.BlockSpec((owners, kept + notes, width), lambda d: (0, 0, 0)),
            pl.BlockSpec((1, spans * width, 2 * width), lambda d: (d, 0, 0)),
        ],
        out_specs=pl.BlockSpec((1, count, width), lambda d: (d, 0, 0)),
    )(heard, matrix)
    place = lax.axis_index("det")
    core = lax.rem(place, 2)
    half = lax.div(place, 2)
    pairs = groups_det // 2
    mine, theirs = call(
        functools.partial(back_kernel, blocks),
        (
            jax.ShapeDtypeStruct((pairs, tile_dev, 3 * part, side), f32),
            jax.ShapeDtypeStruct((pairs, tile_dev, 3 * part, side), bf16),
        ),
        [pltpu.VMEM((3, kept, width), f32), pltpu.VMEM((3 * side, side), f32)],
        in_specs=[smem] + [vmem] * 4,
        out_specs=(vmem, vmem),
    )(core[None].astype(jnp.int32), fields, ids, seg, filtered)

    beside = lax.ppermute(theirs, "det", [(i, i ^ 1) for i in range(groups_det)])

    def of_pair(h):
        pick = lambda values: lax.dynamic_index_in_dim(values, h, 0, keepdims=False).astype(f32)
        return pick(mine) + pick(beside)

    total = of_pair(half)
    for step in range(1, pairs):
        ring = [(i, (i + 2 * step) % groups_det) for i in range(groups_det)]
        total = total + lax.ppermute(
            of_pair(lax.rem(half + step, pairs)).astype(bf16), "det", ring
        ).astype(f32)
    total = total.reshape(tile_dev, 3, part, side)

    def travelling(_):
        position = positions_of(piece_list, tile_home)
        return whole_tiles(
            tiles, position, run_slot, hit_row, hit_col, frac_row, frac_col, angle, noise_coef
        )

    fits = jnp.logical_not(jnp.isnan(total[0, 0, 0, 0]))
    return lax.cond(fits, lambda t: t, travelling, total)


def solution(mesh):
    placed = (
        P("tm", None, "det", None),
        P(),
        P("det", "tm", None),
        P("det", "tm"),
        P("det", "tm"),
        P("det", "tm"),
        P("det", "tm"),
        P("det", "tm"),
        P("det", "tm"),
        P("det", None),
    )
    return jax.shard_map(
        body, mesh=mesh, in_specs=placed, out_specs=P("tm", None, "det", None), check_vma=False
    )
```

```python
import functools
import math

import jax
import jax.numpy as jnp
from jax import lax
from jax.experimental import pallas as pl
from jax.experimental.pallas import tpu as pltpu
from jax.sharding import PartitionSpec as P

LISTED = 32


block_cols = 128
group_runs = 32


def extended_2(cells, sides, width):
    for axis, dim in sides:
        count = lax.axis_size(axis)
        ends = count - 1
        head = lax.slice_in_dim(cells, 0, width, axis=dim)
        tail = lax.slice_in_dim(cells, cells.shape[dim] - width, cells.shape[dim], axis=dim)
        cells = jnp.concatenate(
            [
                lax.ppermute(tail, axis, [(i, (i + 1) % count) for i in range(ends)]),
                cells,
                lax.ppermute(head, axis, [((i + 1) % count, i) for i in range(ends)]),
            ],
            axis=dim,
        )
    return cells


def positions_of(piece_list, tile_home):
    table_rows = jnp.arange(tile_home.shape[0], dtype=jnp.int32)
    matched = piece_list[:, None] == table_rows[None, :]
    return jnp.sum(jnp.where(matched, tile_home[None, :], 0), axis=1)


def run_weights(pixel_index, upper_frac, side_len):
    lower_weight = (1.0 - upper_frac.astype(jnp.float32)).astype(jnp.bfloat16)
    pixels = lax.broadcasted_iota(jnp.int32, pixel_index.shape + (side_len,), pixel_index.ndim)
    zero_value = jnp.zeros((), jnp.bfloat16)
    low_part = jnp.where(pixels == pixel_index[..., None], lower_weight[..., None], zero_value)
    high_part = jnp.where(pixels == pixel_index[..., None] + 1, upper_frac[..., None], zero_value)
    return low_part + high_part


def responses(angles):
    twice = 2.0 * angles
    return jnp.stack([jnp.ones_like(twice), jnp.cos(twice), jnp.sin(twice)], axis=1)


def banded(signal, noise_coef):
    det_count = signal.shape[0]
    half_band = noise_coef.shape[1] - 1
    reach_blocks = half_band // block_cols
    span_cols = (2 * reach_blocks + 1) * block_cols
    weights = jnp.concatenate([noise_coef[:, :1] + 1.0, noise_coef[:, 1:]], axis=1)
    zero_pad = jnp.zeros((det_count, block_cols - 1), jnp.float32)
    kernel_row = jnp.concatenate(
        [
            zero_pad,
            weights[:, ::-1],
            weights[:, 1:],
            zero_pad,
            jnp.zeros((det_count, 1), jnp.float32),
        ],
        axis=1,
    )
    period = span_cols + block_cols
    tiled_rows = jnp.tile(kernel_row, (1, block_cols))[:, : block_cols * (period - 1)]
    tiled_rows = tiled_rows.reshape(det_count, block_cols, period - 1)
    matrix = tiled_rows[:, :, block_cols - 1 : block_cols - 1 + span_cols]
    matrix = matrix.reshape(det_count, block_cols, 2 * reach_blocks + 1, block_cols)
    extended = extended_2(signal, (("tm", 1),), half_band)
    block_count = signal.shape[1] // block_cols
    blocks = extended.reshape(det_count, block_count + 2 * reach_blocks, block_cols)
    stacked = jnp.stack(
        [blocks[:, offset : offset + block_count] for offset in range(2 * reach_blocks + 1)], axis=1
    )
    result = jnp.einsum(
        "diml,dmnl->dni",
        matrix,
        stacked,
        precision=lax.Precision.HIGHEST,
        preferred_element_type=jnp.float32,
    )
    return result.reshape(det_count, block_count * block_cols)


GROUP = 4
UNROLL = 4
META = 16
VMEM_LIMIT = 40 * 1024 * 1024
f32 = jnp.float32
bf16 = jnp.bfloat16


def round_up(value, step):
    return -(-value // step) * step


def iota(shape, dim):
    return lax.broadcasted_iota(jnp.int32, shape, dim)


def dot_nn(a, b):
    return lax.dot_general(a, b, (((1,), (0,)), ((), ())), preferred_element_type=f32)


def dot_nt(a, b):
    return lax.dot_general(a, b, (((1,), (1,)), ((), ())), preferred_element_type=f32)


def ones_where(mask):
    return jnp.where(mask, 1.0, 0.0).astype(bf16)


def pack_kernel(owners, cap, tile_dev, pt_ref, th_ref, slot_ref, r_ref, c_ref, fr_ref, fc_ref, ang_ref, out_ref, meta_ref):
    dets, blocks = slot_ref.shape
    runs = dets * blocks
    width = r_ref.shape[1] // blocks
    listed = pt_ref.shape[0]
    spread = dot_nn(
        slot_ref[...].astype(f32).astype(bf16),
        ones_where(iota((blocks, runs), 1) // dets == iota((blocks, runs), 0)),
    )
    run_id = iota((dets, runs), 1)
    own_det = run_id % dets == iota((dets, runs), 0)
    slot_row = jnp.sum(jnp.where(own_det, spread, 0.0), axis=0, keepdims=True)
    slot_row = slot_row.astype(jnp.int32)
    owner_row = jnp.zeros((1, runs), jnp.int32)
    tile_row = jnp.zeros((1, runs), jnp.int32)
    for k in range(listed):
        pos = th_ref[pt_ref[k]]
        own = lax.div(pos, jnp.int32(tile_dev))
        owner_row = jnp.where(slot_row == k, own, owner_row)
        tile_row = jnp.where(slot_row == k, pos - own * tile_dev, tile_row)
    owner_hot = iota((owners, runs), 0) == owner_row
    owner_one = ones_where(owner_hot)
    before = ones_where(iota((runs, runs), 0) < iota((runs, runs), 1))
    prefix = dot_nn(owner_one, before)
    rank = jnp.sum(jnp.where(owner_hot, prefix, 0.0), axis=0, keepdims=True).astype(jnp.int32)
    counts = dot_nt(jnp.ones((8, runs), bf16), owner_one)
    dest = jnp.where(rank < cap, owner_row * cap + rank, -1)
    place = ones_where(iota((owners * cap, runs), 0) == dest)

    def by_run(ref):
        return jnp.concatenate(
            [ref[:, b * width : (b + 1) * width].astype(f32) for b in range(blocks)], axis=0
        )

    angle = by_run(ang_ref)
    angle_high = angle.astype(bf16)
    angle_low = (angle - angle_high.astype(f32)).astype(bf16)
    fields = [by_run(ref).astype(bf16) for ref in (r_ref, c_ref, fr_ref, fc_ref)]
    fields += [angle_high, angle_low]
    for f, field in enumerate(fields):
        sent = dot_nn(place, field).astype(bf16)
        for o in range(owners):
            out_ref[o, f * cap : (f + 1) * cap, :] = sent[o * cap : (o + 1) * cap]
    sub = iota((8, runs), 0)
    lane_run = iota((8, runs), 1)
    facts = jnp.where(sub == 0, tile_row + 1, jnp.where(sub == 1, lane_run // dets, lane_run % dets))
    facts = dot_nt(facts.astype(f32).astype(bf16), place)
    meta_ref[...] = jnp.zeros_like(meta_ref)
    for o in range(owners):
        meta_ref[o, 0:8, 0:cap] = facts[:, o * cap : (o + 1) * cap]
        meta_ref[o, 8:16, 0:owners] = counts
    out_ref[:, len(fields) * cap :, :] = meta_ref[...].astype(bf16)


def weights_of(fields_ref, axis, run, shape):
    index, high, low = (
        fields_ref[f + axis, pl.ds(run, 1), :].astype(bf16) for f in (0, 2, 6)
    )
    rows = iota(shape, 0).astype(f32).astype(bf16)
    zero = jnp.zeros((), bf16)
    return jnp.where(rows == index, low, jnp.where(rows == index + 1, high, zero))


def segments(seg_ref, tile_dev):
    return [
        jnp.max(seg_ref[8 + tile : 9 + tile, :]).astype(jnp.int32) // GROUP for tile in range(tile_dev)
    ]


def tile_of(group, ends):
    tile = jnp.int32(0)
    for end in ends[:-1]:
        tile = tile + (group >= end).astype(jnp.int32)
    return tile


def project_kernel(
    cap, kept, recv_ref, tiles_ref, out_ref, fields_ref, ids_ref, seg_ref, scratch_ref, sig_ref, lanes_ref
):
    owners = recv_ref.shape[0]
    slots = owners * cap
    width = recv_ref.shape[2]
    groups_det, tile_dev, rows_dev, side = tiles_ref.shape
    part = rows_dev // 3
    for s in range(owners):
        lanes_ref[:, s * cap : (s + 1) * cap] = recv_ref[s, 6 * cap : 6 * cap + META, :].astype(f32)[0:8, 0:cap]
    facts = lanes_ref[...]
    tile1 = facts[0:1].astype(jnp.int32)
    tile_hot = iota((8, slots), 0) + 1 == tile1
    tile_one = ones_where(tile_hot)
    before = ones_where(iota((slots, slots), 0) < iota((slots, slots), 1))
    prefix = dot_nn(tile_one, before)
    count = jnp.sum(jnp.where(tile_hot, 1.0, 0.0), axis=1, keepdims=True)
    padded = jnp.floor((count + (GROUP - 1)) * (1.0 / GROUP)) * GROUP
    padded = jnp.broadcast_to(padded, (8, width))
    start = jnp.zeros((8, width), f32)
    for tile in range(tile_dev - 1):
        start += jnp.where(iota((8, width), 0) > tile, padded[tile : tile + 1], 0.0)
    stop = jnp.minimum(start + padded, float(kept))
    seg_ref[0:8, :] = start
    seg_ref[8:16, :] = stop
    at = 6 * cap + 8
    counts = jnp.concatenate([recv_ref[s, at : at + 8, :].astype(f32)[0:1] for s in range(owners)], axis=0)
    most = jnp.max(jnp.max(counts, axis=0, keepdims=True), axis=1, keepdims=True)
    fullest = jnp.max(jnp.sum(counts, axis=0, keepdims=True), axis=1, keepdims=True)
    over = jnp.logical_or(most > cap, fullest + tile_dev * (GROUP - 1) > kept)
    seg_ref[16:24, :] = jnp.broadcast_to(jnp.where(over, 1.0, 0.0), (8, width))
    where_to = jnp.sum(jnp.where(tile_hot, prefix + start[:, 0:1], 0.0), axis=0, keepdims=True)
    where_to = jnp.where(tile1 > 0, where_to, -1.0).astype(jnp.int32)
    order = ones_where(iota((kept, slots), 0) == where_to)
    source = (iota((1, slots), 1) // cap).astype(f32)
    sub = iota((8, slots), 0)
    facts = jnp.where(sub == 0, jnp.where(tile1 > 0, 1.0, 0.0), jnp.where(sub == 3, source, facts))
    facts = facts.astype(bf16)
    id_lanes = dot_nt(facts, order)
    scratch_ref[...] = jnp.zeros_like(scratch_ref)
    for q in range(-(-kept // width)):
        many = min(width, kept - q * width)
        scratch_ref[q * 8 : q * 8 + 8, 0:many] = id_lanes[:, q * width : q * width + many]
    ids_ref[...] = dot_nt(order, facts)
    sorted_fields = []
    for f in range(6):
        field = jnp.concatenate([recv_ref[s, f * cap : (f + 1) * cap, :] for s in range(owners)], axis=0)
        sorted_fields.append(dot_nn(order, field))
    twice = 2.0 * (sorted_fields[4] + sorted_fields[5])
    for f in range(4):
        fields_ref[f] = sorted_fields[f]
    fields_ref[4] = jnp.cos(twice)
    fields_ref[5] = jnp.sin(twice)
    fields_ref[6] = (1.0 - sorted_fields[2]).astype(bf16).astype(f32)
    fields_ref[7] = (1.0 - sorted_fields[3]).astype(bf16).astype(f32)
    sig_ref[...] = jnp.zeros_like(sig_ref)
    ends = segments(seg_ref, tile_dev)

    def one_group(group):
        tile = tile_of(group, ends)
        rows = jnp.concatenate([tiles_ref[d, tile] for d in range(groups_det)], axis=0)
        base = group * GROUP
        cols = [weights_of(fields_ref, 1, base + k, (side, width)) for k in range(GROUP)]
        partial_rows = dot_nn(rows, jnp.concatenate(cols, axis=1))
        for k in range(GROUP):
            row_weight = weights_of(fields_ref, 0, base + k, (side, width)).astype(f32)
            values = []
            for p in range(3):
                total = None
                for d in range(groups_det):
                    at = d * rows_dev + p * part
                    term = partial_rows[at : at + part, k * width : (k + 1) * width]
                    term = term * row_weight[d * part : (d + 1) * part]
                    total = term if total is None else total + term
                values.append(jnp.sum(total, axis=0, keepdims=True))
            cos = fields_ref[4, pl.ds(base + k, 1), :]
            sin = fields_ref[5, pl.ds(base + k, 1), :]
            sig_ref[pl.ds(base + k, 1), :] = values[0] + cos * values[1] + sin * values[2]

    def step(g, carry):
        for u in range(UNROLL):
            one_group(g * UNROLL + u)
        return carry

    lax.fori_loop(0, (ends[-1] + UNROLL - 1) // UNROLL, step, 0)
    sent = sig_ref[...].astype(bf16)
    notes = scratch_ref[...].astype(bf16)

    def copy(o, carry):
        out_ref[o, 0:kept, :] = sent
        out_ref[o, kept:, :] = notes
        return carry

    lax.fori_loop(0, owners, copy, 0)


def toeplitz_kernel(line_ref, out_ref):
    lines, rows, width = out_ref.shape
    width = width // 2
    blocks = rows // width

    def one(d, carry):
        for m in range(blocks):
            at = (blocks - 1 - m) * width
            piece = jnp.broadcast_to(line_ref[d, :, at : at + 2 * width], (width, 2 * width))
            block = pltpu.roll(piece, width, 1, stride=1, stride_axis=0)[:, :width]
            high = block.astype(bf16)
            out_ref[d, m * width : (m + 1) * width, :width] = high
            out_ref[d, m * width : (m + 1) * width, width:] = (block - high.astype(f32)).astype(bf16)
        return carry

    lax.fori_loop(0, lines, one, 0)


def filter_lines(blocks_dev, kept, recv_ref, mat_ref, filt_ref, line_ref):
    owners, rows, width = recv_ref.shape
    lines, padded, _ = line_ref.shape
    count = owners * blocks_dev
    edge = (padded - count) // 2
    spans = padded - count + 1
    together = math.gcd(owners, 8)
    line_ref[...] = jnp.zeros_like(line_ref)

    def some(first, lines_now, line0):
        at, values = [], []
        for o in range(together):
            notes = recv_ref[first + o, kept:, :].astype(f32)
            notes = [notes[q * 8 : q * 8 + 8] for q in range(notes.shape[0] // 8)]
            notes = jnp.concatenate(notes, axis=1)[:, :kept]
            row = notes[2:3] * count + notes[3:4] * blocks_dev + notes[1:2]
            at.append(jnp.where(notes[0:1] > 0.5, row, -1.0))
            values.append(recv_ref[first + o, 0:kept, :])
        at = jnp.concatenate(at, axis=1).astype(jnp.int32) - line0 * count
        place = ones_where(iota((lines_now * count, together * kept), 0) == at)
        return dot_nn(place, jnp.concatenate(values, axis=0))

    if together == owners:
        found = some(0, lines, 0)
        for d in range(lines):
            line_ref[d, edge : edge + count, :] = found[d * count : (d + 1) * count]
    else:

        def one(g, carry):
            for d in range(lines):
                line_ref[d, edge : edge + count, :] += some(g * together, 1, d)
            return carry

        lax.fori_loop(0, owners // together, one, 0)
    for d in range(lines):
        spread = jnp.concatenate([line_ref[d, m : m + count, :].astype(bf16) for m in range(spans)], axis=1)
        both = dot_nn(spread, mat_ref[d])
        filt_ref[d] = both[:, :width] + both[:, width:]


def back_kernel(
    blocks_dev,
    core_ref,
    recv_ref,
    mat_ref,
    fields_ref,
    ids_ref,
    seg_ref,
    mine_ref,
    theirs_ref,
    filt_ref,
    line_ref,
    scaled_ref,
    acc_ref,
):
    width = fields_ref.shape[2]
    kept = fields_ref.shape[1]
    filter_lines(blocks_dev, kept, recv_ref, mat_ref, filt_ref, line_ref)
    pairs, tile_dev, rows_dev, side = mine_ref.shape
    part = rows_dev // 3
    core = core_ref[0]
    poison = jnp.where(seg_ref[16:17, :] > 0.5, jnp.nan, 0.0)
    lines, count, _ = filt_ref.shape
    ids = ids_ref[...]
    at = ids[:, 2:3] * count + ids[:, 3:4] * blocks_dev + ids[:, 1:2]
    at = jnp.where(ids[:, 0:1] > 0.5, at, -1.0).astype(jnp.int32)
    filtered = jnp.zeros((kept, 2 * width), f32)
    for d in range(lines):
        line = filt_ref[d]
        high = line.astype(bf16)
        pair = jnp.concatenate([high, (line - high.astype(f32)).astype(bf16)], axis=1)
        filtered += dot_nn(ones_where(iota((kept, count), 1) + d * count == at), pair)
    filtered = filtered[:, :width] + filtered[:, width:]
    scaled_ref[0] = filtered
    scaled_ref[1] = filtered * fields_ref[4]
    scaled_ref[2] = filtered * fields_ref[5]
    ends = segments(seg_ref, tile_dev)
    acc_ref[...] = jnp.zeros_like(acc_ref)

    def one_group(group):
        base = group * GROUP
        cols, terms = [], []
        for k in range(GROUP):
            cols.append(weights_of(fields_ref, 1, base + k, (side, width)))
            row_weight = weights_of(fields_ref, 0, base + k, (side, width)).astype(f32)
            scaled = [scaled_ref[p, pl.ds(base + k, 1), :] for p in range(3)]
            terms.append(jnp.concatenate([(x * row_weight).astype(bf16) for x in scaled], axis=0))
        return dot_nt(jnp.concatenate(terms, axis=1), jnp.concatenate(cols, axis=1))

    def step(g, carry):
        for u in range(UNROLL):
            acc_ref[tile_of(g * UNROLL + u, ends)] += one_group(g * UNROLL + u)
        return carry

    lax.fori_loop(0, (ends[-1] + UNROLL - 1) // UNROLL, step, 0)
    for tile in range(tile_dev):
        for h in range(pairs):
            for p in range(3):
                base = p * side + h * 2 * part
                mine = acc_ref[tile, pl.ds(pl.multiple_of(base + core * part, part), part), :]
                theirs = acc_ref[tile, pl.ds(pl.multiple_of(base + (1 - core) * part, part), part), :]
                mine_ref[h, tile, p * part : (p + 1) * part, :] = mine + poison
                theirs_ref[h, tile, p * part : (p + 1) * part, :] = (theirs + poison).astype(bf16)


def call(kernel, out, scratch=(), **more):
    return pl.pallas_call(
        kernel,
        out_shape=out,
        scratch_shapes=list(scratch),
        compiler_params=pltpu.CompilerParams(vmem_limit_bytes=VMEM_LIMIT),
        **more,
    )


def whole_tiles(
    tiles, position, run_slot, hit_row, hit_col, frac_row, frac_col, angle, noise_coef
):
    owner_total = lax.axis_size("tm")
    groups_det, tile_dev, rows_dev, side_len = tiles.shape
    part = rows_dev // 3
    owned_tiles = tiles.reshape(groups_det, tile_dev, 3, part, side_len)
    owned_tiles = owned_tiles.transpose(1, 2, 0, 3, 4).reshape(tile_dev, 3, side_len, side_len)
    listed_total = position.shape[0]
    per_owner = max(1, listed_total // owner_total)
    slot_total = owner_total * per_owner
    owner_of = position // tile_dev
    local_slot = position % tile_dev
    listing = jnp.arange(listed_total, dtype=jnp.int32)
    earlier_same = (owner_of[:, None] == owner_of[None, :]) & (listing[:, None] > listing[None, :])
    rank_within = jnp.sum(earlier_same.astype(jnp.int32), axis=1)
    outbox_row = owner_of * per_owner + rank_within
    slot_rows = jnp.arange(slot_total, dtype=jnp.int32)
    asked_slot = (
        jnp.sum(
            jnp.where(slot_rows[:, None] == outbox_row[None, :], local_slot[None, :] + 1, 0), axis=1
        )
        - 1
    )
    served_slot = lax.all_to_all(asked_slot, "tm", split_axis=0, concat_axis=0, tiled=True)
    every_tile = jnp.broadcast_to(owned_tiles[None], (owner_total,) + owned_tiles.shape)
    every_tile = lax.all_to_all(every_tile, "tm", split_axis=0, concat_axis=0)
    every_tile = every_tile.reshape((owner_total * tile_dev,) + owned_tiles.shape[1:])
    listed = jnp.take(every_tile, position, axis=0)
    det_local, time_local = hit_row.shape
    run_length = time_local // run_slot.shape[1]
    run_total = det_local * run_slot.shape[1]
    per_group = math.gcd(run_total, group_runs)
    group_total = run_total // per_group

    def grouped(values):
        return values.reshape(group_total, per_group, run_length)

    run_items = (
        run_slot.reshape(group_total, per_group),
        grouped(hit_row),
        grouped(hit_col),
        grouped(frac_row),
        grouped(frac_col),
        grouped(angle),
    )

    def project(items):
        slots, rows_at, cols_at, frac_rows, frac_cols, angles = items
        tiles = jnp.take(listed, slots, axis=0)
        row_weight = run_weights(rows_at, frac_rows, side_len).astype(jnp.float32)
        col_weight = run_weights(cols_at, frac_cols, side_len)
        partial_rows = jnp.einsum(
            "bpij,bsj->bpsi", tiles, col_weight, preferred_element_type=jnp.float32
        )
        values = jnp.sum(partial_rows * row_weight[:, None], axis=3)
        return jnp.sum(values * responses(angles), axis=1)

    signal = lax.map(project, run_items).reshape(det_local, time_local)
    filtered = banded(signal, noise_coef)

    def back_project(carry, items):
        slots, rows_at, cols_at, frac_rows, frac_cols, angles, filt_runs = items
        row_weight = run_weights(rows_at, frac_rows, side_len).astype(jnp.float32)
        col_weight = run_weights(cols_at, frac_cols, side_len)
        scaled = responses(angles) * filt_runs[:, None]
        weighted = (scaled[..., None] * row_weight[:, None]).astype(jnp.bfloat16)
        tile_terms = jnp.einsum(
            "bpsi,bsj->bpij", weighted, col_weight, preferred_element_type=jnp.float32
        )
        return (carry.at[slots].add(tile_terms), None)

    initial = jnp.zeros((listed_total, 3, side_len, side_len), jnp.float32)
    contrib, _ = lax.scan(back_project, initial, run_items + (grouped(filtered),))
    outbox = jnp.zeros((slot_total, 3, side_len, side_len), jnp.float32).at[outbox_row].set(contrib)
    arrived = lax.all_to_all(outbox, "tm", split_axis=0, concat_axis=0, tiled=True)
    summed = jnp.stack(
        [
            jnp.sum(jnp.where((served_slot == slot_id)[:, None, None, None], arrived, 0.0), axis=0)
            for slot_id in range(tile_dev)
        ]
    )
    summed = summed.reshape(tile_dev, 3, groups_det, part, side_len)
    shares = lax.all_to_all(summed, "det", split_axis=2, concat_axis=0)
    return jnp.sum(shares.reshape(groups_det, tile_dev, 3, part, side_len), axis=0)


def body(
    sky_map,
    tile_home,
    piece_tiles,
    run_slot,
    hit_row,
    hit_col,
    frac_row,
    frac_col,
    angle,
    noise_coef,
):
    owners = lax.axis_size("tm")
    groups_det = lax.axis_size("det")
    tile_dev, _, part, side = sky_map.shape
    dets, blocks = run_slot.shape
    runs = dets * blocks
    width = hit_row.shape[1] // blocks
    listed = piece_tiles.shape[2]
    half_band = noise_coef.shape[1] - 1
    cap = round_up(2 * runs // min(owners, listed), META)
    kept = round_up(runs + runs // 2, META)
    slots = owners * cap
    piece_list = piece_tiles.reshape(listed)
    smem = pl.BlockSpec(memory_space=pltpu.SMEM)
    vmem = pl.BlockSpec(memory_space=pltpu.VMEM)

    packed = call(
        functools.partial(pack_kernel, owners, cap, tile_dev),
        jax.ShapeDtypeStruct((owners, 6 * cap + META, width), bf16),
        [pltpu.VMEM((owners, META, width), f32)],
        in_specs=[smem, smem] + [vmem] * 6,
        out_specs=vmem,
    )(piece_list, tile_home, run_slot, hit_row, hit_col, frac_row, frac_col, angle)
    recv = lax.all_to_all(packed, "tm", split_axis=0, concat_axis=0, tiled=True)
    tiles = lax.all_gather(sky_map.reshape(tile_dev, 3 * part, side), "det", axis=0)

    weights = jnp.concatenate([noise_coef[:, :1] + 1.0, noise_coef[:, 1:]], axis=1)
    line = jnp.concatenate(
        [
            jnp.zeros((dets, width), f32),
            weights[:, ::-1],
            weights[:, 1:],
            jnp.zeros((dets, width - 1), f32),
        ],
        axis=1,
    )
    spans = 2 * (half_band // width) + 1
    matrix = call(
        toeplitz_kernel,
        pltpu.VMEM((dets, spans * width, 2 * width), bf16),
    )(line[:, None, :])

    notes = round_up(kept, width) // width * 8
    sent, fields, ids, seg = call(
        functools.partial(project_kernel, cap, kept),
        (
            jax.ShapeDtypeStruct((owners, kept + notes, width), bf16),
            jax.ShapeDtypeStruct((8, kept, width), f32),
            jax.ShapeDtypeStruct((kept, 8), f32),
            jax.ShapeDtypeStruct((24, width), f32),
        ),
        [pltpu.VMEM((notes, width), f32), pltpu.VMEM((kept, width), f32), pltpu.VMEM((8, slots), f32)],
    )(recv, tiles)
    heard = lax.all_to_all(sent, "tm", split_axis=0, concat_axis=0, tiled=True)

    count = owners * blocks
    place = lax.axis_index("det")
    core = lax.rem(place, 2)
    half = lax.div(place, 2)
    pairs = groups_det // 2
    mine, theirs = call(
        functools.partial(back_kernel, blocks),
        (
            jax.ShapeDtypeStruct((pairs, tile_dev, 3 * part, side), f32),
            jax.ShapeDtypeStruct((pairs, tile_dev, 3 * part, side), bf16),
        ),
        [
            pltpu.VMEM((dets, count, width), f32),
            pltpu.VMEM((dets, count + spans - 1, width), f32),
            pltpu.VMEM((3, kept, width), f32),
            pltpu.VMEM((tile_dev, 3 * side, side), f32),
        ],
        in_specs=[smem] + [vmem] * 5,
        out_specs=(vmem, vmem),
    )(core[None].astype(jnp.int32), heard, matrix, fields, ids, seg)

    beside = lax.ppermute(theirs, "det", [(i, i ^ 1) for i in range(groups_det)])

    def of_pair(h):
        pick = lambda values: lax.dynamic_index_in_dim(values, h, 0, keepdims=False).astype(f32)
        return pick(mine) + pick(beside)

    total = of_pair(half)
    for step in range(1, pairs):
        ring = [(i, (i + 2 * step) % groups_det) for i in range(groups_det)]
        total = total + lax.ppermute(
            of_pair(lax.rem(half + step, pairs)).astype(bf16), "det", ring
        ).astype(f32)
    total = total.reshape(tile_dev, 3, part, side)

    def travelling(_):
        position = positions_of(piece_list, tile_home)
        return whole_tiles(
            tiles, position, run_slot, hit_row, hit_col, frac_row, frac_col, angle, noise_coef
        )

    fits = jnp.logical_not(jnp.isnan(total[0, 0, 0, 0]))
    return lax.cond(fits, lambda t: t, travelling, total)


def solution(mesh):
    placed = (
        P("tm", None, "det", None),
        P(),
        P("det", "tm", None),
        P("det", "tm"),
        P("det", "tm"),
        P("det", "tm"),
        P("det", "tm"),
        P("det", "tm"),
        P("det", "tm"),
        P("det", None),
    )
    return jax.shard_map(
        body, mesh=mesh, in_specs=placed, out_specs=P("tm", None, "det", None), check_vma=False
    )
```

```python
import functools
import math

import jax
import jax.numpy as jnp
from jax import lax
from jax.experimental import pallas as pl
from jax.experimental.pallas import tpu as pltpu
from jax.sharding import PartitionSpec as P

LISTED = 32


block_cols = 128
group_runs = 32


def extended_2(cells, sides, width):
    for axis, dim in sides:
        count = lax.axis_size(axis)
        ends = count - 1
        head = lax.slice_in_dim(cells, 0, width, axis=dim)
        tail = lax.slice_in_dim(cells, cells.shape[dim] - width, cells.shape[dim], axis=dim)
        cells = jnp.concatenate(
            [
                lax.ppermute(tail, axis, [(i, (i + 1) % count) for i in range(ends)]),
                cells,
                lax.ppermute(head, axis, [((i + 1) % count, i) for i in range(ends)]),
            ],
            axis=dim,
        )
    return cells


def positions_of(piece_list, tile_home):
    table_rows = jnp.arange(tile_home.shape[0], dtype=jnp.int32)
    matched = piece_list[:, None] == table_rows[None, :]
    return jnp.sum(jnp.where(matched, tile_home[None, :], 0), axis=1)


def run_weights(pixel_index, upper_frac, side_len):
    lower_weight = (1.0 - upper_frac.astype(jnp.float32)).astype(jnp.bfloat16)
    pixels = lax.broadcasted_iota(jnp.int32, pixel_index.shape + (side_len,), pixel_index.ndim)
    zero_value = jnp.zeros((), jnp.bfloat16)
    low_part = jnp.where(pixels == pixel_index[..., None], lower_weight[..., None], zero_value)
    high_part = jnp.where(pixels == pixel_index[..., None] + 1, upper_frac[..., None], zero_value)
    return low_part + high_part


def responses(angles):
    twice = 2.0 * angles
    return jnp.stack([jnp.ones_like(twice), jnp.cos(twice), jnp.sin(twice)], axis=1)


def banded(signal, noise_coef):
    det_count = signal.shape[0]
    half_band = noise_coef.shape[1] - 1
    reach_blocks = half_band // block_cols
    span_cols = (2 * reach_blocks + 1) * block_cols
    weights = jnp.concatenate([noise_coef[:, :1] + 1.0, noise_coef[:, 1:]], axis=1)
    zero_pad = jnp.zeros((det_count, block_cols - 1), jnp.float32)
    kernel_row = jnp.concatenate(
        [
            zero_pad,
            weights[:, ::-1],
            weights[:, 1:],
            zero_pad,
            jnp.zeros((det_count, 1), jnp.float32),
        ],
        axis=1,
    )
    period = span_cols + block_cols
    tiled_rows = jnp.tile(kernel_row, (1, block_cols))[:, : block_cols * (period - 1)]
    tiled_rows = tiled_rows.reshape(det_count, block_cols, period - 1)
    matrix = tiled_rows[:, :, block_cols - 1 : block_cols - 1 + span_cols]
    matrix = matrix.reshape(det_count, block_cols, 2 * reach_blocks + 1, block_cols)
    extended = extended_2(signal, (("tm", 1),), half_band)
    block_count = signal.shape[1] // block_cols
    blocks = extended.reshape(det_count, block_count + 2 * reach_blocks, block_cols)
    stacked = jnp.stack(
        [blocks[:, offset : offset + block_count] for offset in range(2 * reach_blocks + 1)], axis=1
    )
    result = jnp.einsum(
        "diml,dmnl->dni",
        matrix,
        stacked,
        precision=lax.Precision.HIGHEST,
        preferred_element_type=jnp.float32,
    )
    return result.reshape(det_count, block_count * block_cols)


GROUP = 4
UNROLL = 4
META = 16
VMEM_LIMIT = 24 * 1024 * 1024
f32 = jnp.float32
bf16 = jnp.bfloat16


def round_up(value, step):
    return -(-value // step) * step


def iota(shape, dim):
    return lax.broadcasted_iota(jnp.int32, shape, dim)


def dot_nn(a, b):
    return lax.dot_general(a, b, (((1,), (0,)), ((), ())), preferred_element_type=f32)


def dot_nt(a, b):
    return lax.dot_general(a, b, (((1,), (1,)), ((), ())), preferred_element_type=f32)


def ones_where(mask):
    return jnp.where(mask, 1.0, 0.0).astype(bf16)


def pack_kernel(
    owners,
    cap,
    tile_dev,
    pt_ref,
    th_ref,
    slot_ref,
    r_ref,
    c_ref,
    fr_ref,
    fc_ref,
    ang_ref,
    out_ref,
    counts_ref,
    meta_ref,
):
    dets, blocks = slot_ref.shape
    runs = dets * blocks
    width = r_ref.shape[1] // blocks
    listed = pt_ref.shape[0]
    spread = dot_nn(
        slot_ref[...].astype(f32).astype(bf16),
        ones_where(iota((blocks, runs), 1) // dets == iota((blocks, runs), 0)),
    )
    run_id = iota((dets, runs), 1)
    own_det = run_id % dets == iota((dets, runs), 0)
    slot_row = jnp.sum(jnp.where(own_det, spread, 0.0), axis=0, keepdims=True)
    slot_row = slot_row.astype(jnp.int32)
    owner_row = jnp.zeros((1, runs), jnp.int32)
    tile_row = jnp.zeros((1, runs), jnp.int32)
    for k in range(listed):
        pos = th_ref[pt_ref[k]]
        own = lax.div(pos, jnp.int32(tile_dev))
        owner_row = jnp.where(slot_row == k, own, owner_row)
        tile_row = jnp.where(slot_row == k, pos - own * tile_dev, tile_row)
    owner_hot = iota((owners, runs), 0) == owner_row
    owner_one = ones_where(owner_hot)
    before = ones_where(iota((runs, runs), 0) < iota((runs, runs), 1))
    prefix = dot_nn(owner_one, before)
    rank = jnp.sum(jnp.where(owner_hot, prefix, 0.0), axis=0, keepdims=True).astype(jnp.int32)
    counts = dot_nt(jnp.ones((8, runs), bf16), owner_one)
    dest = jnp.where(rank < cap, owner_row * cap + rank, -1)
    place = ones_where(iota((owners * cap, runs), 0) == dest)

    def by_run(ref):
        return jnp.concatenate(
            [ref[:, b * width : (b + 1) * width].astype(f32) for b in range(blocks)], axis=0
        )

    angle = by_run(ang_ref)
    angle_high = angle.astype(bf16)
    angle_low = (angle - angle_high.astype(f32)).astype(bf16)
    fields = [by_run(ref).astype(bf16) for ref in (r_ref, c_ref, fr_ref, fc_ref)]
    fields += [angle_high, angle_low]
    for f, field in enumerate(fields):
        sent = dot_nn(place, field).astype(bf16)
        for o in range(owners):
            out_ref[o, f * cap : (f + 1) * cap, :] = sent[o * cap : (o + 1) * cap]
    sub = iota((8, runs), 0)
    lane_run = iota((8, runs), 1)
    facts = jnp.where(sub == 0, tile_row + 1, jnp.where(sub == 1, lane_run // dets, lane_run % dets))
    facts = dot_nt(facts.astype(f32).astype(bf16), place)
    meta_ref[...] = jnp.zeros_like(meta_ref)
    for o in range(owners):
        meta_ref[o, 0:8, 0:cap] = facts[:, o * cap : (o + 1) * cap]
        meta_ref[o, 8:16, 0:owners] = counts
    out_ref[:, len(fields) * cap :, :] = meta_ref[...].astype(bf16)
    meta_ref[0] = jnp.zeros(meta_ref.shape[1:], f32)
    meta_ref[0, 0:8, 0:owners] = counts
    counts_ref[...] = meta_ref[0].astype(bf16)


def weights_of(fields_ref, axis, run, shape):
    index, high, low = (
        fields_ref[f + axis, pl.ds(run, 1), :].astype(bf16) for f in (0, 2, 6)
    )
    rows = iota(shape, 0).astype(f32).astype(bf16)
    zero = jnp.zeros((), bf16)
    return jnp.where(rows == index, low, jnp.where(rows == index + 1, high, zero))


def segments(seg_ref, tile_dev):
    return [
        jnp.max(seg_ref[8 + tile : 9 + tile, :]).astype(jnp.int32) // GROUP for tile in range(tile_dev)
    ]


def tile_of(group, ends):
    tile = jnp.int32(0)
    for end in ends[:-1]:
        tile = tile + (group >= end).astype(jnp.int32)
    return tile


def project_kernel(
    cap, kept, tile_dev, recv_ref, tiles_ref, out_ref, fields_ref, ids_ref, seg_ref, scratch_ref, sig_ref, lanes_ref
):
    owners = recv_ref.shape[0]
    slots = owners * cap
    width = recv_ref.shape[2]
    groups_det, tile_rows, side = tiles_ref.shape
    tile_rows = tile_rows - META
    rows_dev = tile_rows // tile_dev
    part = rows_dev // 3
    for s in range(owners):
        lanes_ref[:, s * cap : (s + 1) * cap] = recv_ref[s, 6 * cap : 6 * cap + META, :].astype(f32)[0:8, 0:cap]
    facts = lanes_ref[...]
    tile1 = facts[0:1].astype(jnp.int32)
    tile_hot = iota((8, slots), 0) + 1 == tile1
    tile_one = ones_where(tile_hot)
    before = ones_where(iota((slots, slots), 0) < iota((slots, slots), 1))
    prefix = dot_nn(tile_one, before)
    count = jnp.sum(jnp.where(tile_hot, 1.0, 0.0), axis=1, keepdims=True)
    padded = jnp.floor((count + (GROUP - 1)) * (1.0 / GROUP)) * GROUP
    padded = jnp.broadcast_to(padded, (8, width))
    start = jnp.zeros((8, width), f32)
    for tile in range(tile_dev - 1):
        start += jnp.where(iota((8, width), 0) > tile, padded[tile : tile + 1], 0.0)
    stop = jnp.minimum(start + padded, float(kept))
    seg_ref[0:8, :] = start
    seg_ref[8:16, :] = stop
    where_to = jnp.sum(jnp.where(tile_hot, prefix + start[:, 0:1], 0.0), axis=0, keepdims=True)
    where_to = jnp.where(tile1 > 0, where_to, -1.0).astype(jnp.int32)
    order = ones_where(iota((kept, slots), 0) == where_to)
    source = (iota((1, slots), 1) // cap).astype(f32)
    sub = iota((8, slots), 0)
    facts = jnp.where(sub == 0, jnp.where(tile1 > 0, 1.0, 0.0), jnp.where(sub == 3, source, facts))
    facts = facts.astype(bf16)
    id_lanes = dot_nt(facts, order)
    scratch_ref[...] = jnp.zeros_like(scratch_ref)
    for q in range(-(-kept // width)):
        many = min(width, kept - q * width)
        scratch_ref[q * 8 : q * 8 + 8, 0:many] = id_lanes[:, q * width : q * width + many]
    for d in range(groups_det):
        scratch_ref[4 + d : 5 + d, :] = tiles_ref[d, tile_rows:, :].astype(f32)[0:1]
    ids_ref[...] = dot_nt(order, facts)
    sorted_fields = []
    for f in range(6):
        field = jnp.concatenate([recv_ref[s, f * cap : (f + 1) * cap, :] for s in range(owners)], axis=0)
        sorted_fields.append(dot_nn(order, field))
    twice = 2.0 * (sorted_fields[4] + sorted_fields[5])
    for f in range(4):
        fields_ref[f] = sorted_fields[f]
    fields_ref[4] = jnp.cos(twice)
    fields_ref[5] = jnp.sin(twice)
    fields_ref[6] = (1.0 - sorted_fields[2]).astype(bf16).astype(f32)
    fields_ref[7] = (1.0 - sorted_fields[3]).astype(bf16).astype(f32)
    sig_ref[...] = jnp.zeros_like(sig_ref)
    ends = segments(seg_ref, tile_dev)

    def one_group(group):
        tile = tile_of(group, ends)
        at_tile = pl.ds(pl.multiple_of(tile * rows_dev, rows_dev), rows_dev)
        rows = jnp.concatenate([tiles_ref[d, at_tile, :] for d in range(groups_det)], axis=0)
        base = group * GROUP
        cols = [weights_of(fields_ref, 1, base + k, (side, width)) for k in range(GROUP)]
        partial_rows = dot_nn(rows, jnp.concatenate(cols, axis=1))
        for k in range(GROUP):
            row_weight = weights_of(fields_ref, 0, base + k, (side, width)).astype(f32)
            values = []
            for p in range(3):
                total = None
                for d in range(groups_det):
                    at = d * rows_dev + p * part
                    term = partial_rows[at : at + part, k * width : (k + 1) * width]
                    term = term * row_weight[d * part : (d + 1) * part]
                    total = term if total is None else total + term
                values.append(jnp.sum(total, axis=0, keepdims=True))
            cos = fields_ref[4, pl.ds(base + k, 1), :]
            sin = fields_ref[5, pl.ds(base + k, 1), :]
            sig_ref[pl.ds(base + k, 1), :] = values[0] + cos * values[1] + sin * values[2]

    def step(g, carry):
        for u in range(UNROLL):
            one_group(g * UNROLL + u)
        return carry

    lax.fori_loop(0, (ends[-1] + UNROLL - 1) // UNROLL, step, 0)
    sent = sig_ref[...].astype(bf16)
    notes = scratch_ref[...].astype(bf16)

    def copy(o, carry):
        out_ref[o, 0:kept, :] = sent
        out_ref[o, kept:, :] = notes
        return carry

    lax.fori_loop(0, owners, copy, 0)


def toeplitz_kernel(line_ref, out_ref):
    lines, rows, width = out_ref.shape
    blocks = rows // width

    def one(d, carry):
        for m in range(blocks):
            at = (blocks - 1 - m) * width
            piece = jnp.broadcast_to(line_ref[d, :, at : at + 2 * width], (width, 2 * width))
            block = pltpu.roll(piece, width, 1, stride=1, stride_axis=0)[:, :width]
            out_ref[d, m * width : (m + 1) * width, :] = block.astype(bf16)
        return carry

    lax.fori_loop(0, lines, one, 0)


def filter_lines(blocks_dev, kept, recv_ref, mat_ref, coef_ref, filt_ref, line_ref):
    owners, rows, width = recv_ref.shape
    lines, padded, _ = line_ref.shape
    count = owners * blocks_dev
    edge = (padded - count) // 2
    spans = padded - count + 1
    together = math.gcd(owners, 8)
    line_ref[...] = jnp.zeros_like(line_ref)

    def some(first, lines_now, line0):
        at, values = [], []
        for o in range(together):
            notes = recv_ref[first + o, kept:, :].astype(f32)
            notes = [notes[q * 8 : q * 8 + 8] for q in range(notes.shape[0] // 8)]
            notes = jnp.concatenate(notes, axis=1)[:, :kept]
            row = notes[2:3] * count + notes[3:4] * blocks_dev + notes[1:2]
            at.append(jnp.where(notes[0:1] > 0.5, row, -1.0))
            values.append(recv_ref[first + o, 0:kept, :])
        at = jnp.concatenate(at, axis=1).astype(jnp.int32) - line0 * count
        place = ones_where(iota((lines_now * count, together * kept), 0) == at)
        return dot_nn(place, jnp.concatenate(values, axis=0))

    if together == owners:
        found = some(0, lines, 0)
        for d in range(lines):
            line_ref[d, edge : edge + count, :] = found[d * count : (d + 1) * count]
    else:

        def one(g, carry):
            for d in range(lines):
                line_ref[d, edge : edge + count, :] += some(g * together, 1, d)
            return carry

        lax.fori_loop(0, owners // together, one, 0)
    for d in range(lines):
        spread = jnp.concatenate([line_ref[d, m : m + count, :].astype(bf16) for m in range(spans)], axis=1)
        weight = coef_ref[d : d + 1, 0:1] + 1.0
        rest = weight - weight.astype(bf16).astype(f32)
        filt_ref[d] = dot_nn(spread, mat_ref[d]) + rest * line_ref[d, edge : edge + count, :]


def back_kernel(
    blocks_dev,
    cap,
    core_ref,
    recv_ref,
    mat_ref,
    coef_ref,
    fields_ref,
    ids_ref,
    seg_ref,
    mine_ref,
    theirs_ref,
    over_ref,
    filt_ref,
    line_ref,
    scaled_ref,
    acc_ref,
):
    width = fields_ref.shape[2]
    kept = fields_ref.shape[1]
    filter_lines(blocks_dev, kept, recv_ref, mat_ref, coef_ref, filt_ref, line_ref)
    pairs, tile_dev, rows_dev, side = mine_ref.shape
    part = rows_dev // 3
    core = core_ref[0]
    owners = recv_ref.shape[0]
    most = totals = jnp.zeros((4, width), f32)
    for s in range(owners):
        counts = recv_ref[s, kept : kept + META, :].astype(f32)[4:8]
        most, totals = jnp.maximum(most, counts), totals + counts
    most = jnp.max(most)
    fullest = jnp.max(totals) + tile_dev * (GROUP - 1)
    over_ref[0] = jnp.logical_or(most > cap, fullest > kept).astype(jnp.int32)
    lines, count, _ = filt_ref.shape
    ids = ids_ref[...]
    at = ids[:, 2:3] * count + ids[:, 3:4] * blocks_dev + ids[:, 1:2]
    at = jnp.where(ids[:, 0:1] > 0.5, at, -1.0).astype(jnp.int32)
    filtered = jnp.zeros((kept, 2 * width), f32)
    for d in range(lines):
        line = filt_ref[d]
        high = line.astype(bf16)
        pair = jnp.concatenate([high, (line - high.astype(f32)).astype(bf16)], axis=1)
        filtered += dot_nn(ones_where(iota((kept, count), 1) + d * count == at), pair)
    filtered = filtered[:, :width] + filtered[:, width:]
    scaled_ref[0] = filtered
    scaled_ref[1] = filtered * fields_ref[4]
    scaled_ref[2] = filtered * fields_ref[5]
    ends = segments(seg_ref, tile_dev)
    acc_ref[...] = jnp.zeros_like(acc_ref)

    def one_group(group):
        base = group * GROUP
        cols, terms = [], []
        for k in range(GROUP):
            cols.append(weights_of(fields_ref, 1, base + k, (side, width)))
            row_weight = weights_of(fields_ref, 0, base + k, (side, width)).astype(f32)
            scaled = [scaled_ref[p, pl.ds(base + k, 1), :] for p in range(3)]
            terms.append(jnp.concatenate([(x * row_weight).astype(bf16) for x in scaled], axis=0))
        return dot_nt(jnp.concatenate(terms, axis=1), jnp.concatenate(cols, axis=1))

    def step(g, carry):
        for u in range(UNROLL):
            acc_ref[tile_of(g * UNROLL + u, ends)] += one_group(g * UNROLL + u)
        return carry

    lax.fori_loop(0, (ends[-1] + UNROLL - 1) // UNROLL, step, 0)
    for tile in range(tile_dev):
        for h in range(pairs):
            for p in range(3):
                base = p * side + h * 2 * part
                mine = acc_ref[tile, pl.ds(pl.multiple_of(base + core * part, part), part), :]
                theirs = acc_ref[tile, pl.ds(pl.multiple_of(base + (1 - core) * part, part), part), :]
                mine_ref[h, tile, p * part : (p + 1) * part, :] = mine
                theirs_ref[h, tile, p * part : (p + 1) * part, :] = theirs.astype(bf16)


def call(kernel, out, scratch=(), **more):
    return pl.pallas_call(
        kernel,
        out_shape=out,
        scratch_shapes=list(scratch),
        compiler_params=pltpu.CompilerParams(vmem_limit_bytes=VMEM_LIMIT),
        **more,
    )


def whole_tiles(
    tiles, position, run_slot, hit_row, hit_col, frac_row, frac_col, angle, noise_coef
):
    owner_total = lax.axis_size("tm")
    groups_det, tile_dev, rows_dev, side_len = tiles.shape
    part = rows_dev // 3
    owned_tiles = tiles.reshape(groups_det, tile_dev, 3, part, side_len)
    owned_tiles = owned_tiles.transpose(1, 2, 0, 3, 4).reshape(tile_dev, 3, side_len, side_len)
    listed_total = position.shape[0]
    per_owner = max(1, listed_total // owner_total)
    slot_total = owner_total * per_owner
    owner_of = position // tile_dev
    local_slot = position % tile_dev
    listing = jnp.arange(listed_total, dtype=jnp.int32)
    earlier_same = (owner_of[:, None] == owner_of[None, :]) & (listing[:, None] > listing[None, :])
    rank_within = jnp.sum(earlier_same.astype(jnp.int32), axis=1)
    outbox_row = owner_of * per_owner + rank_within
    slot_rows = jnp.arange(slot_total, dtype=jnp.int32)
    asked_slot = (
        jnp.sum(
            jnp.where(slot_rows[:, None] == outbox_row[None, :], local_slot[None, :] + 1, 0), axis=1
        )
        - 1
    )
    served_slot = lax.all_to_all(asked_slot, "tm", split_axis=0, concat_axis=0, tiled=True)
    every_tile = jnp.broadcast_to(owned_tiles[None], (owner_total,) + owned_tiles.shape)
    every_tile = lax.all_to_all(every_tile, "tm", split_axis=0, concat_axis=0)
    every_tile = every_tile.reshape((owner_total * tile_dev,) + owned_tiles.shape[1:])
    listed = jnp.take(every_tile, position, axis=0)
    det_local, time_local = hit_row.shape
    run_length = time_local // run_slot.shape[1]
    run_total = det_local * run_slot.shape[1]
    per_group = math.gcd(run_total, group_runs)
    group_total = run_total // per_group

    def grouped(values):
        return values.reshape(group_total, per_group, run_length)

    run_items = (
        run_slot.reshape(group_total, per_group),
        grouped(hit_row),
        grouped(hit_col),
        grouped(frac_row),
        grouped(frac_col),
        grouped(angle),
    )

    def project(items):
        slots, rows_at, cols_at, frac_rows, frac_cols, angles = items
        tiles = jnp.take(listed, slots, axis=0)
        row_weight = run_weights(rows_at, frac_rows, side_len).astype(jnp.float32)
        col_weight = run_weights(cols_at, frac_cols, side_len)
        partial_rows = jnp.einsum(
            "bpij,bsj->bpsi", tiles, col_weight, preferred_element_type=jnp.float32
        )
        values = jnp.sum(partial_rows * row_weight[:, None], axis=3)
        return jnp.sum(values * responses(angles), axis=1)

    signal = lax.map(project, run_items).reshape(det_local, time_local)
    filtered = banded(signal, noise_coef)

    def back_project(carry, items):
        slots, rows_at, cols_at, frac_rows, frac_cols, angles, filt_runs = items
        row_weight = run_weights(rows_at, frac_rows, side_len).astype(jnp.float32)
        col_weight = run_weights(cols_at, frac_cols, side_len)
        scaled = responses(angles) * filt_runs[:, None]
        weighted = (scaled[..., None] * row_weight[:, None]).astype(jnp.bfloat16)
        tile_terms = jnp.einsum(
            "bpsi,bsj->bpij", weighted, col_weight, preferred_element_type=jnp.float32
        )
        return (carry.at[slots].add(tile_terms), None)

    initial = jnp.zeros((listed_total, 3, side_len, side_len), jnp.float32)
    contrib, _ = lax.scan(back_project, initial, run_items + (grouped(filtered),))
    outbox = jnp.zeros((slot_total, 3, side_len, side_len), jnp.float32).at[outbox_row].set(contrib)
    arrived = lax.all_to_all(outbox, "tm", split_axis=0, concat_axis=0, tiled=True)
    summed = jnp.stack(
        [
            jnp.sum(jnp.where((served_slot == slot_id)[:, None, None, None], arrived, 0.0), axis=0)
            for slot_id in range(tile_dev)
        ]
    )
    summed = summed.reshape(tile_dev, 3, groups_det, part, side_len)
    shares = lax.all_to_all(summed, "det", split_axis=2, concat_axis=0)
    return jnp.sum(shares.reshape(groups_det, tile_dev, 3, part, side_len), axis=0)


def body(
    sky_map,
    tile_home,
    piece_tiles,
    run_slot,
    hit_row,
    hit_col,
    frac_row,
    frac_col,
    angle,
    noise_coef,
):
    owners = lax.axis_size("tm")
    groups_det = lax.axis_size("det")
    tile_dev, _, part, side = sky_map.shape
    dets, blocks = run_slot.shape
    runs = dets * blocks
    width = hit_row.shape[1] // blocks
    listed = piece_tiles.shape[2]
    half_band = noise_coef.shape[1] - 1
    cap = round_up(2 * runs // min(owners, listed), META)
    kept = round_up(runs + runs // 2, META)
    slots = owners * cap
    piece_list = piece_tiles.reshape(listed)
    smem = pl.BlockSpec(memory_space=pltpu.SMEM)
    vmem = pl.BlockSpec(memory_space=pltpu.VMEM)

    packed, counts = call(
        functools.partial(pack_kernel, owners, cap, tile_dev),
        (
            jax.ShapeDtypeStruct((owners, 6 * cap + META, width), bf16),
            jax.ShapeDtypeStruct((META, width), bf16),
        ),
        [pltpu.VMEM((owners, META, width), f32)],
        in_specs=[smem, smem] + [vmem] * 6,
        out_specs=(vmem, vmem),
    )(
        piece_list,
        tile_home,
        run_slot,
        hit_row,
        hit_col,
        frac_row,
        frac_col,
        angle,
    )
    recv = lax.all_to_all(packed, "tm", split_axis=0, concat_axis=0, tiled=True)
    rows = jnp.concatenate([sky_map.reshape(tile_dev * 3 * part, side), counts], axis=0)
    tiles = lax.all_gather(rows, "det", axis=0)

    weights = jnp.concatenate([noise_coef[:, :1] + 1.0, noise_coef[:, 1:]], axis=1)
    line = jnp.concatenate(
        [
            jnp.zeros((dets, width), f32),
            weights[:, ::-1],
            weights[:, 1:],
            jnp.zeros((dets, width - 1), f32),
        ],
        axis=1,
    )
    spans = 2 * (half_band // width) + 1
    matrix = call(
        toeplitz_kernel,
        pltpu.VMEM((dets, spans * width, width), bf16),
    )(line[:, None, :])

    notes = round_up(kept, width) // width * 8
    sent, fields, ids, seg = call(
        functools.partial(project_kernel, cap, kept, tile_dev),
        (
            jax.ShapeDtypeStruct((owners, kept + notes, width), bf16),
            jax.ShapeDtypeStruct((8, kept, width), f32),
            jax.ShapeDtypeStruct((kept, 8), f32),
            jax.ShapeDtypeStruct((16, width), f32),
        ),
        [pltpu.VMEM((notes, width), f32), pltpu.VMEM((kept, width), f32), pltpu.VMEM((8, slots), f32)],
    )(recv, tiles)
    heard = lax.all_to_all(sent, "tm", split_axis=0, concat_axis=0, tiled=True)

    count = owners * blocks
    place = lax.axis_index("det")
    core = lax.rem(place, 2)
    half = lax.div(place, 2)
    pairs = groups_det // 2
    mine, theirs, over = call(
        functools.partial(back_kernel, blocks, cap),
        (
            jax.ShapeDtypeStruct((pairs, tile_dev, 3 * part, side), f32),
            jax.ShapeDtypeStruct((pairs, tile_dev, 3 * part, side), bf16),
            jax.ShapeDtypeStruct((1,), jnp.int32),
        ),
        [
            pltpu.VMEM((dets, count, width), f32),
            pltpu.VMEM((dets, count + spans - 1, width), f32),
            pltpu.VMEM((3, kept, width), f32),
            pltpu.VMEM((tile_dev, 3 * side, side), f32),
        ],
        in_specs=[smem] + [vmem] * 6,
        out_specs=(vmem, vmem, smem),
    )(core[None].astype(jnp.int32), heard, matrix, noise_coef, fields, ids, seg)

    beside = lax.ppermute(theirs, "det", [(i, i ^ 1) for i in range(groups_det)])

    def of_pair(h):
        pick = lambda values: lax.dynamic_index_in_dim(values, h, 0, keepdims=False).astype(f32)
        return pick(mine) + pick(beside)

    others = []
    for step in range(1, pairs):
        ring = [(i, (i + 2 * step) % groups_det) for i in range(groups_det)]
        sent_on = of_pair(lax.rem(half + step, pairs)).astype(bf16)
        others.append(lax.ppermute(sent_on, "det", ring))

    def summed(_):
        total = of_pair(half)
        for other in others:
            total = total + other.astype(f32)
        return total.reshape(tile_dev, 3, part, side)

    def travelling(_):
        position = positions_of(piece_list, tile_home)
        whole = tiles[:, : tile_dev * 3 * part].reshape(groups_det, tile_dev, 3 * part, side)
        return whole_tiles(
            whole, position, run_slot, hit_row, hit_col, frac_row, frac_col, angle, noise_coef
        )

    return lax.cond(over[0] == 0, summed, travelling, 0)


def solution(mesh):
    placed = (
        P("tm", None, "det", None),
        P(),
        P("det", "tm", None),
        P("det", "tm"),
        P("det", "tm"),
        P("det", "tm"),
        P("det", "tm"),
        P("det", "tm"),
        P("det", "tm"),
        P("det", None),
    )
    return jax.shard_map(
        body, mesh=mesh, in_specs=placed, out_specs=P("tm", None, "det", None), check_vma=False
    )
```

```python
import functools
import math

import jax
import jax.numpy as jnp
from jax import lax
from jax.experimental import pallas as pl
from jax.experimental.pallas import tpu as pltpu
from jax.sharding import PartitionSpec as P

LISTED = 32


block_cols = 128
group_runs = 32


def extended_2(cells, sides, width):
    for axis, dim in sides:
        count = lax.axis_size(axis)
        ends = count - 1
        head = lax.slice_in_dim(cells, 0, width, axis=dim)
        tail = lax.slice_in_dim(cells, cells.shape[dim] - width, cells.shape[dim], axis=dim)
        cells = jnp.concatenate(
            [
                lax.ppermute(tail, axis, [(i, (i + 1) % count) for i in range(ends)]),
                cells,
                lax.ppermute(head, axis, [((i + 1) % count, i) for i in range(ends)]),
            ],
            axis=dim,
        )
    return cells


def positions_of(piece_list, tile_home):
    table_rows = jnp.arange(tile_home.shape[0], dtype=jnp.int32)
    matched = piece_list[:, None] == table_rows[None, :]
    return jnp.sum(jnp.where(matched, tile_home[None, :], 0), axis=1)


def run_weights(pixel_index, upper_frac, side_len):
    lower_weight = (1.0 - upper_frac.astype(jnp.float32)).astype(jnp.bfloat16)
    pixels = lax.broadcasted_iota(jnp.int32, pixel_index.shape + (side_len,), pixel_index.ndim)
    zero_value = jnp.zeros((), jnp.bfloat16)
    low_part = jnp.where(pixels == pixel_index[..., None], lower_weight[..., None], zero_value)
    high_part = jnp.where(pixels == pixel_index[..., None] + 1, upper_frac[..., None], zero_value)
    return low_part + high_part


def responses(angles):
    twice = 2.0 * angles
    return jnp.stack([jnp.ones_like(twice), jnp.cos(twice), jnp.sin(twice)], axis=1)


def banded(signal, noise_coef):
    det_count = signal.shape[0]
    half_band = noise_coef.shape[1] - 1
    reach_blocks = half_band // block_cols
    span_cols = (2 * reach_blocks + 1) * block_cols
    weights = jnp.concatenate([noise_coef[:, :1] + 1.0, noise_coef[:, 1:]], axis=1)
    zero_pad = jnp.zeros((det_count, block_cols - 1), jnp.float32)
    kernel_row = jnp.concatenate(
        [
            zero_pad,
            weights[:, ::-1],
            weights[:, 1:],
            zero_pad,
            jnp.zeros((det_count, 1), jnp.float32),
        ],
        axis=1,
    )
    period = span_cols + block_cols
    tiled_rows = jnp.tile(kernel_row, (1, block_cols))[:, : block_cols * (period - 1)]
    tiled_rows = tiled_rows.reshape(det_count, block_cols, period - 1)
    matrix = tiled_rows[:, :, block_cols - 1 : block_cols - 1 + span_cols]
    matrix = matrix.reshape(det_count, block_cols, 2 * reach_blocks + 1, block_cols)
    extended = extended_2(signal, (("tm", 1),), half_band)
    block_count = signal.shape[1] // block_cols
    blocks = extended.reshape(det_count, block_count + 2 * reach_blocks, block_cols)
    stacked = jnp.stack(
        [blocks[:, offset : offset + block_count] for offset in range(2 * reach_blocks + 1)], axis=1
    )
    result = jnp.einsum(
        "diml,dmnl->dni",
        matrix,
        stacked,
        precision=lax.Precision.HIGHEST,
        preferred_element_type=jnp.float32,
    )
    return result.reshape(det_count, block_count * block_cols)


GROUP = 4
UNROLL = 6
META = 16
VMEM_LIMIT = 24 * 1024 * 1024
f32 = jnp.float32
bf16 = jnp.bfloat16


def round_up(value, step):
    return -(-value // step) * step


def iota(shape, dim):
    return lax.broadcasted_iota(jnp.int32, shape, dim)


def dot_nn(a, b):
    return lax.dot_general(a, b, (((1,), (0,)), ((), ())), preferred_element_type=f32)


def dot_nt(a, b):
    return lax.dot_general(a, b, (((1,), (1,)), ((), ())), preferred_element_type=f32)


def ones_where(mask):
    return jnp.where(mask, 1.0, 0.0).astype(bf16)


def pack_kernel(
    owners,
    cap,
    tile_dev,
    pt_ref,
    th_ref,
    slot_ref,
    r_ref,
    c_ref,
    fr_ref,
    fc_ref,
    ang_ref,
    out_ref,
    counts_ref,
    meta_ref,
):
    dets, blocks = slot_ref.shape
    runs = dets * blocks
    width = r_ref.shape[1] // blocks
    listed = pt_ref.shape[0]
    spread = dot_nn(
        slot_ref[...].astype(f32).astype(bf16),
        ones_where(iota((blocks, runs), 1) // dets == iota((blocks, runs), 0)),
    )
    run_id = iota((dets, runs), 1)
    own_det = run_id % dets == iota((dets, runs), 0)
    slot_row = jnp.sum(jnp.where(own_det, spread, 0.0), axis=0, keepdims=True)
    slot_row = slot_row.astype(jnp.int32)
    owner_row = jnp.zeros((1, runs), jnp.int32)
    tile_row = jnp.zeros((1, runs), jnp.int32)
    for k in range(listed):
        pos = th_ref[pt_ref[k]]
        own = lax.div(pos, jnp.int32(tile_dev))
        owner_row = jnp.where(slot_row == k, own, owner_row)
        tile_row = jnp.where(slot_row == k, pos - own * tile_dev, tile_row)
    owner_hot = iota((owners, runs), 0) == owner_row
    owner_one = ones_where(owner_hot)
    before = ones_where(iota((runs, runs), 0) < iota((runs, runs), 1))
    prefix = dot_nn(owner_one, before)
    rank = jnp.sum(jnp.where(owner_hot, prefix, 0.0), axis=0, keepdims=True).astype(jnp.int32)
    counts = dot_nt(jnp.ones((8, runs), bf16), owner_one)
    dest = jnp.where(rank < cap, owner_row * cap + rank, -1)
    place = ones_where(iota((owners * cap, runs), 0) == dest)

    def by_run(ref):
        return jnp.concatenate(
            [ref[:, b * width : (b + 1) * width].astype(f32) for b in range(blocks)], axis=0
        )

    angle = by_run(ang_ref)
    angle_high = angle.astype(bf16)
    angle_low = (angle - angle_high.astype(f32)).astype(bf16)
    fields = [by_run(ref).astype(bf16) for ref in (r_ref, c_ref, fr_ref, fc_ref)]
    fields += [angle_high, angle_low]
    for f, field in enumerate(fields):
        sent = dot_nn(place, field).astype(bf16)
        for o in range(owners):
            out_ref[o, f * cap : (f + 1) * cap, :] = sent[o * cap : (o + 1) * cap]
    sub = iota((8, runs), 0)
    lane_run = iota((8, runs), 1)
    facts = jnp.where(sub == 0, tile_row + 1, jnp.where(sub == 1, lane_run // dets, lane_run % dets))
    facts = dot_nt(facts.astype(f32).astype(bf16), place)
    meta_ref[...] = jnp.zeros_like(meta_ref)
    for o in range(owners):
        meta_ref[o, 0:8, 0:cap] = facts[:, o * cap : (o + 1) * cap]
        meta_ref[o, 8:16, 0:owners] = counts
    out_ref[:, len(fields) * cap :, :] = meta_ref[...].astype(bf16)
    meta_ref[0] = jnp.zeros(meta_ref.shape[1:], f32)
    meta_ref[0, 0:8, 0:owners] = counts
    counts_ref[...] = meta_ref[0].astype(bf16)


def weights_of(fields_ref, axis, index, run, shape):
    index, high, low = (
        fields_ref[f, pl.ds(run, 1), :].astype(bf16) for f in (index, 2 + axis, 6 + axis)
    )
    rows = iota(shape, 0).astype(f32).astype(bf16)
    zero = jnp.zeros((), bf16)
    return jnp.where(rows == index, low, jnp.where(rows == index + 1, high, zero))


def segments(seg_ref, tile_dev):
    return [
        jnp.max(seg_ref[8 + tile : 9 + tile, :]).astype(jnp.int32) // GROUP for tile in range(tile_dev)
    ]


def tile_of(group, ends):
    tile = jnp.int32(0)
    for end in ends[:-1]:
        tile = tile + (group >= end).astype(jnp.int32)
    return tile


def project_kernel(
    cap,
    kept,
    tile_dev,
    recv_ref,
    tiles_ref,
    out_ref,
    fields_ref,
    ids_ref,
    seg_ref,
    scratch_ref,
    sig_ref,
    lanes_ref,
    half_ref,
):
    owners = recv_ref.shape[0]
    slots = owners * cap
    width = recv_ref.shape[2]
    groups_det, tile_rows, side = tiles_ref.shape
    tile_rows = tile_rows - META
    rows_dev = tile_rows // tile_dev
    part = rows_dev // 3
    for s in range(owners):
        lanes_ref[:, s * cap : (s + 1) * cap] = recv_ref[s, 6 * cap : 6 * cap + META, :].astype(f32)[0:8, 0:cap]
    facts = lanes_ref[...]
    tile1 = facts[0:1].astype(jnp.int32)
    tile_hot = iota((8, slots), 0) + 1 == tile1
    tile_one = ones_where(tile_hot)
    before = ones_where(iota((slots, slots), 0) < iota((slots, slots), 1))
    prefix = dot_nn(tile_one, before)
    count = jnp.sum(jnp.where(tile_hot, 1.0, 0.0), axis=1, keepdims=True)
    padded = jnp.floor((count + (GROUP - 1)) * (1.0 / GROUP)) * GROUP
    padded = jnp.broadcast_to(padded, (8, width))
    start = jnp.zeros((8, width), f32)
    for tile in range(tile_dev - 1):
        start += jnp.where(iota((8, width), 0) > tile, padded[tile : tile + 1], 0.0)
    stop = jnp.minimum(start + padded, float(kept))
    seg_ref[0:8, :] = start
    seg_ref[8:16, :] = stop
    where_to = jnp.sum(jnp.where(tile_hot, prefix + start[:, 0:1], 0.0), axis=0, keepdims=True)
    where_to = jnp.where(tile1 > 0, where_to, -1.0).astype(jnp.int32)
    order = ones_where(iota((kept, slots), 0) == where_to)
    source = (iota((1, slots), 1) // cap).astype(f32)
    sub = iota((8, slots), 0)
    facts = jnp.where(sub == 0, jnp.where(tile1 > 0, 1.0, 0.0), jnp.where(sub == 3, source, facts))
    facts = facts.astype(bf16)
    id_lanes = dot_nt(facts, order)
    scratch_ref[...] = jnp.zeros_like(scratch_ref)
    for q in range(-(-kept // width)):
        many = min(width, kept - q * width)
        scratch_ref[q * 8 : q * 8 + 8, 0:many] = id_lanes[:, q * width : q * width + many]
    for d in range(groups_det):
        scratch_ref[4 + d : 5 + d, :] = tiles_ref[d, tile_rows:, :].astype(f32)[0:1]
    ids_ref[...] = dot_nt(order, facts)
    sorted_fields = []
    for f in range(6):
        field = jnp.concatenate([recv_ref[s, f * cap : (f + 1) * cap, :] for s in range(owners)], axis=0)
        sorted_fields.append(dot_nn(order, field))
    twice = 2.0 * (sorted_fields[4] + sorted_fields[5])
    reach = side // 2 + META
    upper = jnp.where(sorted_fields[0] >= side // 2, 1.0, 0.0)
    fields_ref[0] = sorted_fields[0] - upper * (side - reach)
    fields_ref[1] = sorted_fields[1] + upper * side
    for f in (2, 3):
        fields_ref[f] = sorted_fields[f]
    fields_ref[8] = sorted_fields[0]
    fields_ref[9] = sorted_fields[1]
    fields_ref[4] = jnp.cos(twice)
    fields_ref[5] = jnp.sin(twice)
    fields_ref[6] = (1.0 - sorted_fields[2]).astype(bf16).astype(f32)
    fields_ref[7] = (1.0 - sorted_fields[3]).astype(bf16).astype(f32)
    sig_ref[...] = jnp.zeros_like(sig_ref)
    for tile in range(tile_dev):
        for p in range(3):
            at = tile * rows_dev + p * part
            plane = jnp.concatenate([tiles_ref[d, at : at + part, :] for d in range(groups_det)], axis=0)
            halves = jnp.concatenate([plane[:reach], plane[side - reach :]], axis=1)
            half_ref[tile, p * reach : (p + 1) * reach, :] = halves
    ends = segments(seg_ref, tile_dev)

    def one_group(group):
        tile = tile_of(group, ends)
        base = group * GROUP
        cols = [weights_of(fields_ref, 1, 1, base + k, (2 * side, width)) for k in range(GROUP)]
        partial_rows = dot_nn(half_ref[tile], jnp.concatenate(cols, axis=1))
        for k in range(GROUP):
            row_weight = weights_of(fields_ref, 0, 0, base + k, (reach, width)).astype(f32)
            values = []
            for p in range(3):
                term = partial_rows[p * reach : (p + 1) * reach, k * width : (k + 1) * width]
                values.append(jnp.sum(term * row_weight, axis=0, keepdims=True))
            cos = fields_ref[4, pl.ds(base + k, 1), :]
            sin = fields_ref[5, pl.ds(base + k, 1), :]
            sig_ref[pl.ds(base + k, 1), :] = values[0] + cos * values[1] + sin * values[2]

    def step(g, carry):
        for u in range(UNROLL):
            one_group(g * UNROLL + u)
        return carry

    lax.fori_loop(0, (ends[-1] + UNROLL - 1) // UNROLL, step, 0)
    sent = sig_ref[...].astype(bf16)
    notes = scratch_ref[...].astype(bf16)

    def copy(o, carry):
        out_ref[o, 0:kept, :] = sent
        out_ref[o, kept:, :] = notes
        return carry

    lax.fori_loop(0, owners, copy, 0)


def toeplitz_kernel(line_ref, out_ref):
    lines, rows, width = out_ref.shape
    blocks = rows // width

    def one(d, carry):
        for m in range(blocks):
            at = (blocks - 1 - m) * width
            piece = jnp.broadcast_to(line_ref[d, :, at : at + 2 * width], (width, 2 * width))
            block = pltpu.roll(piece, width, 1, stride=1, stride_axis=0)[:, :width]
            out_ref[d, m * width : (m + 1) * width, :] = block.astype(bf16)
        return carry

    lax.fori_loop(0, lines, one, 0)


def filter_lines(blocks_dev, kept, recv_ref, mat_ref, coef_ref, filt_ref, line_ref):
    owners, rows, width = recv_ref.shape
    lines, padded, _ = line_ref.shape
    count = owners * blocks_dev
    edge = (padded - count) // 2
    spans = padded - count + 1
    together = math.gcd(owners, 8)
    line_ref[...] = jnp.zeros_like(line_ref)

    def some(first, lines_now, line0):
        at, values = [], []
        for o in range(together):
            notes = recv_ref[first + o, kept:, :].astype(f32)
            notes = [notes[q * 8 : q * 8 + 8] for q in range(notes.shape[0] // 8)]
            notes = jnp.concatenate(notes, axis=1)[:, :kept]
            row = notes[2:3] * count + notes[3:4] * blocks_dev + notes[1:2]
            at.append(jnp.where(notes[0:1] > 0.5, row, -1.0))
            values.append(recv_ref[first + o, 0:kept, :])
        at = jnp.concatenate(at, axis=1).astype(jnp.int32) - line0 * count
        place = ones_where(iota((lines_now * count, together * kept), 0) == at)
        return dot_nn(place, jnp.concatenate(values, axis=0))

    if together == owners:
        found = some(0, lines, 0)
        for d in range(lines):
            line_ref[d, edge : edge + count, :] = found[d * count : (d + 1) * count]
    else:

        def one(g, carry):
            for d in range(lines):
                line_ref[d, edge : edge + count, :] += some(g * together, 1, d)
            return carry

        lax.fori_loop(0, owners // together, one, 0)
    for d in range(lines):
        spread = jnp.concatenate([line_ref[d, m : m + count, :].astype(bf16) for m in range(spans)], axis=1)
        weight = coef_ref[d : d + 1, 0:1] + 1.0
        rest = weight - weight.astype(bf16).astype(f32)
        filt_ref[d] = dot_nn(spread, mat_ref[d]) + rest * line_ref[d, edge : edge + count, :]


def back_kernel(
    blocks_dev,
    cap,
    core_ref,
    recv_ref,
    mat_ref,
    coef_ref,
    fields_ref,
    ids_ref,
    seg_ref,
    mine_ref,
    theirs_ref,
    over_ref,
    filt_ref,
    line_ref,
    scaled_ref,
    acc_ref,
):
    width = fields_ref.shape[2]
    kept = fields_ref.shape[1]
    filter_lines(blocks_dev, kept, recv_ref, mat_ref, coef_ref, filt_ref, line_ref)
    pairs, tile_dev, rows_dev, side = mine_ref.shape
    part = rows_dev // 3
    core = core_ref[0]
    owners = recv_ref.shape[0]
    most = totals = jnp.zeros((4, width), f32)
    for s in range(owners):
        counts = recv_ref[s, kept : kept + META, :].astype(f32)[4:8]
        most, totals = jnp.maximum(most, counts), totals + counts
    most = jnp.max(most)
    fullest = jnp.max(totals) + tile_dev * (GROUP - 1)
    over_ref[0] = jnp.logical_or(most > cap, fullest > kept).astype(jnp.int32)
    lines, count, _ = filt_ref.shape
    ids = ids_ref[...]
    at = ids[:, 2:3] * count + ids[:, 3:4] * blocks_dev + ids[:, 1:2]
    at = jnp.where(ids[:, 0:1] > 0.5, at, -1.0).astype(jnp.int32)
    filtered = jnp.zeros((kept, 2 * width), f32)
    for d in range(lines):
        line = filt_ref[d]
        high = line.astype(bf16)
        pair = jnp.concatenate([high, (line - high.astype(f32)).astype(bf16)], axis=1)
        filtered += dot_nn(ones_where(iota((kept, count), 1) + d * count == at), pair)
    filtered = filtered[:, :width] + filtered[:, width:]
    scaled_ref[0] = filtered
    scaled_ref[1] = filtered * fields_ref[4]
    scaled_ref[2] = filtered * fields_ref[5]
    ends = segments(seg_ref, tile_dev)
    acc_ref[...] = jnp.zeros_like(acc_ref)

    def one_group(group):
        base = group * GROUP
        cols, terms = [], []
        for k in range(GROUP):
            cols.append(weights_of(fields_ref, 1, 9, base + k, (side, width)))
            row_weight = weights_of(fields_ref, 0, 8, base + k, (side, width)).astype(f32)
            scaled = [scaled_ref[p, pl.ds(base + k, 1), :] for p in range(3)]
            terms.append(jnp.concatenate([(x * row_weight).astype(bf16) for x in scaled], axis=0))
        return dot_nt(jnp.concatenate(terms, axis=1), jnp.concatenate(cols, axis=1))

    def step(g, carry):
        for u in range(UNROLL):
            acc_ref[tile_of(g * UNROLL + u, ends)] += one_group(g * UNROLL + u)
        return carry

    lax.fori_loop(0, (ends[-1] + UNROLL - 1) // UNROLL, step, 0)
    for tile in range(tile_dev):
        for h in range(pairs):
            for p in range(3):
                base = p * side + h * 2 * part
                mine = acc_ref[tile, pl.ds(pl.multiple_of(base + core * part, part), part), :]
                theirs = acc_ref[tile, pl.ds(pl.multiple_of(base + (1 - core) * part, part), part), :]
                mine_ref[h, tile, p * part : (p + 1) * part, :] = mine
                theirs_ref[h, tile, p * part : (p + 1) * part, :] = theirs.astype(bf16)


def call(kernel, out, scratch=(), **more):
    return pl.pallas_call(
        kernel,
        out_shape=out,
        scratch_shapes=list(scratch),
        compiler_params=pltpu.CompilerParams(vmem_limit_bytes=VMEM_LIMIT),
        **more,
    )


def whole_tiles(
    tiles, position, run_slot, hit_row, hit_col, frac_row, frac_col, angle, noise_coef
):
    owner_total = lax.axis_size("tm")
    groups_det, tile_dev, rows_dev, side_len = tiles.shape
    part = rows_dev // 3
    owned_tiles = tiles.reshape(groups_det, tile_dev, 3, part, side_len)
    owned_tiles = owned_tiles.transpose(1, 2, 0, 3, 4).reshape(tile_dev, 3, side_len, side_len)
    listed_total = position.shape[0]
    per_owner = max(1, listed_total // owner_total)
    slot_total = owner_total * per_owner
    owner_of = position // tile_dev
    local_slot = position % tile_dev
    listing = jnp.arange(listed_total, dtype=jnp.int32)
    earlier_same = (owner_of[:, None] == owner_of[None, :]) & (listing[:, None] > listing[None, :])
    rank_within = jnp.sum(earlier_same.astype(jnp.int32), axis=1)
    outbox_row = owner_of * per_owner + rank_within
    slot_rows = jnp.arange(slot_total, dtype=jnp.int32)
    asked_slot = (
        jnp.sum(
            jnp.where(slot_rows[:, None] == outbox_row[None, :], local_slot[None, :] + 1, 0), axis=1
        )
        - 1
    )
    served_slot = lax.all_to_all(asked_slot, "tm", split_axis=0, concat_axis=0, tiled=True)
    every_tile = jnp.broadcast_to(owned_tiles[None], (owner_total,) + owned_tiles.shape)
    every_tile = lax.all_to_all(every_tile, "tm", split_axis=0, concat_axis=0)
    every_tile = every_tile.reshape((owner_total * tile_dev,) + owned_tiles.shape[1:])
    listed = jnp.take(every_tile, position, axis=0)
    det_local, time_local = hit_row.shape
    run_length = time_local // run_slot.shape[1]
    run_total = det_local * run_slot.shape[1]
    per_group = math.gcd(run_total, group_runs)
    group_total = run_total // per_group

    def grouped(values):
        return values.reshape(group_total, per_group, run_length)

    run_items = (
        run_slot.reshape(group_total, per_group),
        grouped(hit_row),
        grouped(hit_col),
        grouped(frac_row),
        grouped(frac_col),
        grouped(angle),
    )

    def project(items):
        slots, rows_at, cols_at, frac_rows, frac_cols, angles = items
        tiles = jnp.take(listed, slots, axis=0)
        row_weight = run_weights(rows_at, frac_rows, side_len).astype(jnp.float32)
        col_weight = run_weights(cols_at, frac_cols, side_len)
        partial_rows = jnp.einsum(
            "bpij,bsj->bpsi", tiles, col_weight, preferred_element_type=jnp.float32
        )
        values = jnp.sum(partial_rows * row_weight[:, None], axis=3)
        return jnp.sum(values * responses(angles), axis=1)

    signal = lax.map(project, run_items).reshape(det_local, time_local)
    filtered = banded(signal, noise_coef)

    def back_project(carry, items):
        slots, rows_at, cols_at, frac_rows, frac_cols, angles, filt_runs = items
        row_weight = run_weights(rows_at, frac_rows, side_len).astype(jnp.float32)
        col_weight = run_weights(cols_at, frac_cols, side_len)
        scaled = responses(angles) * filt_runs[:, None]
        weighted = (scaled[..., None] * row_weight[:, None]).astype(jnp.bfloat16)
        tile_terms = jnp.einsum(
            "bpsi,bsj->bpij", weighted, col_weight, preferred_element_type=jnp.float32
        )
        return (carry.at[slots].add(tile_terms), None)

    initial = jnp.zeros((listed_total, 3, side_len, side_len), jnp.float32)
    contrib, _ = lax.scan(back_project, initial, run_items + (grouped(filtered),))
    outbox = jnp.zeros((slot_total, 3, side_len, side_len), jnp.float32).at[outbox_row].set(contrib)
    arrived = lax.all_to_all(outbox, "tm", split_axis=0, concat_axis=0, tiled=True)
    summed = jnp.stack(
        [
            jnp.sum(jnp.where((served_slot == slot_id)[:, None, None, None], arrived, 0.0), axis=0)
            for slot_id in range(tile_dev)
        ]
    )
    summed = summed.reshape(tile_dev, 3, groups_det, part, side_len)
    shares = lax.all_to_all(summed, "det", split_axis=2, concat_axis=0)
    return jnp.sum(shares.reshape(groups_det, tile_dev, 3, part, side_len), axis=0)


def body(
    sky_map,
    tile_home,
    piece_tiles,
    run_slot,
    hit_row,
    hit_col,
    frac_row,
    frac_col,
    angle,
    noise_coef,
):
    owners = lax.axis_size("tm")
    groups_det = lax.axis_size("det")
    tile_dev, _, part, side = sky_map.shape
    dets, blocks = run_slot.shape
    runs = dets * blocks
    width = hit_row.shape[1] // blocks
    listed = piece_tiles.shape[2]
    half_band = noise_coef.shape[1] - 1
    cap = round_up(2 * runs // min(owners, listed), META)
    kept = round_up(runs + runs // 2, math.lcm(META, GROUP * UNROLL))
    slots = owners * cap
    reach = side // 2 + META
    piece_list = piece_tiles.reshape(listed)
    smem = pl.BlockSpec(memory_space=pltpu.SMEM)
    vmem = pl.BlockSpec(memory_space=pltpu.VMEM)

    packed, counts = call(
        functools.partial(pack_kernel, owners, cap, tile_dev),
        (
            jax.ShapeDtypeStruct((owners, 6 * cap + META, width), bf16),
            jax.ShapeDtypeStruct((META, width), bf16),
        ),
        [pltpu.VMEM((owners, META, width), f32)],
        in_specs=[smem, smem] + [vmem] * 6,
        out_specs=(vmem, vmem),
    )(
        piece_list,
        tile_home,
        run_slot,
        hit_row,
        hit_col,
        frac_row,
        frac_col,
        angle,
    )
    recv = lax.all_to_all(packed, "tm", split_axis=0, concat_axis=0, tiled=True)
    rows = jnp.concatenate([sky_map.reshape(tile_dev * 3 * part, side), counts], axis=0)
    tiles = lax.all_gather(rows, "det", axis=0)

    weights = jnp.concatenate([noise_coef[:, :1] + 1.0, noise_coef[:, 1:]], axis=1)
    line = jnp.concatenate(
        [
            jnp.zeros((dets, width), f32),
            weights[:, ::-1],
            weights[:, 1:],
            jnp.zeros((dets, width - 1), f32),
        ],
        axis=1,
    )
    spans = 2 * (half_band // width) + 1
    matrix = call(
        toeplitz_kernel,
        pltpu.VMEM((dets, spans * width, width), bf16),
    )(line[:, None, :])

    notes = round_up(kept, width) // width * 8
    sent, fields, ids, seg = call(
        functools.partial(project_kernel, cap, kept, tile_dev),
        (
            jax.ShapeDtypeStruct((owners, kept + notes, width), bf16),
            jax.ShapeDtypeStruct((10, kept, width), f32),
            jax.ShapeDtypeStruct((kept, 8), f32),
            jax.ShapeDtypeStruct((16, width), f32),
        ),
        [
            pltpu.VMEM((notes, width), f32),
            pltpu.VMEM((kept, width), f32),
            pltpu.VMEM((8, slots), f32),
            pltpu.VMEM((tile_dev, 3 * reach, 2 * side), bf16),
        ],
    )(recv, tiles)
    heard = lax.all_to_all(sent, "tm", split_axis=0, concat_axis=0, tiled=True)

    count = owners * blocks
    place = lax.axis_index("det")
    core = lax.rem(place, 2)
    half = lax.div(place, 2)
    pairs = groups_det // 2
    mine, theirs, over = call(
        functools.partial(back_kernel, blocks, cap),
        (
            jax.ShapeDtypeStruct((pairs, tile_dev, 3 * part, side), f32),
            jax.ShapeDtypeStruct((pairs, tile_dev, 3 * part, side), bf16),
            jax.ShapeDtypeStruct((1,), jnp.int32),
        ),
        [
            pltpu.VMEM((dets, count, width), f32),
            pltpu.VMEM((dets, count + spans - 1, width), f32),
            pltpu.VMEM((3, kept, width), f32),
            pltpu.VMEM((tile_dev, 3 * side, side), f32),
        ],
        in_specs=[smem] + [vmem] * 6,
        out_specs=(vmem, vmem, smem),
    )(core[None].astype(jnp.int32), heard, matrix, noise_coef, fields, ids, seg)

    beside = lax.ppermute(theirs, "det", [(i, i ^ 1) for i in range(groups_det)])

    def of_pair(h):
        pick = lambda values: lax.dynamic_index_in_dim(values, h, 0, keepdims=False).astype(f32)
        return pick(mine) + pick(beside)

    others = []
    for step in range(1, pairs):
        ring = [(i, (i + 2 * step) % groups_det) for i in range(groups_det)]
        sent_on = of_pair(lax.rem(half + step, pairs)).astype(bf16)
        others.append(lax.ppermute(sent_on, "det", ring))

    def summed(_):
        total = of_pair(half)
        for other in others:
            total = total + other.astype(f32)
        return total.reshape(tile_dev, 3, part, side)

    def travelling(_):
        position = positions_of(piece_list, tile_home)
        whole = tiles[:, : tile_dev * 3 * part].reshape(groups_det, tile_dev, 3 * part, side)
        return whole_tiles(
            whole, position, run_slot, hit_row, hit_col, frac_row, frac_col, angle, noise_coef
        )

    return lax.cond(over[0] == 0, summed, travelling, 0)


def solution(mesh):
    placed = (
        P("tm", None, "det", None),
        P(),
        P("det", "tm", None),
        P("det", "tm"),
        P("det", "tm"),
        P("det", "tm"),
        P("det", "tm"),
        P("det", "tm"),
        P("det", "tm"),
        P("det", None),
    )
    return jax.shard_map(
        body, mesh=mesh, in_specs=placed, out_specs=P("tm", None, "det", None), check_vma=False
    )
```

```python
import functools
import math

import jax
import jax.numpy as jnp
from jax import lax
from jax.experimental import pallas as pl
from jax.experimental.pallas import tpu as pltpu
from jax.sharding import PartitionSpec as P

LISTED = 32


block_cols = 128
group_runs = 32


def extended_2(cells, sides, width):
    for axis, dim in sides:
        count = lax.axis_size(axis)
        ends = count - 1
        head = lax.slice_in_dim(cells, 0, width, axis=dim)
        tail = lax.slice_in_dim(cells, cells.shape[dim] - width, cells.shape[dim], axis=dim)
        cells = jnp.concatenate(
            [
                lax.ppermute(tail, axis, [(i, (i + 1) % count) for i in range(ends)]),
                cells,
                lax.ppermute(head, axis, [((i + 1) % count, i) for i in range(ends)]),
            ],
            axis=dim,
        )
    return cells


def positions_of(piece_list, tile_home):
    table_rows = jnp.arange(tile_home.shape[0], dtype=jnp.int32)
    matched = piece_list[:, None] == table_rows[None, :]
    return jnp.sum(jnp.where(matched, tile_home[None, :], 0), axis=1)


def run_weights(pixel_index, upper_frac, side_len):
    lower_weight = (1.0 - upper_frac.astype(jnp.float32)).astype(jnp.bfloat16)
    pixels = lax.broadcasted_iota(jnp.int32, pixel_index.shape + (side_len,), pixel_index.ndim)
    zero_value = jnp.zeros((), jnp.bfloat16)
    low_part = jnp.where(pixels == pixel_index[..., None], lower_weight[..., None], zero_value)
    high_part = jnp.where(pixels == pixel_index[..., None] + 1, upper_frac[..., None], zero_value)
    return low_part + high_part


def responses(angles):
    twice = 2.0 * angles
    return jnp.stack([jnp.ones_like(twice), jnp.cos(twice), jnp.sin(twice)], axis=1)


def banded(signal, noise_coef):
    det_count = signal.shape[0]
    half_band = noise_coef.shape[1] - 1
    reach_blocks = half_band // block_cols
    span_cols = (2 * reach_blocks + 1) * block_cols
    weights = jnp.concatenate([noise_coef[:, :1] + 1.0, noise_coef[:, 1:]], axis=1)
    zero_pad = jnp.zeros((det_count, block_cols - 1), jnp.float32)
    kernel_row = jnp.concatenate(
        [
            zero_pad,
            weights[:, ::-1],
            weights[:, 1:],
            zero_pad,
            jnp.zeros((det_count, 1), jnp.float32),
        ],
        axis=1,
    )
    period = span_cols + block_cols
    tiled_rows = jnp.tile(kernel_row, (1, block_cols))[:, : block_cols * (period - 1)]
    tiled_rows = tiled_rows.reshape(det_count, block_cols, period - 1)
    matrix = tiled_rows[:, :, block_cols - 1 : block_cols - 1 + span_cols]
    matrix = matrix.reshape(det_count, block_cols, 2 * reach_blocks + 1, block_cols)
    extended = extended_2(signal, (("tm", 1),), half_band)
    block_count = signal.shape[1] // block_cols
    blocks = extended.reshape(det_count, block_count + 2 * reach_blocks, block_cols)
    stacked = jnp.stack(
        [blocks[:, offset : offset + block_count] for offset in range(2 * reach_blocks + 1)], axis=1
    )
    result = jnp.einsum(
        "diml,dmnl->dni",
        matrix,
        stacked,
        precision=lax.Precision.HIGHEST,
        preferred_element_type=jnp.float32,
    )
    return result.reshape(det_count, block_count * block_cols)


GROUP = 4
UNROLL = 6
META = 16
VMEM_LIMIT = 24 * 1024 * 1024
f32 = jnp.float32
bf16 = jnp.bfloat16


def round_up(value, step):
    return -(-value // step) * step


def iota(shape, dim):
    return lax.broadcasted_iota(jnp.int32, shape, dim)


def dot_nn(a, b):
    return lax.dot_general(a, b, (((1,), (0,)), ((), ())), preferred_element_type=f32)


def dot_nt(a, b):
    return lax.dot_general(a, b, (((1,), (1,)), ((), ())), preferred_element_type=f32)


def ones_where(mask):
    return jnp.where(mask, 1.0, 0.0).astype(bf16)


def pack_kernel(
    owners,
    cap,
    tile_dev,
    pt_ref,
    th_ref,
    slot_ref,
    r_ref,
    c_ref,
    fr_ref,
    fc_ref,
    ang_ref,
    out_ref,
    counts_ref,
    meta_ref,
):
    dets, blocks = slot_ref.shape
    runs = dets * blocks
    width = r_ref.shape[1] // blocks
    listed = pt_ref.shape[0]
    spread = dot_nn(
        slot_ref[...].astype(f32).astype(bf16),
        ones_where(iota((blocks, runs), 1) // dets == iota((blocks, runs), 0)),
    )
    run_id = iota((dets, runs), 1)
    own_det = run_id % dets == iota((dets, runs), 0)
    slot_row = jnp.sum(jnp.where(own_det, spread, 0.0), axis=0, keepdims=True)
    slot_row = slot_row.astype(jnp.int32)
    owner_row = jnp.zeros((1, runs), jnp.int32)
    tile_row = jnp.zeros((1, runs), jnp.int32)
    for k in range(listed):
        pos = th_ref[pt_ref[k]]
        own = lax.div(pos, jnp.int32(tile_dev))
        owner_row = jnp.where(slot_row == k, own, owner_row)
        tile_row = jnp.where(slot_row == k, pos - own * tile_dev, tile_row)
    owner_hot = iota((owners, runs), 0) == owner_row
    owner_one = ones_where(owner_hot)
    before = ones_where(iota((runs, runs), 0) < iota((runs, runs), 1))
    prefix = dot_nn(owner_one, before)
    rank = jnp.sum(jnp.where(owner_hot, prefix, 0.0), axis=0, keepdims=True).astype(jnp.int32)
    counts = dot_nt(jnp.ones((8, runs), bf16), owner_one)
    dest = jnp.where(rank < cap, owner_row * cap + rank, -1)
    place = ones_where(iota((owners * cap, runs), 0) == dest)

    def by_run(ref):
        return jnp.concatenate(
            [ref[:, b * width : (b + 1) * width].astype(f32) for b in range(blocks)], axis=0
        )

    angle = by_run(ang_ref)
    angle_high = angle.astype(bf16)
    angle_low = (angle - angle_high.astype(f32)).astype(bf16)
    fields = [by_run(ref).astype(bf16) for ref in (r_ref, c_ref, fr_ref, fc_ref)]
    fields += [angle_high, angle_low]
    for f, field in enumerate(fields):
        sent = dot_nn(place, field).astype(bf16)
        for o in range(owners):
            out_ref[o, f * cap : (f + 1) * cap, :] = sent[o * cap : (o + 1) * cap]
    sub = iota((8, runs), 0)
    lane_run = iota((8, runs), 1)
    facts = jnp.where(sub == 0, tile_row + 1, jnp.where(sub == 1, lane_run // dets, lane_run % dets))
    facts = dot_nt(facts.astype(f32).astype(bf16), place)
    meta_ref[...] = jnp.zeros_like(meta_ref)
    for o in range(owners):
        meta_ref[o, 0:8, 0:cap] = facts[:, o * cap : (o + 1) * cap]
        meta_ref[o, 8:16, 0:owners] = counts
    out_ref[:, len(fields) * cap :, :] = meta_ref[...].astype(bf16)
    meta_ref[0] = jnp.zeros(meta_ref.shape[1:], f32)
    meta_ref[0, 0:8, 0:owners] = counts
    counts_ref[...] = meta_ref[0].astype(bf16)


def weights_of(fields_ref, axis, index, run, shape):
    index, high, low = (
        fields_ref[f, pl.ds(run, 1), :].astype(bf16) for f in (index, 2 + axis, 6 + axis)
    )
    rows = iota(shape, 0).astype(f32).astype(bf16)
    zero = jnp.zeros((), bf16)
    return jnp.where(rows == index, low, jnp.where(rows == index + 1, high, zero))


def segments(seg_ref, tile_dev):
    return [
        jnp.max(seg_ref[8 + tile : 9 + tile, :]).astype(jnp.int32) // GROUP for tile in range(tile_dev)
    ]


def tile_of(group, ends):
    tile = jnp.int32(0)
    for end in ends[:-1]:
        tile = tile + (group >= end).astype(jnp.int32)
    return tile


def project_kernel(
    cap,
    kept,
    tile_dev,
    recv_ref,
    tiles_ref,
    out_ref,
    fields_ref,
    ids_ref,
    seg_ref,
    scratch_ref,
    sig_ref,
    lanes_ref,
    half_ref,
):
    owners = recv_ref.shape[0]
    slots = owners * cap
    width = recv_ref.shape[2]
    groups_det, tile_rows, side = tiles_ref.shape
    tile_rows = tile_rows - META
    rows_dev = tile_rows // tile_dev
    part = rows_dev // 3
    for s in range(owners):
        lanes_ref[:, s * cap : (s + 1) * cap] = recv_ref[s, 6 * cap : 6 * cap + META, :].astype(f32)[0:8, 0:cap]
    facts = lanes_ref[...]
    tile1 = facts[0:1].astype(jnp.int32)
    tile_hot = iota((8, slots), 0) + 1 == tile1
    tile_one = ones_where(tile_hot)
    before = ones_where(iota((slots, slots), 0) < iota((slots, slots), 1))
    prefix = dot_nn(tile_one, before)
    count = jnp.sum(jnp.where(tile_hot, 1.0, 0.0), axis=1, keepdims=True)
    padded = jnp.floor((count + (GROUP - 1)) * (1.0 / GROUP)) * GROUP
    padded = jnp.broadcast_to(padded, (8, width))
    start = jnp.zeros((8, width), f32)
    for tile in range(tile_dev - 1):
        start += jnp.where(iota((8, width), 0) > tile, padded[tile : tile + 1], 0.0)
    stop = jnp.minimum(start + padded, float(kept))
    seg_ref[0:8, :] = start
    seg_ref[8:16, :] = stop
    where_to = jnp.sum(jnp.where(tile_hot, prefix + start[:, 0:1], 0.0), axis=0, keepdims=True)
    where_to = jnp.where(tile1 > 0, where_to, -1.0).astype(jnp.int32)
    order = ones_where(iota((kept, slots), 0) == where_to)
    source = (iota((1, slots), 1) // cap).astype(f32)
    sub = iota((8, slots), 0)
    facts = jnp.where(sub == 0, jnp.where(tile1 > 0, 1.0, 0.0), jnp.where(sub == 3, source, facts))
    facts = facts.astype(bf16)
    id_lanes = dot_nt(facts, order)
    scratch_ref[...] = jnp.zeros_like(scratch_ref)
    for q in range(-(-kept // width)):
        many = min(width, kept - q * width)
        scratch_ref[q * 8 : q * 8 + 8, 0:many] = id_lanes[:, q * width : q * width + many]
    for d in range(groups_det):
        scratch_ref[4 + d : 5 + d, :] = tiles_ref[d, tile_rows:, :].astype(f32)[0:1]
    ids_ref[...] = dot_nt(order, facts)
    sorted_fields = dot_nn(
        order,
        jnp.concatenate(
            [
                jnp.concatenate([recv_ref[s, f * cap : (f + 1) * cap, :] for s in range(owners)], axis=0)
                for f in range(6)
            ],
            axis=1,
        ),
    )
    sorted_fields = [sorted_fields[:, f * width : (f + 1) * width] for f in range(6)]
    twice = 2.0 * (sorted_fields[4] + sorted_fields[5])
    reach = side // 2 + META
    upper = jnp.where(sorted_fields[0] >= side // 2, 1.0, 0.0)
    fields_ref[0] = sorted_fields[0] - upper * (side - reach)
    fields_ref[1] = sorted_fields[1] + upper * side
    for f in (2, 3):
        fields_ref[f] = sorted_fields[f]
    fields_ref[8] = sorted_fields[0]
    fields_ref[9] = sorted_fields[1]
    fields_ref[4] = jnp.cos(twice)
    fields_ref[5] = jnp.sin(twice)
    fields_ref[6] = (1.0 - sorted_fields[2]).astype(bf16).astype(f32)
    fields_ref[7] = (1.0 - sorted_fields[3]).astype(bf16).astype(f32)
    sig_ref[...] = jnp.zeros_like(sig_ref)
    for tile in range(tile_dev):
        for p in range(3):
            at = tile * rows_dev + p * part
            plane = jnp.concatenate([tiles_ref[d, at : at + part, :] for d in range(groups_det)], axis=0)
            halves = jnp.concatenate([plane[:reach], plane[side - reach :]], axis=1)
            half_ref[tile, p * reach : (p + 1) * reach, :] = halves
    ends = segments(seg_ref, tile_dev)

    def one_group(group):
        tile = tile_of(group, ends)
        base = group * GROUP
        cols = [weights_of(fields_ref, 1, 1, base + k, (2 * side, width)) for k in range(GROUP)]
        partial_rows = dot_nn(half_ref[tile], jnp.concatenate(cols, axis=1))
        for k in range(GROUP):
            row_weight = weights_of(fields_ref, 0, 0, base + k, (reach, width)).astype(f32)
            values = []
            for p in range(3):
                term = partial_rows[p * reach : (p + 1) * reach, k * width : (k + 1) * width]
                values.append(jnp.sum(term * row_weight, axis=0, keepdims=True))
            cos = fields_ref[4, pl.ds(base + k, 1), :]
            sin = fields_ref[5, pl.ds(base + k, 1), :]
            sig_ref[pl.ds(base + k, 1), :] = values[0] + cos * values[1] + sin * values[2]

    def step(g, carry):
        for u in range(UNROLL):
            one_group(g * UNROLL + u)
        return carry

    lax.fori_loop(0, (ends[-1] + UNROLL - 1) // UNROLL, step, 0)
    sent = sig_ref[...].astype(bf16)
    notes = scratch_ref[...].astype(bf16)

    def copy(o, carry):
        out_ref[o, 0:kept, :] = sent
        out_ref[o, kept:, :] = notes
        return carry

    lax.fori_loop(0, owners, copy, 0)


def toeplitz_kernel(line_ref, out_ref):
    lines, rows, width = out_ref.shape
    blocks = rows // width

    def one(d, carry):
        for m in range(blocks):
            at = (blocks - 1 - m) * width
            piece = jnp.broadcast_to(line_ref[d, :, at : at + 2 * width], (width, 2 * width))
            block = pltpu.roll(piece, width, 1, stride=1, stride_axis=0)[:, :width]
            out_ref[d, m * width : (m + 1) * width, :] = block.astype(bf16)
        return carry

    lax.fori_loop(0, lines, one, 0)


def lines_kernel(blocks_dev, kept, cap, tile_dev, edge, recv_ref, line_ref, over_ref):
    owners, rows, width = recv_ref.shape
    lines = line_ref.shape[0]
    count = owners * blocks_dev
    most = totals = jnp.zeros((4, width), f32)
    for s in range(owners):
        counts = recv_ref[s, kept : kept + META, :].astype(f32)[4:8]
        most, totals = jnp.maximum(most, counts), totals + counts
    most = jnp.max(most)
    fullest = jnp.max(totals) + tile_dev * (GROUP - 1)
    over_ref[0] = jnp.logical_or(most > cap, fullest > kept).astype(jnp.int32)
    together = math.gcd(owners, 8)
    line_ref[...] = jnp.zeros_like(line_ref)

    def some(first, lines_now, line0):
        at, det, values = [], [], []
        for o in range(together):
            notes = recv_ref[first + o, kept:, :].astype(f32)
            notes = [notes[q * 8 : q * 8 + 8] for q in range(notes.shape[0] // 8)]
            notes = jnp.concatenate(notes, axis=1)[:, :kept]
            row = notes[3:4] * blocks_dev + notes[1:2]
            at.append(jnp.where(notes[0:1] > 0.5, row, -1.0))
            det.append(notes[2:3])
            values.append(recv_ref[first + o, 0:kept, :])
        at = jnp.concatenate(at, axis=1).astype(jnp.int32)
        det = jnp.concatenate(det, axis=1)
        place = ones_where(iota((count, together * kept), 0) == at)
        place = [place * ones_where(det == line0 + d) for d in range(lines_now)]
        return dot_nn(jnp.concatenate(place, axis=0), jnp.concatenate(values, axis=0))

    if together == owners:
        found = some(0, lines, 0)
        for d in range(lines):
            line_ref[d, edge : edge + count, :] = found[d * count : (d + 1) * count]
    else:

        def one(g, carry):
            for d in range(lines):
                line_ref[d, edge : edge + count, :] += some(g * together, 1, d)
            return carry

        lax.fori_loop(0, owners // together, one, 0)


def filter_lines(line_ref, mat_ref, coef_ref, filt_ref):
    lines, padded, width = line_ref.shape
    count = filt_ref.shape[1]
    spans = padded - count + 1
    edge = spans // 2
    for d in range(lines):
        spread = jnp.concatenate([line_ref[d, m : m + count, :].astype(bf16) for m in range(spans)], axis=1)
        weight = coef_ref[d : d + 1, 0:1] + 1.0
        rest = weight - weight.astype(bf16).astype(f32)
        filt_ref[d] = dot_nn(spread, mat_ref[d]) + rest * line_ref[d, edge : edge + count, :]


def back_kernel(
    blocks_dev,
    core_ref,
    line_ref,
    mat_ref,
    coef_ref,
    fields_ref,
    ids_ref,
    seg_ref,
    mine_ref,
    theirs_ref,
    filt_ref,
    scaled_ref,
    acc_ref,
):
    width = fields_ref.shape[2]
    kept = fields_ref.shape[1]
    filter_lines(line_ref, mat_ref, coef_ref, filt_ref)
    pairs, tile_dev, rows_dev, side = mine_ref.shape
    part = rows_dev // 3
    core = core_ref[0]
    lines, count, _ = filt_ref.shape
    ids = ids_ref[...]
    at = ids[:, 2:3] * count + ids[:, 3:4] * blocks_dev + ids[:, 1:2]
    at = jnp.where(ids[:, 0:1] > 0.5, at, -1.0).astype(jnp.int32)
    filtered = jnp.zeros((kept, 2 * width), f32)
    for d in range(lines):
        line = filt_ref[d]
        high = line.astype(bf16)
        pair = jnp.concatenate([high, (line - high.astype(f32)).astype(bf16)], axis=1)
        filtered += dot_nn(ones_where(iota((kept, count), 1) + d * count == at), pair)
    filtered = filtered[:, :width] + filtered[:, width:]
    scaled_ref[0] = filtered
    scaled_ref[1] = filtered * fields_ref[4]
    scaled_ref[2] = filtered * fields_ref[5]
    ends = segments(seg_ref, tile_dev)
    acc_ref[...] = jnp.zeros_like(acc_ref)

    def one_group(group):
        base = group * GROUP
        cols, terms = [], []
        for k in range(GROUP):
            cols.append(weights_of(fields_ref, 1, 9, base + k, (side, width)))
            row_weight = weights_of(fields_ref, 0, 8, base + k, (side, width)).astype(f32)
            scaled = [scaled_ref[p, pl.ds(base + k, 1), :] for p in range(3)]
            terms.append(jnp.concatenate([(x * row_weight).astype(bf16) for x in scaled], axis=0))
        return dot_nt(jnp.concatenate(terms, axis=1), jnp.concatenate(cols, axis=1))

    def step(g, carry):
        for u in range(UNROLL):
            acc_ref[tile_of(g * UNROLL + u, ends)] += one_group(g * UNROLL + u)
        return carry

    lax.fori_loop(0, (ends[-1] + UNROLL - 1) // UNROLL, step, 0)
    for tile in range(tile_dev):
        for h in range(pairs):
            for p in range(3):
                base = p * side + h * 2 * part
                mine = acc_ref[tile, pl.ds(pl.multiple_of(base + core * part, part), part), :]
                theirs = acc_ref[tile, pl.ds(pl.multiple_of(base + (1 - core) * part, part), part), :]
                mine_ref[h, tile, p * part : (p + 1) * part, :] = mine
                theirs_ref[h, tile, p * part : (p + 1) * part, :] = theirs.astype(bf16)


def call(kernel, out, scratch=(), **more):
    return pl.pallas_call(
        kernel,
        out_shape=out,
        scratch_shapes=list(scratch),
        compiler_params=pltpu.CompilerParams(vmem_limit_bytes=VMEM_LIMIT),
        **more,
    )


def whole_tiles(
    tiles, position, run_slot, hit_row, hit_col, frac_row, frac_col, angle, noise_coef
):
    owner_total = lax.axis_size("tm")
    groups_det, tile_dev, rows_dev, side_len = tiles.shape
    part = rows_dev // 3
    owned_tiles = tiles.reshape(groups_det, tile_dev, 3, part, side_len)
    owned_tiles = owned_tiles.transpose(1, 2, 0, 3, 4).reshape(tile_dev, 3, side_len, side_len)
    listed_total = position.shape[0]
    per_owner = max(1, listed_total // owner_total)
    slot_total = owner_total * per_owner
    owner_of = position // tile_dev
    local_slot = position % tile_dev
    listing = jnp.arange(listed_total, dtype=jnp.int32)
    earlier_same = (owner_of[:, None] == owner_of[None, :]) & (listing[:, None] > listing[None, :])
    rank_within = jnp.sum(earlier_same.astype(jnp.int32), axis=1)
    outbox_row = owner_of * per_owner + rank_within
    slot_rows = jnp.arange(slot_total, dtype=jnp.int32)
    asked_slot = (
        jnp.sum(
            jnp.where(slot_rows[:, None] == outbox_row[None, :], local_slot[None, :] + 1, 0), axis=1
        )
        - 1
    )
    served_slot = lax.all_to_all(asked_slot, "tm", split_axis=0, concat_axis=0, tiled=True)
    every_tile = jnp.broadcast_to(owned_tiles[None], (owner_total,) + owned_tiles.shape)
    every_tile = lax.all_to_all(every_tile, "tm", split_axis=0, concat_axis=0)
    every_tile = every_tile.reshape((owner_total * tile_dev,) + owned_tiles.shape[1:])
    listed = jnp.take(every_tile, position, axis=0)
    det_local, time_local = hit_row.shape
    run_length = time_local // run_slot.shape[1]
    run_total = det_local * run_slot.shape[1]
    per_group = math.gcd(run_total, group_runs)
    group_total = run_total // per_group

    def grouped(values):
        return values.reshape(group_total, per_group, run_length)

    run_items = (
        run_slot.reshape(group_total, per_group),
        grouped(hit_row),
        grouped(hit_col),
        grouped(frac_row),
        grouped(frac_col),
        grouped(angle),
    )

    def project(items):
        slots, rows_at, cols_at, frac_rows, frac_cols, angles = items
        tiles = jnp.take(listed, slots, axis=0)
        row_weight = run_weights(rows_at, frac_rows, side_len).astype(jnp.float32)
        col_weight = run_weights(cols_at, frac_cols, side_len)
        partial_rows = jnp.einsum(
            "bpij,bsj->bpsi", tiles, col_weight, preferred_element_type=jnp.float32
        )
        values = jnp.sum(partial_rows * row_weight[:, None], axis=3)
        return jnp.sum(values * responses(angles), axis=1)

    signal = lax.map(project, run_items).reshape(det_local, time_local)
    filtered = banded(signal, noise_coef)

    def back_project(carry, items):
        slots, rows_at, cols_at, frac_rows, frac_cols, angles, filt_runs = items
        row_weight = run_weights(rows_at, frac_rows, side_len).astype(jnp.float32)
        col_weight = run_weights(cols_at, frac_cols, side_len)
        scaled = responses(angles) * filt_runs[:, None]
        weighted = (scaled[..., None] * row_weight[:, None]).astype(jnp.bfloat16)
        tile_terms = jnp.einsum(
            "bpsi,bsj->bpij", weighted, col_weight, preferred_element_type=jnp.float32
        )
        return (carry.at[slots].add(tile_terms), None)

    initial = jnp.zeros((listed_total, 3, side_len, side_len), jnp.float32)
    contrib, _ = lax.scan(back_project, initial, run_items + (grouped(filtered),))
    outbox = jnp.zeros((slot_total, 3, side_len, side_len), jnp.float32).at[outbox_row].set(contrib)
    arrived = lax.all_to_all(outbox, "tm", split_axis=0, concat_axis=0, tiled=True)
    summed = jnp.stack(
        [
            jnp.sum(jnp.where((served_slot == slot_id)[:, None, None, None], arrived, 0.0), axis=0)
            for slot_id in range(tile_dev)
        ]
    )
    summed = summed.reshape(tile_dev, 3, groups_det, part, side_len)
    shares = lax.all_to_all(summed, "det", split_axis=2, concat_axis=0)
    return jnp.sum(shares.reshape(groups_det, tile_dev, 3, part, side_len), axis=0)


def body(
    sky_map,
    tile_home,
    piece_tiles,
    run_slot,
    hit_row,
    hit_col,
    frac_row,
    frac_col,
    angle,
    noise_coef,
):
    owners = lax.axis_size("tm")
    groups_det = lax.axis_size("det")
    tile_dev, _, part, side = sky_map.shape
    dets, blocks = run_slot.shape
    runs = dets * blocks
    width = hit_row.shape[1] // blocks
    listed = piece_tiles.shape[2]
    half_band = noise_coef.shape[1] - 1
    cap = round_up(2 * runs // min(owners, listed), META)
    kept = round_up(runs + runs // 2, math.lcm(META, GROUP * UNROLL))
    slots = owners * cap
    reach = side // 2 + META
    piece_list = piece_tiles.reshape(listed)
    smem = pl.BlockSpec(memory_space=pltpu.SMEM)
    vmem = pl.BlockSpec(memory_space=pltpu.VMEM)

    packed, counts = call(
        functools.partial(pack_kernel, owners, cap, tile_dev),
        (
            jax.ShapeDtypeStruct((owners, 6 * cap + META, width), bf16),
            jax.ShapeDtypeStruct((META, width), bf16),
        ),
        [pltpu.VMEM((owners, META, width), f32)],
        in_specs=[smem, smem] + [vmem] * 6,
        out_specs=(vmem, vmem),
    )(
        piece_list,
        tile_home,
        run_slot,
        hit_row,
        hit_col,
        frac_row,
        frac_col,
        angle,
    )
    recv = lax.all_to_all(packed, "tm", split_axis=0, concat_axis=0, tiled=True)
    rows = jnp.concatenate([sky_map.reshape(tile_dev * 3 * part, side), counts], axis=0)
    tiles = lax.all_gather(rows, "det", axis=0)

    weights = jnp.concatenate([noise_coef[:, :1] + 1.0, noise_coef[:, 1:]], axis=1)
    line = jnp.concatenate(
        [
            jnp.zeros((dets, width), f32),
            weights[:, ::-1],
            weights[:, 1:],
            jnp.zeros((dets, width - 1), f32),
        ],
        axis=1,
    )
    spans = 2 * (half_band // width) + 1
    matrix = call(
        toeplitz_kernel,
        pltpu.VMEM((dets, spans * width, width), bf16),
    )(line[:, None, :])

    notes = round_up(kept, width) // width * 8
    sent, fields, ids, seg = call(
        functools.partial(project_kernel, cap, kept, tile_dev),
        (
            jax.ShapeDtypeStruct((owners, kept + notes, width), bf16),
            jax.ShapeDtypeStruct((10, kept, width), f32),
            jax.ShapeDtypeStruct((kept, 8), f32),
            jax.ShapeDtypeStruct((16, width), f32),
        ),
        [
            pltpu.VMEM((notes, width), f32),
            pltpu.VMEM((kept, width), f32),
            pltpu.VMEM((8, slots), f32),
            pltpu.VMEM((tile_dev, 3 * reach, 2 * side), bf16),
        ],
    )(recv, tiles)
    heard = lax.all_to_all(sent, "tm", split_axis=0, concat_axis=0, tiled=True)

    count = owners * blocks
    place = lax.axis_index("det")
    core = lax.rem(place, 2)
    half = lax.div(place, 2)
    pairs = groups_det // 2
    heard, over = call(
        functools.partial(lines_kernel, blocks, kept, cap, tile_dev, spans // 2),
        (
            jax.ShapeDtypeStruct((dets, count + spans - 1, width), f32),
            jax.ShapeDtypeStruct((1,), jnp.int32),
        ),
        in_specs=[vmem],
        out_specs=(vmem, smem),
    )(heard)
    mine, theirs = call(
        functools.partial(back_kernel, blocks),
        (
            jax.ShapeDtypeStruct((pairs, tile_dev, 3 * part, side), f32),
            jax.ShapeDtypeStruct((pairs, tile_dev, 3 * part, side), bf16),
        ),
        [
            pltpu.VMEM((dets, count, width), f32),
            pltpu.VMEM((3, kept, width), f32),
            pltpu.VMEM((tile_dev, 3 * side, side), f32),
        ],
        in_specs=[smem] + [vmem] * 6,
        out_specs=(vmem, vmem),
    )(core[None].astype(jnp.int32), heard, matrix, noise_coef, fields, ids, seg)

    beside = lax.ppermute(theirs, "det", [(i, i ^ 1) for i in range(groups_det)])

    def of_pair(h):
        pick = lambda values: lax.dynamic_index_in_dim(values, h, 0, keepdims=False).astype(f32)
        return pick(mine) + pick(beside)

    others = []
    for step in range(1, pairs):
        ring = [(i, (i + 2 * step) % groups_det) for i in range(groups_det)]
        sent_on = of_pair(lax.rem(half + step, pairs)).astype(bf16)
        others.append(lax.ppermute(sent_on, "det", ring))

    def summed(_):
        total = of_pair(half)
        for other in others:
            total = total + other.astype(f32)
        return total.reshape(tile_dev, 3, part, side)

    def travelling(_):
        position = positions_of(piece_list, tile_home)
        whole = tiles[:, : tile_dev * 3 * part].reshape(groups_det, tile_dev, 3 * part, side)
        return whole_tiles(
            whole, position, run_slot, hit_row, hit_col, frac_row, frac_col, angle, noise_coef
        )

    return lax.cond(over[0] == 0, summed, travelling, 0)


def solution(mesh):
    placed = (
        P("tm", None, "det", None),
        P(),
        P("det", "tm", None),
        P("det", "tm"),
        P("det", "tm"),
        P("det", "tm"),
        P("det", "tm"),
        P("det", "tm"),
        P("det", "tm"),
        P("det", None),
    )
    return jax.shard_map(
        body, mesh=mesh, in_specs=placed, out_specs=P("tm", None, "det", None), check_vma=False
    )
```

```python
import functools
import math

import jax
import jax.numpy as jnp
from jax import lax
from jax.experimental import pallas as pl
from jax.experimental.pallas import tpu as pltpu
from jax.sharding import PartitionSpec as P

LISTED = 32


block_cols = 128
group_runs = 32


def extended_2(cells, sides, width):
    for axis, dim in sides:
        count = lax.axis_size(axis)
        ends = count - 1
        head = lax.slice_in_dim(cells, 0, width, axis=dim)
        tail = lax.slice_in_dim(cells, cells.shape[dim] - width, cells.shape[dim], axis=dim)
        cells = jnp.concatenate(
            [
                lax.ppermute(tail, axis, [(i, (i + 1) % count) for i in range(ends)]),
                cells,
                lax.ppermute(head, axis, [((i + 1) % count, i) for i in range(ends)]),
            ],
            axis=dim,
        )
    return cells


def positions_of(piece_list, tile_home):
    table_rows = jnp.arange(tile_home.shape[0], dtype=jnp.int32)
    matched = piece_list[:, None] == table_rows[None, :]
    return jnp.sum(jnp.where(matched, tile_home[None, :], 0), axis=1)


def run_weights(pixel_index, upper_frac, side_len):
    lower_weight = (1.0 - upper_frac.astype(jnp.float32)).astype(jnp.bfloat16)
    pixels = lax.broadcasted_iota(jnp.int32, pixel_index.shape + (side_len,), pixel_index.ndim)
    zero_value = jnp.zeros((), jnp.bfloat16)
    low_part = jnp.where(pixels == pixel_index[..., None], lower_weight[..., None], zero_value)
    high_part = jnp.where(pixels == pixel_index[..., None] + 1, upper_frac[..., None], zero_value)
    return low_part + high_part


def responses(angles):
    twice = 2.0 * angles
    return jnp.stack([jnp.ones_like(twice), jnp.cos(twice), jnp.sin(twice)], axis=1)


def banded(signal, noise_coef):
    det_count = signal.shape[0]
    half_band = noise_coef.shape[1] - 1
    reach_blocks = half_band // block_cols
    span_cols = (2 * reach_blocks + 1) * block_cols
    weights = jnp.concatenate([noise_coef[:, :1] + 1.0, noise_coef[:, 1:]], axis=1)
    zero_pad = jnp.zeros((det_count, block_cols - 1), jnp.float32)
    kernel_row = jnp.concatenate(
        [
            zero_pad,
            weights[:, ::-1],
            weights[:, 1:],
            zero_pad,
            jnp.zeros((det_count, 1), jnp.float32),
        ],
        axis=1,
    )
    period = span_cols + block_cols
    tiled_rows = jnp.tile(kernel_row, (1, block_cols))[:, : block_cols * (period - 1)]
    tiled_rows = tiled_rows.reshape(det_count, block_cols, period - 1)
    matrix = tiled_rows[:, :, block_cols - 1 : block_cols - 1 + span_cols]
    matrix = matrix.reshape(det_count, block_cols, 2 * reach_blocks + 1, block_cols)
    extended = extended_2(signal, (("tm", 1),), half_band)
    block_count = signal.shape[1] // block_cols
    blocks = extended.reshape(det_count, block_count + 2 * reach_blocks, block_cols)
    stacked = jnp.stack(
        [blocks[:, offset : offset + block_count] for offset in range(2 * reach_blocks + 1)], axis=1
    )
    result = jnp.einsum(
        "diml,dmnl->dni",
        matrix,
        stacked,
        precision=lax.Precision.HIGHEST,
        preferred_element_type=jnp.float32,
    )
    return result.reshape(det_count, block_count * block_cols)


GROUP = 4
UNROLL = 6
META = 16
VMEM_LIMIT = 24 * 1024 * 1024
f32 = jnp.float32
bf16 = jnp.bfloat16


def round_up(value, step):
    return -(-value // step) * step


def iota(shape, dim):
    return lax.broadcasted_iota(jnp.int32, shape, dim)


def dot_nn(a, b):
    return lax.dot_general(a, b, (((1,), (0,)), ((), ())), preferred_element_type=f32)


def dot_nt(a, b):
    return lax.dot_general(a, b, (((1,), (1,)), ((), ())), preferred_element_type=f32)


def ones_where(mask):
    return jnp.where(mask, 1.0, 0.0).astype(bf16)


def pack_kernel(
    owners,
    cap,
    tile_dev,
    pt_ref,
    th_ref,
    slot_ref,
    r_ref,
    c_ref,
    fr_ref,
    fc_ref,
    ang_ref,
    out_ref,
    counts_ref,
    meta_ref,
):
    dets, blocks = slot_ref.shape
    runs = dets * blocks
    width = r_ref.shape[1] // blocks
    listed = pt_ref.shape[0]
    spread = dot_nn(
        slot_ref[...].astype(f32).astype(bf16),
        ones_where(iota((blocks, runs), 1) // dets == iota((blocks, runs), 0)),
    )
    run_id = iota((dets, runs), 1)
    own_det = run_id % dets == iota((dets, runs), 0)
    slot_row = jnp.sum(jnp.where(own_det, spread, 0.0), axis=0, keepdims=True)
    slot_row = slot_row.astype(jnp.int32)
    owner_row = jnp.zeros((1, runs), jnp.int32)
    tile_row = jnp.zeros((1, runs), jnp.int32)
    for k in range(listed):
        pos = th_ref[pt_ref[k]]
        own = lax.div(pos, jnp.int32(tile_dev))
        owner_row = jnp.where(slot_row == k, own, owner_row)
        tile_row = jnp.where(slot_row == k, pos - own * tile_dev, tile_row)
    owner_hot = iota((owners, runs), 0) == owner_row
    owner_one = ones_where(owner_hot)
    before = ones_where(iota((runs, runs), 0) < iota((runs, runs), 1))
    prefix = dot_nn(owner_one, before)
    rank = jnp.sum(jnp.where(owner_hot, prefix, 0.0), axis=0, keepdims=True).astype(jnp.int32)
    counts = dot_nt(jnp.ones((8, runs), bf16), owner_one)
    dest = jnp.where(rank < cap, owner_row * cap + rank, -1)
    place = ones_where(iota((owners * cap, runs), 0) == dest)

    def by_run(ref):
        return jnp.concatenate(
            [ref[:, b * width : (b + 1) * width].astype(f32) for b in range(blocks)], axis=0
        )

    angle = by_run(ang_ref)
    angle_high = angle.astype(bf16)
    angle_low = (angle - angle_high.astype(f32)).astype(bf16)
    fields = [by_run(ref).astype(bf16) for ref in (r_ref, c_ref, fr_ref, fc_ref)]
    fields += [angle_high, angle_low]
    sent = dot_nn(place, jnp.concatenate(fields, axis=1)).astype(bf16)
    for f in range(len(fields)):
        for o in range(owners):
            out_ref[o, f * cap : (f + 1) * cap, :] = sent[o * cap : (o + 1) * cap, f * width : (f + 1) * width]
    sub = iota((8, runs), 0)
    lane_run = iota((8, runs), 1)
    facts = jnp.where(sub == 0, tile_row + 1, jnp.where(sub == 1, lane_run // dets, lane_run % dets))
    facts = dot_nt(facts.astype(f32).astype(bf16), place)
    meta_ref[...] = jnp.zeros_like(meta_ref)
    for o in range(owners):
        meta_ref[o, 0:8, 0:cap] = facts[:, o * cap : (o + 1) * cap]
        meta_ref[o, 8:16, 0:owners] = counts
    out_ref[:, len(fields) * cap :, :] = meta_ref[...].astype(bf16)
    meta_ref[0] = jnp.zeros(meta_ref.shape[1:], f32)
    meta_ref[0, 0:8, 0:owners] = counts
    counts_ref[...] = meta_ref[0].astype(bf16)


def weights_of(fields_ref, axis, index, run, shape):
    index, high, low = (
        fields_ref[f, pl.ds(run, 1), :].astype(bf16) for f in (index, 2 + axis, 6 + axis)
    )
    rows = iota(shape, 0).astype(f32).astype(bf16)
    zero = jnp.zeros((), bf16)
    return jnp.where(rows == index, low, jnp.where(rows == index + 1, high, zero))


def segments(seg_ref, tile_dev):
    return [
        jnp.max(seg_ref[8 + tile : 9 + tile, :]).astype(jnp.int32) // GROUP for tile in range(tile_dev)
    ]


def tile_of(group, ends):
    tile = jnp.int32(0)
    for end in ends[:-1]:
        tile = tile + (group >= end).astype(jnp.int32)
    return tile


def project_kernel(
    cap,
    kept,
    tile_dev,
    recv_ref,
    tiles_ref,
    out_ref,
    fields_ref,
    ids_ref,
    seg_ref,
    scratch_ref,
    sig_ref,
    lanes_ref,
    half_ref,
):
    owners = recv_ref.shape[0]
    slots = owners * cap
    width = recv_ref.shape[2]
    groups_det, tile_rows, side = tiles_ref.shape
    tile_rows = tile_rows - META
    rows_dev = tile_rows // tile_dev
    part = rows_dev // 3
    for s in range(owners):
        lanes_ref[:, s * cap : (s + 1) * cap] = recv_ref[s, 6 * cap : 6 * cap + META, :].astype(f32)[0:8, 0:cap]
    facts = lanes_ref[...]
    tile1 = facts[0:1].astype(jnp.int32)
    tile_hot = iota((8, slots), 0) + 1 == tile1
    tile_one = ones_where(tile_hot)
    before = ones_where(iota((slots, slots), 0) < iota((slots, slots), 1))
    prefix = dot_nn(tile_one, before)
    count = jnp.sum(jnp.where(tile_hot, 1.0, 0.0), axis=1, keepdims=True)
    padded = jnp.floor((count + (GROUP - 1)) * (1.0 / GROUP)) * GROUP
    padded = jnp.broadcast_to(padded, (8, width))
    start = jnp.zeros((8, width), f32)
    for tile in range(tile_dev - 1):
        start += jnp.where(iota((8, width), 0) > tile, padded[tile : tile + 1], 0.0)
    stop = jnp.minimum(start + padded, float(kept))
    seg_ref[0:8, :] = start
    seg_ref[8:16, :] = stop
    where_to = jnp.sum(jnp.where(tile_hot, prefix + start[:, 0:1], 0.0), axis=0, keepdims=True)
    where_to = jnp.where(tile1 > 0, where_to, -1.0).astype(jnp.int32)
    order = ones_where(iota((kept, slots), 0) == where_to)
    source = (iota((1, slots), 1) // cap).astype(f32)
    sub = iota((8, slots), 0)
    facts = jnp.where(sub == 0, jnp.where(tile1 > 0, 1.0, 0.0), jnp.where(sub == 3, source, facts))
    facts = facts.astype(bf16)
    id_lanes = dot_nt(facts, order)
    scratch_ref[...] = jnp.zeros_like(scratch_ref)
    for q in range(-(-kept // width)):
        many = min(width, kept - q * width)
        scratch_ref[q * 8 : q * 8 + 8, 0:many] = id_lanes[:, q * width : q * width + many]
    for d in range(groups_det):
        scratch_ref[4 + d : 5 + d, :] = tiles_ref[d, tile_rows:, :].astype(f32)[0:1]
    ids_ref[...] = dot_nt(order, facts)
    sorted_fields = dot_nn(
        order,
        jnp.concatenate(
            [
                jnp.concatenate([recv_ref[s, f * cap : (f + 1) * cap, :] for s in range(owners)], axis=0)
                for f in range(6)
            ],
            axis=1,
        ),
    )
    sorted_fields = [sorted_fields[:, f * width : (f + 1) * width] for f in range(6)]
    twice = 2.0 * (sorted_fields[4] + sorted_fields[5])
    reach = side // 2 + META
    upper = jnp.where(sorted_fields[0] >= side // 2, 1.0, 0.0)
    fields_ref[0] = sorted_fields[0] - upper * (side - reach)
    fields_ref[1] = sorted_fields[1] + upper * side
    for f in (2, 3):
        fields_ref[f] = sorted_fields[f]
    fields_ref[8] = sorted_fields[0]
    fields_ref[9] = sorted_fields[1]
    fields_ref[4] = jnp.cos(twice)
    fields_ref[5] = jnp.sin(twice)
    fields_ref[6] = (1.0 - sorted_fields[2]).astype(bf16).astype(f32)
    fields_ref[7] = (1.0 - sorted_fields[3]).astype(bf16).astype(f32)
    sig_ref[...] = jnp.zeros_like(sig_ref)
    for tile in range(tile_dev):
        for p in range(3):
            at = tile * rows_dev + p * part
            plane = jnp.concatenate([tiles_ref[d, at : at + part, :] for d in range(groups_det)], axis=0)
            halves = jnp.concatenate([plane[:reach], plane[side - reach :]], axis=1)
            half_ref[tile, p * reach : (p + 1) * reach, :] = halves
    ends = segments(seg_ref, tile_dev)

    def one_group(group):
        tile = tile_of(group, ends)
        base = group * GROUP
        cols = [weights_of(fields_ref, 1, 1, base + k, (2 * side, width)) for k in range(GROUP)]
        partial_rows = dot_nn(half_ref[tile], jnp.concatenate(cols, axis=1))
        for k in range(GROUP):
            row_weight = weights_of(fields_ref, 0, 0, base + k, (reach, width)).astype(f32)
            values = []
            for p in range(3):
                term = partial_rows[p * reach : (p + 1) * reach, k * width : (k + 1) * width]
                values.append(jnp.sum(term * row_weight, axis=0, keepdims=True))
            cos = fields_ref[4, pl.ds(base + k, 1), :]
            sin = fields_ref[5, pl.ds(base + k, 1), :]
            sig_ref[pl.ds(base + k, 1), :] = values[0] + cos * values[1] + sin * values[2]

    def step(g, carry):
        for u in range(UNROLL):
            one_group(g * UNROLL + u)
        return carry

    lax.fori_loop(0, (ends[-1] + UNROLL - 1) // UNROLL, step, 0)
    sent = sig_ref[...].astype(bf16)
    notes = scratch_ref[...].astype(bf16)

    def copy(o, carry):
        out_ref[o, 0:kept, :] = sent
        out_ref[o, kept:, :] = notes
        return carry

    lax.fori_loop(0, owners, copy, 0)


def toeplitz_kernel(line_ref, out_ref):
    lines, rows, width = out_ref.shape
    blocks = rows // width

    def one(d, carry):
        for m in range(blocks):
            at = (blocks - 1 - m) * width
            piece = jnp.broadcast_to(line_ref[d, :, at : at + 2 * width], (width, 2 * width))
            block = pltpu.roll(piece, width, 1, stride=1, stride_axis=0)[:, :width]
            out_ref[d, m * width : (m + 1) * width, :] = block.astype(bf16)
        return carry

    lax.fori_loop(0, lines, one, 0)


def lines_kernel(blocks_dev, kept, cap, tile_dev, edge, recv_ref, line_ref, over_ref):
    owners, rows, width = recv_ref.shape
    lines = line_ref.shape[0]
    count = owners * blocks_dev
    most = totals = jnp.zeros((4, width), f32)
    for s in range(owners):
        counts = recv_ref[s, kept : kept + META, :].astype(f32)[4:8]
        most, totals = jnp.maximum(most, counts), totals + counts
    most = jnp.max(most)
    fullest = jnp.max(totals) + tile_dev * (GROUP - 1)
    over_ref[0] = jnp.logical_or(most > cap, fullest > kept).astype(jnp.int32)
    together = math.gcd(owners, 8)
    line_ref[...] = jnp.zeros_like(line_ref)

    def some(first, lines_now, line0):
        at, det, values = [], [], []
        for o in range(together):
            notes = recv_ref[first + o, kept:, :].astype(f32)
            notes = [notes[q * 8 : q * 8 + 8] for q in range(notes.shape[0] // 8)]
            notes = jnp.concatenate(notes, axis=1)[:, :kept]
            row = notes[3:4] * blocks_dev + notes[1:2]
            at.append(jnp.where(notes[0:1] > 0.5, row, -1.0))
            det.append(notes[2:3])
            values.append(recv_ref[first + o, 0:kept, :])
        at = jnp.concatenate(at, axis=1).astype(jnp.int32)
        det = jnp.concatenate(det, axis=1)
        place = ones_where(iota((count, together * kept), 0) == at)
        place = [place * ones_where(det == line0 + d) for d in range(lines_now)]
        return dot_nn(jnp.concatenate(place, axis=0), jnp.concatenate(values, axis=0))

    if together == owners:
        found = some(0, lines, 0)
        for d in range(lines):
            line_ref[d, edge : edge + count, :] = found[d * count : (d + 1) * count]
    else:

        def one(g, carry):
            for d in range(lines):
                line_ref[d, edge : edge + count, :] += some(g * together, 1, d)
            return carry

        lax.fori_loop(0, owners // together, one, 0)


def filter_lines(line_ref, mat_ref, coef_ref, filt_ref):
    lines, padded, width = line_ref.shape
    count = filt_ref.shape[1]
    spans = padded - count + 1
    edge = spans // 2
    for d in range(lines):
        spread = jnp.concatenate([line_ref[d, m : m + count, :].astype(bf16) for m in range(spans)], axis=1)
        weight = coef_ref[d : d + 1, 0:1] + 1.0
        rest = weight - weight.astype(bf16).astype(f32)
        filt_ref[d] = dot_nn(spread, mat_ref[d]) + rest * line_ref[d, edge : edge + count, :]


def back_kernel(
    blocks_dev,
    core_ref,
    line_ref,
    mat_ref,
    coef_ref,
    fields_ref,
    ids_ref,
    seg_ref,
    mine_ref,
    theirs_ref,
    filt_ref,
    scaled_ref,
    acc_ref,
):
    width = fields_ref.shape[2]
    kept = fields_ref.shape[1]
    filter_lines(line_ref, mat_ref, coef_ref, filt_ref)
    pairs, tile_dev, rows_dev, side = mine_ref.shape
    part = rows_dev // 3
    core = core_ref[0]
    lines, count, _ = filt_ref.shape
    ids = ids_ref[...]
    at = ids[:, 2:3] * count + ids[:, 3:4] * blocks_dev + ids[:, 1:2]
    at = jnp.where(ids[:, 0:1] > 0.5, at, -1.0).astype(jnp.int32)
    filtered = jnp.zeros((kept, 2 * width), f32)
    for d in range(lines):
        line = filt_ref[d]
        high = line.astype(bf16)
        pair = jnp.concatenate([high, (line - high.astype(f32)).astype(bf16)], axis=1)
        filtered += dot_nn(ones_where(iota((kept, count), 1) + d * count == at), pair)
    filtered = filtered[:, :width] + filtered[:, width:]
    scaled_ref[0] = filtered
    scaled_ref[1] = filtered * fields_ref[4]
    scaled_ref[2] = filtered * fields_ref[5]
    ends = segments(seg_ref, tile_dev)
    acc_ref[...] = jnp.zeros_like(acc_ref)

    def one_group(group):
        base = group * GROUP
        cols, terms = [], []
        for k in range(GROUP):
            cols.append(weights_of(fields_ref, 1, 9, base + k, (side, width)))
            row_weight = weights_of(fields_ref, 0, 8, base + k, (side, width)).astype(f32)
            scaled = [scaled_ref[p, pl.ds(base + k, 1), :] for p in range(3)]
            terms.append(jnp.concatenate([(x * row_weight).astype(bf16) for x in scaled], axis=0))
        return dot_nt(jnp.concatenate(terms, axis=1), jnp.concatenate(cols, axis=1))

    def step(g, carry):
        for u in range(UNROLL):
            acc_ref[tile_of(g * UNROLL + u, ends)] += one_group(g * UNROLL + u)
        return carry

    lax.fori_loop(0, (ends[-1] + UNROLL - 1) // UNROLL, step, 0)
    for tile in range(tile_dev):
        for h in range(pairs):
            for p in range(3):
                base = p * side + h * 2 * part
                mine = acc_ref[tile, pl.ds(pl.multiple_of(base + core * part, part), part), :]
                theirs = acc_ref[tile, pl.ds(pl.multiple_of(base + (1 - core) * part, part), part), :]
                mine_ref[h, tile, p * part : (p + 1) * part, :] = mine
                theirs_ref[h, tile, p * part : (p + 1) * part, :] = theirs.astype(bf16)


def call(kernel, out, scratch=(), **more):
    return pl.pallas_call(
        kernel,
        out_shape=out,
        scratch_shapes=list(scratch),
        compiler_params=pltpu.CompilerParams(vmem_limit_bytes=VMEM_LIMIT),
        **more,
    )


def whole_tiles(
    tiles, position, run_slot, hit_row, hit_col, frac_row, frac_col, angle, noise_coef
):
    owner_total = lax.axis_size("tm")
    groups_det, tile_dev, rows_dev, side_len = tiles.shape
    part = rows_dev // 3
    owned_tiles = tiles.reshape(groups_det, tile_dev, 3, part, side_len)
    owned_tiles = owned_tiles.transpose(1, 2, 0, 3, 4).reshape(tile_dev, 3, side_len, side_len)
    listed_total = position.shape[0]
    per_owner = max(1, listed_total // owner_total)
    slot_total = owner_total * per_owner
    owner_of = position // tile_dev
    local_slot = position % tile_dev
    listing = jnp.arange(listed_total, dtype=jnp.int32)
    earlier_same = (owner_of[:, None] == owner_of[None, :]) & (listing[:, None] > listing[None, :])
    rank_within = jnp.sum(earlier_same.astype(jnp.int32), axis=1)
    outbox_row = owner_of * per_owner + rank_within
    slot_rows = jnp.arange(slot_total, dtype=jnp.int32)
    asked_slot = (
        jnp.sum(
            jnp.where(slot_rows[:, None] == outbox_row[None, :], local_slot[None, :] + 1, 0), axis=1
        )
        - 1
    )
    served_slot = lax.all_to_all(asked_slot, "tm", split_axis=0, concat_axis=0, tiled=True)
    every_tile = jnp.broadcast_to(owned_tiles[None], (owner_total,) + owned_tiles.shape)
    every_tile = lax.all_to_all(every_tile, "tm", split_axis=0, concat_axis=0)
    every_tile = every_tile.reshape((owner_total * tile_dev,) + owned_tiles.shape[1:])
    listed = jnp.take(every_tile, position, axis=0)
    det_local, time_local = hit_row.shape
    run_length = time_local // run_slot.shape[1]
    run_total = det_local * run_slot.shape[1]
    per_group = math.gcd(run_total, group_runs)
    group_total = run_total // per_group

    def grouped(values):
        return values.reshape(group_total, per_group, run_length)

    run_items = (
        run_slot.reshape(group_total, per_group),
        grouped(hit_row),
        grouped(hit_col),
        grouped(frac_row),
        grouped(frac_col),
        grouped(angle),
    )

    def project(items):
        slots, rows_at, cols_at, frac_rows, frac_cols, angles = items
        tiles = jnp.take(listed, slots, axis=0)
        row_weight = run_weights(rows_at, frac_rows, side_len).astype(jnp.float32)
        col_weight = run_weights(cols_at, frac_cols, side_len)
        partial_rows = jnp.einsum(
            "bpij,bsj->bpsi", tiles, col_weight, preferred_element_type=jnp.float32
        )
        values = jnp.sum(partial_rows * row_weight[:, None], axis=3)
        return jnp.sum(values * responses(angles), axis=1)

    signal = lax.map(project, run_items).reshape(det_local, time_local)
    filtered = banded(signal, noise_coef)

    def back_project(carry, items):
        slots, rows_at, cols_at, frac_rows, frac_cols, angles, filt_runs = items
        row_weight = run_weights(rows_at, frac_rows, side_len).astype(jnp.float32)
        col_weight = run_weights(cols_at, frac_cols, side_len)
        scaled = responses(angles) * filt_runs[:, None]
        weighted = (scaled[..., None] * row_weight[:, None]).astype(jnp.bfloat16)
        tile_terms = jnp.einsum(
            "bpsi,bsj->bpij", weighted, col_weight, preferred_element_type=jnp.float32
        )
        return (carry.at[slots].add(tile_terms), None)

    initial = jnp.zeros((listed_total, 3, side_len, side_len), jnp.float32)
    contrib, _ = lax.scan(back_project, initial, run_items + (grouped(filtered),))
    outbox = jnp.zeros((slot_total, 3, side_len, side_len), jnp.float32).at[outbox_row].set(contrib)
    arrived = lax.all_to_all(outbox, "tm", split_axis=0, concat_axis=0, tiled=True)
    summed = jnp.stack(
        [
            jnp.sum(jnp.where((served_slot == slot_id)[:, None, None, None], arrived, 0.0), axis=0)
            for slot_id in range(tile_dev)
        ]
    )
    summed = summed.reshape(tile_dev, 3, groups_det, part, side_len)
    shares = lax.all_to_all(summed, "det", split_axis=2, concat_axis=0)
    return jnp.sum(shares.reshape(groups_det, tile_dev, 3, part, side_len), axis=0)


def body(
    sky_map,
    tile_home,
    piece_tiles,
    run_slot,
    hit_row,
    hit_col,
    frac_row,
    frac_col,
    angle,
    noise_coef,
):
    owners = lax.axis_size("tm")
    groups_det = lax.axis_size("det")
    tile_dev, _, part, side = sky_map.shape
    dets, blocks = run_slot.shape
    runs = dets * blocks
    width = hit_row.shape[1] // blocks
    listed = piece_tiles.shape[2]
    half_band = noise_coef.shape[1] - 1
    cap = round_up(2 * runs // min(owners, listed), META)
    kept = round_up(runs + runs // 2, math.lcm(META, GROUP * UNROLL))
    slots = owners * cap
    reach = side // 2 + META
    piece_list = piece_tiles.reshape(listed)
    smem = pl.BlockSpec(memory_space=pltpu.SMEM)
    vmem = pl.BlockSpec(memory_space=pltpu.VMEM)

    packed, counts = call(
        functools.partial(pack_kernel, owners, cap, tile_dev),
        (
            jax.ShapeDtypeStruct((owners, 6 * cap + META, width), bf16),
            jax.ShapeDtypeStruct((META, width), bf16),
        ),
        [pltpu.VMEM((owners, META, width), f32)],
        in_specs=[smem, smem] + [vmem] * 6,
        out_specs=(vmem, vmem),
    )(
        piece_list,
        tile_home,
        run_slot,
        hit_row,
        hit_col,
        frac_row,
        frac_col,
        angle,
    )
    recv = lax.all_to_all(packed, "tm", split_axis=0, concat_axis=0, tiled=True)
    rows = jnp.concatenate([sky_map.reshape(tile_dev * 3 * part, side), counts], axis=0)
    tiles = lax.all_gather(rows, "det", axis=0)

    weights = jnp.concatenate([noise_coef[:, :1] + 1.0, noise_coef[:, 1:]], axis=1)
    line = jnp.concatenate(
        [
            jnp.zeros((dets, width), f32),
            weights[:, ::-1],
            weights[:, 1:],
            jnp.zeros((dets, width - 1), f32),
        ],
        axis=1,
    )
    spans = 2 * (half_band // width) + 1
    matrix = call(
        toeplitz_kernel,
        pltpu.VMEM((dets, spans * width, width), bf16),
    )(line[:, None, :])

    notes = round_up(kept, width) // width * 8
    sent, fields, ids, seg = call(
        functools.partial(project_kernel, cap, kept, tile_dev),
        (
            jax.ShapeDtypeStruct((owners, kept + notes, width), bf16),
            jax.ShapeDtypeStruct((10, kept, width), f32),
            jax.ShapeDtypeStruct((kept, 8), f32),
            jax.ShapeDtypeStruct((16, width), f32),
        ),
        [
            pltpu.VMEM((notes, width), f32),
            pltpu.VMEM((kept, width), f32),
            pltpu.VMEM((8, slots), f32),
            pltpu.VMEM((tile_dev, 3 * reach, 2 * side), bf16),
        ],
    )(recv, tiles)
    heard = lax.all_to_all(sent, "tm", split_axis=0, concat_axis=0, tiled=True)

    count = owners * blocks
    place = lax.axis_index("det")
    core = lax.rem(place, 2)
    half = lax.div(place, 2)
    pairs = groups_det // 2
    heard, over = call(
        functools.partial(lines_kernel, blocks, kept, cap, tile_dev, spans // 2),
        (
            jax.ShapeDtypeStruct((dets, count + spans - 1, width), f32),
            jax.ShapeDtypeStruct((1,), jnp.int32),
        ),
        in_specs=[vmem],
        out_specs=(vmem, smem),
    )(heard)
    mine, theirs = call(
        functools.partial(back_kernel, blocks),
        (
            jax.ShapeDtypeStruct((pairs, tile_dev, 3 * part, side), f32),
            jax.ShapeDtypeStruct((pairs, tile_dev, 3 * part, side), bf16),
        ),
        [
            pltpu.VMEM((dets, count, width), f32),
            pltpu.VMEM((3, kept, width), f32),
            pltpu.VMEM((tile_dev, 3 * side, side), f32),
        ],
        in_specs=[smem] + [vmem] * 6,
        out_specs=(vmem, vmem),
    )(core[None].astype(jnp.int32), heard, matrix, noise_coef, fields, ids, seg)

    beside = lax.ppermute(theirs, "det", [(i, i ^ 1) for i in range(groups_det)])

    def of_pair(h):
        pick = lambda values: lax.dynamic_index_in_dim(values, h, 0, keepdims=False).astype(f32)
        return pick(mine) + pick(beside)

    others = []
    for step in range(1, pairs):
        ring = [(i, (i + 2 * step) % groups_det) for i in range(groups_det)]
        sent_on = of_pair(lax.rem(half + step, pairs)).astype(bf16)
        others.append(lax.ppermute(sent_on, "det", ring))

    def summed(_):
        total = of_pair(half)
        for other in others:
            total = total + other.astype(f32)
        return total.reshape(tile_dev, 3, part, side)

    def travelling(_):
        position = positions_of(piece_list, tile_home)
        whole = tiles[:, : tile_dev * 3 * part].reshape(groups_det, tile_dev, 3 * part, side)
        return whole_tiles(
            whole, position, run_slot, hit_row, hit_col, frac_row, frac_col, angle, noise_coef
        )

    return lax.cond(over[0] == 0, summed, travelling, 0)


def solution(mesh):
    placed = (
        P("tm", None, "det", None),
        P(),
        P("det", "tm", None),
        P("det", "tm"),
        P("det", "tm"),
        P("det", "tm"),
        P("det", "tm"),
        P("det", "tm"),
        P("det", "tm"),
        P("det", None),
    )
    return jax.shard_map(
        body, mesh=mesh, in_specs=placed, out_specs=P("tm", None, "det", None), check_vma=False
    )
```
